32 devices in a mesh: dp: 8 (over z, x), mp: 4 (over y, core).
Axes of the slice: x: 2, y: 2, z: 4, core: 2. Of those that a mesh axis runs over, the one named last changes fastest.
Arguments:
- text_embed: bfloat16 [8192, 2048], P(('dp', 'mp')), may hold values from -6 to 6
- clip_feats: bfloat16 [16, 256, 1024], P('dp'), may hold values from -6 to 6
- type_table: bfloat16 [3, 2048], replicated, may hold values from -3 to 3
- gain_attn_in: float32 [2048], replicated, may hold values from 0.5 to 1.5
- qkv_weight: bfloat16 [2048, 3, 2048], P(None, None, 'mp'), may hold values from -0.125 to 0.125
- gain_attn_out: float32 [2048], P('mp'), may hold values from 0.5 to 1.5
- out_weight: bfloat16 [2048, 2048], P('mp'), may hold values from -0.125 to 0.125
- gain_ffn_in: float32 [2048], replicated, may hold values from 0.5 to 1.5
- up_weight: bfloat16 [2048, 8192], P(None, 'mp'), may hold values from -0.125 to 0.125
- gain_ffn_out: float32 [8192], P('mp'), may hold values from 0.5 to 1.5
- down_weight: bfloat16 [8192, 2048], P('mp'), may hold values from -0.0625 to 0.0625
- res_query: bfloat16 [64, 2048], P(None, 'mp'), may hold values from -6 to 6
- res_key: bfloat16 [1024, 2048], P(None, 'mp'), may hold values from -0.1875 to 0.1875
- res_value: bfloat16 [1024, 2048], P(None, 'mp'), may hold values from -0.1875 to 0.1875
- res_out: bfloat16 [2048, 2048], P('mp'), may hold values from -1.5 to 1.5
- cotangent: bfloat16 [8192, 2048], P(('dp', 'mp')), may hold values from -6 to 6
- owner_count: int32 [8], replicated, may hold values from 1 to 2, as said below
- image_seq: int32 [16], replicated, may hold values from 0 to 7, as said below
- slot_block: int32 [8, 4], replicated, may hold values from 0 to 15, as said below
- seq_kind: int32 [8], replicated, may hold values from 0 to 2
Outputs:
- layer_out: float32 [8192, 2048], P(('dp', 'mp'))
- text_grad: float32 [8192, 2048], P(('dp', 'mp'))
- clip_grad: float32 [16, 256, 1024], P('dp', 'mp')
- type_grad: float32 [3, 2048], replicated
- gain_attn_in_grad: float32 [2048], replicated
- qkv_grad: float32 [2048, 3, 2048], P('dp', None, 'mp')
- gain_attn_out_grad: float32 [2048], replicated
- out_grad: float32 [2048, 2048], P('mp', 'dp')
- gain_ffn_in_grad: float32 [2048], replicated
- up_grad: float32 [2048, 8192], P('dp', 'mp')
- gain_ffn_out_grad: float32 [8192], replicated
- down_grad: float32 [8192, 2048], P('mp', 'dp')
- query_grad: float32 [64, 2048], replicated
- key_grad: float32 [1024, 2048], P('dp', 'mp')
- value_grad: float32 [1024, 2048], P('dp', 'mp')
- res_out_grad: float32 [2048, 2048], P('mp', 'dp')
The draws below stay inside these ranges and needn't reach their ends.
Inputs may be any that keep to these rules, and one draw needn't show every extreme that they name: Places 2 o to 2 o + owner_count[o] - 1 of owner o hold real images, the rest are padding; some owner is full. `image_seq`: the sequence into which a real image goes; a sequence receives at most 4 real images and some sequence exactly 4; sequences of kind 0 receive none and of kind 1 at most one; entries of padding places are ignored. `slot_block`: each row holds 4 distinct blocks of 64 positions in increasing order; entries past a sequence's image count are ignored.
All inputs are finite; a program needn't handle non-finite values.
Results may differ from the reference program's by a relative error of at most 0.022.
Values may be sent and summed in bfloat16 or wider, within the bound.
A program may use at most 256 MiB of HBM per device.

```python
import jax
import jax.numpy as jnp
from jax import lax

D = 2048
HEADS = 32
HEAD = 64
FF = 8192
CLIP_D = 1024
PATCHES = 256
LATENT = 64
SEQ = 1024
IMG_DEV = 2
SLOTS = 4
N_SEQ = 8
TOKENS = 8192
NIMG = 16
N_MP = 4


def joint_draw(key):
    base_key = jax.random.fold_in(key, 1234)
    key_kind, key_count, key_prio, key_pad, key_block = jax.random.split(base_key, 5)
    seq_ids = jnp.arange(N_SEQ, dtype=jnp.int32)
    pattern = jnp.where(seq_ids < N_SEQ // 2, 2, jnp.where(seq_ids < 3 * N_SEQ // 4, 1, 0)).astype(jnp.int32)
    shuffle = jax.random.permutation(key_kind, N_SEQ).astype(jnp.int32)
    middle = N_SEQ // 2
    zero_at = jnp.argsort(shuffle)[0].astype(jnp.int32)
    middle_value = shuffle[middle]
    shuffle = shuffle.at[zero_at].set(middle_value)
    shuffle = shuffle.at[middle].set(0)
    kinds = pattern[shuffle]
    full_seq = jnp.int32(middle)
    counts = jax.random.randint(key_count, (N_SEQ,), 1, IMG_DEV + 1).astype(jnp.int32)
    counts = counts.at[shuffle[1]].set(IMG_DEV)
    counts = counts.at[shuffle[2]].set(1)
    image_ids = jnp.arange(NIMG, dtype=jnp.int32)
    is_real = image_ids % IMG_DEV < counts[image_ids // IMG_DEV]
    real_int = is_real.astype(jnp.int32)
    total_real = jnp.sum(real_int)
    start_rank = jnp.sum(jnp.where(image_ids < IMG_DEV * middle, real_int, 0))
    real_rank = jnp.maximum(jnp.cumsum(real_int) - 1, 0)
    real_rank = jnp.mod(real_rank - start_rank + total_real, total_real).astype(jnp.int32)
    ticket_ids = jnp.arange(N_SEQ * SLOTS, dtype=jnp.int32)
    ticket_seq = ticket_ids // SLOTS
    ticket_slot = ticket_ids % SLOTS
    capacity = jnp.where(kinds == 2, SLOTS, jnp.where(kinds == 1, 1, 0))
    valid = ticket_slot < capacity[ticket_seq]
    priority = jax.random.randint(key_prio, (N_SEQ * SLOTS,), 0, 1 << 20).astype(jnp.int32)
    priority = jnp.where(ticket_seq == full_seq, 1 << 21, priority)
    score = jnp.where(valid, priority + 1, 0) * (N_SEQ * SLOTS) + ticket_ids
    order = jnp.argsort(-score)
    chosen = ticket_seq[order]
    padding_seq = jax.random.randint(key_pad, (NIMG,), 0, N_SEQ).astype(jnp.int32)
    image_seq = jnp.where(is_real, chosen[real_rank], padding_seq).astype(jnp.int32)
    block_count = SEQ // LATENT
    first_other = block_count // N_MP
    block_ids = jnp.arange(block_count, dtype=jnp.int32)
    block_score = jax.random.randint(key_block, (N_SEQ, block_count), 1, 1 << 20).astype(jnp.int32)
    is_full = seq_ids[:, None] == full_seq
    forced = is_full & ((block_ids[None, :] == first_other) | (block_ids[None, :] == block_count - 1))
    barred = is_full & (block_ids[None, :] < first_other)
    block_score = jnp.where(forced, 1 << 21, jnp.where(barred, 0, block_score)) * block_count + block_ids[None, :]
    picked = jnp.argsort(-block_score, axis=1)[:, :SLOTS]
    slot_block = jnp.sort(picked, axis=1).astype(jnp.int32)
    return (counts, image_seq, slot_block, kinds)


def draw_owner_count(key, part):
    return joint_draw(key)[0]


def draw_image_seq(key, part):
    return joint_draw(key)[1]


def draw_slot_block(key, part):
    return joint_draw(key)[2]


def draw_seq_kind(key, part):
    return joint_draw(key)[3]


def levels(key, extent, cuts, least, largest):
    factor_of, own = 1.0, jax.random.fold_in(key, 6)
    for dim, shards_of in cuts:
        steps = jnp.exp(jax.random.uniform(jax.random.fold_in(own, dim), (shards_of,), jnp.float32, least / len(cuts), largest / len(cuts)))
        factor_of = factor_of * jnp.repeat(steps, extent[dim] // shards_of).reshape([-1 if axis == dim else 1 for axis in range(len(extent))])
    return factor_of


def gaussian(key, dims, deviation, most, cuts=(), kind=jnp.bfloat16):
    level = levels(key, dims, cuts, -0.22, 0.18) if cuts else 1.0
    array = jax.random.normal(key, dims, jnp.float32) * deviation * level
    return jnp.minimum(jnp.maximum(array, -most), most).astype(kind)


def setup_inputs(seed: int = 0) -> dict:
    seeds = jax.random.split(jax.random.key(seed), 21)
    return {
        "text_embed": gaussian(seeds[0], (TOKENS, D), 1.0, 6.0, ((0, 32),)),
        "clip_feats": gaussian(seeds[1], (NIMG, PATCHES, CLIP_D), 1.0, 6.0, ((0, 8),)),
        "type_table": gaussian(seeds[2], (3, D), 0.5, 3.0),
        "gain_attn_in": jnp.clip(1.0 + 0.1 * jax.random.normal(seeds[3], (D,), jnp.float32), 0.5, 1.5),
        "qkv_weight": gaussian(seeds[4], (D, 3, D), D ** -0.5, 0.125, ((2, 4),)),
        "gain_attn_out": jnp.clip(1.0 + 0.1 * jax.random.normal(seeds[5], (D,), jnp.float32), 0.5, 1.5),
        "out_weight": gaussian(seeds[6], (D, D), D ** -0.5, 0.125, ((0, 4),)),
        "gain_ffn_in": jnp.clip(1.0 + 0.1 * jax.random.normal(seeds[7], (D,), jnp.float32), 0.5, 1.5),
        "up_weight": gaussian(seeds[8], (D, FF), D ** -0.5, 0.125, ((1, 4),)),
        "gain_ffn_out": jnp.clip(1.0 + 0.1 * jax.random.normal(seeds[9], (FF,), jnp.float32), 0.5, 1.5),
        "down_weight": gaussian(seeds[10], (FF, D), FF ** -0.5, 0.0625, ((0, 4),)),
        "res_query": gaussian(seeds[11], (LATENT, D), 1.0, 6.0, ((1, 4),)),
        "res_key": gaussian(seeds[12], (CLIP_D, D), CLIP_D ** -0.5, 0.1875, ((1, 4),)),
        "res_value": gaussian(seeds[13], (CLIP_D, D), CLIP_D ** -0.5, 0.1875, ((1, 4),)),
        "res_out": gaussian(seeds[14], (D, D), (D // 128) ** -0.5, 1.5, ((0, 4),)),
        "cotangent": gaussian(seeds[15], (TOKENS, D), 1.0, 6.0, ((0, 32),)),
        "owner_count": draw_owner_count(jax.random.fold_in(seeds[20], 71), 0),
        "image_seq": draw_image_seq(jax.random.fold_in(seeds[20], 71), 0),
        "slot_block": draw_slot_block(jax.random.fold_in(seeds[20], 71), 0),
        "seq_kind": draw_seq_kind(jax.random.fold_in(seeds[20], 71), 0),
    }


EPS = 1e-05
NEG = -1e+30
XPOS_BASE = 512.0

@jax.custom_vjp
def low(v):
    return lax.optimization_barrier(v.astype(jnp.bfloat16)).astype(jnp.float32)

@jax.custom_vjp
def low_back(v):
    return v

def low_keep(v):
    return (low(v), None)

def low_pass(kept, grad):
    return (grad,)

def back_keep(v):
    return (v, None)

def back_low(kept, grad):
    return (low(grad),)
low.defvjp(low_keep, low_pass)
low_back.defvjp(back_keep, back_low)

def both(value):
    return low_back(low(value))

def product(form, left, right):
    return jnp.einsum(form, left, right, precision=lax.Precision.HIGHEST)

def layer_norm(values, gain):
    mean = lax.optimization_barrier(jnp.mean(values, axis=-1, keepdims=True))
    square = lax.optimization_barrier(jnp.mean(values * values, axis=-1, keepdims=True))
    return (values - mean) * lax.rsqrt(square - mean * mean + EPS) * gain

def rotate_scale(values, sign, positions, center):
    size = values.shape[-1]
    half = size // 2
    ladder = jnp.arange(half, dtype=jnp.float32)
    frequency = jnp.power(10000.0, -2.0 * ladder / size)
    angle = positions[:, None] * frequency[None, :]
    decay = (2.0 * ladder + 0.4 * size) / (1.4 * size)
    scale = jnp.power(decay[None, :], sign * (positions[:, None] - center) / XPOS_BASE)
    cosine = (jnp.cos(angle) * scale)[:, None, :]
    sine = (jnp.sin(angle) * scale)[:, None, :]
    first = values[..., :half]
    second = values[..., half:]
    return jnp.concatenate([first * cosine - second * sine, second * cosine + first * sine], axis=-1)

def attend_one(item):
    query, keys, values = item
    length = query.shape[0]
    scores = low_back(product('qhe,khe->hqk', query, keys) * 0.125)
    allowed = jnp.arange(length)[:, None] >= jnp.arange(length)[None, :]
    scores = jnp.where(allowed[None], scores, NEG)
    shares = jnp.exp(scores - jax.nn.logsumexp(scores, axis=-1, keepdims=True))
    return product('hqk,khe->qhe', low(shares), values)

def reference(text_embed, clip_feats, type_table, gain_attn_in, qkv_weight, gain_attn_out, out_weight, gain_ffn_in, up_weight, gain_ffn_out, down_weight, res_query, res_key, res_value, res_out, cotangent, owner_count, image_seq, slot_block, seq_kind):
    image_ids = jnp.arange(NIMG, dtype=jnp.int32)
    is_real = image_ids % IMG_DEV < owner_count[image_ids // IMG_DEV]
    earlier = (image_seq[None, :] == image_seq[:, None]) & is_real[None, :] & (image_ids[None, :] < image_ids[:, None])
    ranks = jnp.minimum(lax.optimization_barrier(jnp.sum(earlier.astype(jnp.int32), axis=1)), SLOTS - 1).astype(jnp.int32)
    blocks = slot_block[image_seq, ranks]
    block_count = SEQ // LATENT
    cells = jnp.arange(N_SEQ * block_count, dtype=jnp.int32)
    match = is_real[None, :] & (image_seq[None, :] == (cells // block_count)[:, None]) & (blocks[None, :] == (cells % block_count)[:, None])
    has_image = jnp.any(match, axis=1)
    source = lax.optimization_barrier(jnp.sum(jnp.where(match, image_ids[None, :], 0), axis=1)).astype(jnp.int32)
    token_ids = jnp.arange(TOKENS, dtype=jnp.int32)
    row_has = has_image[token_ids // LATENT]
    row_source = (source[token_ids // LATENT] * LATENT + token_ids % LATENT).astype(jnp.int32)
    row_kind = seq_kind[token_ids // SEQ]
    positions = (token_ids % SEQ).astype(jnp.float32)
    center = SEQ // 2

    def forward(text_embed, clip_feats, type_table, gain_attn_in, qkv_weight, gain_attn_out, out_weight, gain_ffn_in, up_weight, gain_ffn_out, down_weight, res_query, res_key, res_value, res_out):
        key_proj = both(product('ipc,cd->ipd', clip_feats, res_key)).reshape(NIMG, PATCHES, HEADS, HEAD)
        value_proj = both(product('ipc,cd->ipd', clip_feats, res_value)).reshape(NIMG, PATCHES, HEADS, HEAD)
        pool_scores = low_back(product('lhe,iphe->ihlp', res_query.reshape(LATENT, HEADS, HEAD), key_proj) * 0.125)
        pool_shares = jnp.exp(pool_scores - jax.nn.logsumexp(pool_scores, axis=-1, keepdims=True))
        pool_heads = both(product('ihlp,iphe->ilhe', low(pool_shares), value_proj)).reshape(NIMG, LATENT, D)
        pooled = both(product('ild,de->ile', pool_heads, res_out)).reshape(NIMG * LATENT, D)
        mixed = jnp.where(row_has[:, None], jnp.take(pooled, row_source, axis=0), text_embed) + jnp.take(type_table, row_kind, axis=0)
        normed_in = low(layer_norm(mixed, gain_attn_in))
        qkv = low_back(product('td,dce->tce', normed_in, qkv_weight))
        query = low(rotate_scale(qkv[:, 0].reshape(TOKENS, HEADS, HEAD), 1.0, positions, center))
        keys = low(rotate_scale(qkv[:, 1].reshape(TOKENS, HEADS, HEAD), -1.0, positions, center))
        values = low(qkv[:, 2].reshape(TOKENS, HEADS, HEAD))
        shape = (N_SEQ, SEQ, HEADS, HEAD)
        attended = lax.map(jax.checkpoint(attend_one), (query.reshape(shape), keys.reshape(shape), values.reshape(shape)))
        attended = low_back(attended.reshape(TOKENS, D))
        mid = low(layer_norm(attended, gain_attn_out))
        after_attn = mixed + low_back(product('td,de->te', mid, out_weight))
        normed_ffn = low(layer_norm(after_attn, gain_ffn_in))
        pre_act = low_back(product('td,df->tf', normed_ffn, up_weight))
        up_out = low(layer_norm(jax.nn.gelu(pre_act, approximate=False), gain_ffn_out))
        return after_attn + low_back(product('tf,fd->td', up_out, down_weight))
    primal = (text_embed.astype(jnp.float32), clip_feats.astype(jnp.float32), type_table.astype(jnp.float32), gain_attn_in.astype(jnp.float32), qkv_weight.astype(jnp.float32), gain_attn_out.astype(jnp.float32), out_weight.astype(jnp.float32), gain_ffn_in.astype(jnp.float32), up_weight.astype(jnp.float32), gain_ffn_out.astype(jnp.float32), down_weight.astype(jnp.float32), res_query.astype(jnp.float32), res_key.astype(jnp.float32), res_value.astype(jnp.float32), res_out.astype(jnp.float32))
    layer_out, pullback = jax.vjp(forward, *primal)
    grads = pullback(cotangent.astype(jnp.float32))
    return (layer_out, grads[0], grads[1], grads[2], grads[3], grads[4], grads[5], grads[6], grads[7], grads[8], grads[9], grads[10], grads[11], grads[12], grads[13], grads[14])
```

```python
import functools

import jax
import jax.numpy as jnp
from jax import lax
from jax.experimental import pallas as pl
from jax.experimental.pallas import tpu as pltpu
from jax.sharding import PartitionSpec as P

HEAD = 64
LANES = 128
EPS = 1e-05
NEG = -1e30
XPOS_BASE = 512.0
BF = jnp.bfloat16
F32 = jnp.float32
ROWS_BY_ROWS = (((1,), (1,)), ((), ()))
PLAIN = (((1,), (0,)), ((), ()))
OVER_ROWS = (((0,), (0,)), ((), ()))
KIND, PART, GROUP, REAL, POS, SOURCE, BLOCK, RANK = 0, 1, 2, 4, 8, 12, 16, 32
VMEM_BYTES = 56 * 1024 * 1024


def dot(left, right, form=PLAIN):
    return lax.dot_general(left, right, form, preferred_element_type=F32)


def dot_exact(left, right, form=ROWS_BY_ROWS):
    return lax.dot_general(
        left, right, form, precision=lax.Precision.HIGHEST, preferred_element_type=F32
    )


def swap(values, axis, bit):
    size = lax.axis_size(axis)
    return lax.ppermute(values, axis, [(i, i ^ bit) for i in range(size)])


def bits_of(size):
    return [1 << i for i in range(size.bit_length() - 1)]


def gather_rel(values):
    size = lax.axis_size("mp")
    pieces = {0: values}
    for bit in reversed(bits_of(size)):
        pieces[bit] = swap(values, "mp", bit)
    for j in range(size):
        if j not in pieces:
            low = j & -j
            pieces[j] = swap(pieces[j ^ low], "mp", low)
    return [pieces[j] for j in range(size)]


def add_low(first, second):
    return (first.astype(F32) + second.astype(F32)).astype(BF)


def scatter_rel(parts):
    near = add_low(parts[2], swap(parts[3], "mp", 1))
    last = swap(near, "mp", 2)
    return parts[0], swap(parts[1], "mp", 1), last


def sum_three(parts):
    own, core, far = scatter_rel(parts)
    return own.astype(F32) + core.astype(F32) + far.astype(F32)


def spread_stats(values):
    return [values] + [swap(values, "mp", b) for b in range(1, lax.axis_size("mp"))]


def pick(values, indices):
    return jnp.stack([lax.dynamic_index_in_dim(values, i, 0, keepdims=False) for i in indices])


def by_mp(values):
    me = lax.axis_index("mp")
    return pick(values, [me ^ j for j in range(lax.axis_size("mp"))])


def gather_dp(values):
    size = lax.axis_size("dp")
    depth = len(bits_of(size))
    for level, bit in enumerate(reversed(bits_of(size))):
        values = jnp.stack([values, swap(values, "dp", bit)], axis=level)
    return values.reshape((size,) + values.shape[depth:])


def halve(values, axis):
    return (
        lax.index_in_dim(values, 0, axis, keepdims=False),
        lax.index_in_dim(values, 1, axis, keepdims=False),
    )


def scatter_dp(values, bits, last):
    for bit in bits:
        values = values.reshape((-1, 2) + values.shape[1:])
        keep, send = halve(values, 1)
        got = swap(send, "dp", bit)
        total = keep.astype(F32) + got.astype(F32)
        values = total.astype(last if bit == bits[-1] else BF)
    return values[0]


def sum_small(over_all, over_dp):
    size = lax.axis_size("mp")
    count, width = over_all.shape
    cut = by_mp(jnp.swapaxes(over_all.reshape(count, size, width // size), 0, 1))
    parts = {j: cut[j] for j in range(size)}
    for bit in bits_of(size):
        for j in sorted(parts, reverse=True):
            if j & bit:
                parts[j ^ bit] = parts[j ^ bit] + swap(parts.pop(j), "mp", bit)
    flat = jnp.concatenate([parts[0].reshape(-1), over_dp])
    for bit in bits_of(lax.axis_size("dp")):
        flat = flat + swap(flat, "dp", bit)
    whole = by_mp(jnp.stack(gather_rel(flat)))
    edge = count * (width // size)
    first = jnp.swapaxes(whole[:, :edge].reshape(size, count, width // size), 0, 1)
    return first.reshape(count, width), whole[:, edge:]


def call(body, meta, grid, ins, outs, scratch=(), flops=0, aliases=None, size=None):
    arrays, specs = [], []
    moved = 0
    for item in ins:
        arrays.append(item[0])
        moved += item[0].size * item[0].dtype.itemsize
        if len(item) == 1:
            dims = item[0].ndim
            specs.append(
                pl.BlockSpec(
                    item[0].shape,
                    lambda *_, dims=dims: (0,) * dims,
                    pipeline_mode=pl.Buffered(1),
                )
            )
        elif item[1] is None:
            specs.append(pl.BlockSpec(memory_space=pl.ANY))
        else:
            specs.append(pl.BlockSpec(item[1], item[2]))
    shapes, out_specs = [], []
    for shape, dtype, block, index in outs:
        shapes.append(jax.ShapeDtypeStruct(shape, dtype))
        moved += functools.reduce(lambda a, b: a * b, shape, 1) * jnp.dtype(dtype).itemsize
        if block is None:
            dims = len(shape)
            out_specs.append(pl.BlockSpec(shape, lambda *_, dims=dims: (0,) * dims))
        else:
            out_specs.append(pl.BlockSpec(block, index))
    return pl.pallas_call(
        body,
        out_shape=shapes,
        grid_spec=pltpu.PrefetchScalarGridSpec(
            num_scalar_prefetch=1,
            grid=grid,
            in_specs=specs,
            out_specs=out_specs,
            scratch_shapes=list(scratch),
        ),
        input_output_aliases=aliases or {},
        compiler_params=pltpu.CompilerParams(vmem_limit_bytes=size or VMEM_BYTES),
        cost_estimate=pl.CostEstimate(
            flops=int(flops), bytes_accessed=int(moved), transcendentals=0
        ),
    )(meta, *arrays)


def norm_parts(values):
    width = values.shape[-1]
    mean = jnp.sum(values, axis=-1, keepdims=True) / width
    square = jnp.sum(values * values, axis=-1, keepdims=True) / width
    inv_std = lax.rsqrt(square - mean * mean + EPS)
    return (values - mean) * inv_std, inv_std


def norm_back(upstream, normed, inv_std, gain):
    width = upstream.shape[-1]
    scaled = upstream * gain
    first = jnp.sum(scaled, axis=-1, keepdims=True) / width
    second = jnp.sum(scaled * normed, axis=-1, keepdims=True) / width
    return inv_std * (scaled - first - normed * second)


def columns_of(rows):
    count, length = rows.shape
    full = jnp.concatenate([rows, jnp.zeros((LANES - count, length), F32)], axis=0)
    return full.T


def lane_sums(values):
    total = values[:, :LANES]
    for start in range(LANES, values.shape[1], LANES):
        total = total + values[:, start : start + LANES]
    return total


def rows_from(partials):
    return dot_exact(jnp.ones((8, LANES), F32), partials)


def two_rows(first, second):
    row = lax.broadcasted_iota(jnp.int32, first.shape, 0)
    return jnp.where(row == 0, first, jnp.where(row == 1, second, 0.0))


def meta_body(count_ref, seq_ref, slot_ref, kind_ref, me_ref, out_ref, *, image_local, slots, images):
    me_m, me_d = me_ref[0], me_ref[1]

    def clear(i, _):
        out_ref[i] = 0
        return 0

    lax.fori_loop(0, BLOCK, clear, 0)

    def absent(i, _):
        out_ref[BLOCK + i] = -1
        return 0

    lax.fori_loop(0, RANK - BLOCK + images, absent, 0)
    out_ref[KIND] = kind_ref[me_d]
    out_ref[PART] = me_m
    out_ref[GROUP] = me_d
    for s in range(slots):
        out_ref[POS + s] = slot_ref[me_d, s]

    def one(i, found):
        owner = i // image_local
        inside = i - owner * image_local
        here = jnp.logical_and(inside < count_ref[owner], seq_ref[i] == me_d)
        rank = jnp.minimum(found, slots - 1)

        @pl.when(here)
        def _():
            out_ref[REAL + rank] = 1
            out_ref[SOURCE + rank] = (owner ^ me_d) * image_local + inside
            out_ref[BLOCK + slot_ref[me_d, rank]] = rank
            out_ref[RANK + i] = rank

        return found + here.astype(jnp.int32)

    lax.fori_loop(0, images, one, jnp.int32(0))


def make_meta(owner_count, image_seq, slot_block, seq_kind, image_local):
    me = jnp.stack([lax.axis_index("mp"), lax.axis_index("dp")]).astype(jnp.int32)
    images = image_seq.shape[0]
    smem = pl.BlockSpec(memory_space=pltpu.SMEM)
    return pl.pallas_call(
        functools.partial(
            meta_body, image_local=image_local, slots=slot_block.shape[1], images=images
        ),
        out_shape=jax.ShapeDtypeStruct((RANK + images,), jnp.int32),
        in_specs=[smem] * 5,
        out_specs=smem,
    )(owner_count, image_seq, slot_block, seq_kind, me)


def kind_of(meta, table_ref):
    return table_ref[pl.ds(meta[KIND], 1), :]


def text_body(meta, text_ref, table_ref, gain_ref, out_ref):
    mixed = text_ref[...].astype(F32) + kind_of(meta, table_ref)
    out_ref[...] = (norm_parts(mixed)[0] * gain_ref[...]).astype(BF)


def rotated(values, cosine, sine):
    width = values.shape[1]
    lane = lax.broadcasted_iota(jnp.int32, values.shape, 1)
    other = jnp.where(
        lane % HEAD < HEAD // 2,
        pltpu.roll(values, width - HEAD // 2, 1),
        pltpu.roll(values, HEAD // 2, 1),
    )
    repeat = width // LANES
    cosine = jnp.concatenate([cosine] * repeat, axis=1)
    sine = jnp.concatenate([sine] * repeat, axis=1)
    return values * cosine + other * sine


def qkv_body(meta, near_ref, far_ref, weight_ref, table_ref, q_ref, k_ref, v_ref, in_ref, *more):
    rows = jnp.where(pl.program_id(0) == 0, near_ref[...], far_ref[...])
    qkv_rows(rows, weight_ref, table_ref, q_ref, k_ref, v_ref)
    in_ref[...] = rows


def qkv_rows(rows, weight_ref, table_ref, q_ref, k_ref, v_ref):
    width = q_ref.shape[1]
    query = dot(rows, weight_ref[:, :width])
    q_ref[...] = rotated(query, table_ref[0], table_ref[1]).astype(BF)
    keys = dot(rows, weight_ref[:, width : 2 * width])
    k_ref[...] = rotated(keys, table_ref[2], table_ref[3]).astype(BF)
    v_ref[...] = dot(rows, weight_ref[:, 2 * width :]).astype(BF)


def slot_body(
    meta, *refs, mp, slots, latent
):
    pieces = refs[:mp]
    table_ref, gain_ref, weight_ref, turn_ref, q_in, k_in, v_in, x_in = refs[mp : mp + 8]
    q_ref, k_ref, v_ref, x_ref, slots_ref, rows_ref, qkv_ref, norm_ref = refs[mp + 8 :]
    step = pl.program_id(0)
    part = latent // mp

    @pl.when(step == 0)
    def _():
        for j in range(mp):
            place = pl.multiple_of((meta[PART] ^ j) * part, part)
            for s in range(slots):
                rows_ref[s, pl.ds(place, part), :] = pieces[j][s].astype(F32)
        mixed = rows_ref[...].reshape(slots * latent, -1)
        slots_ref[...] = mixed.astype(BF).reshape(slots_ref.shape)
        mixed = mixed + kind_of(meta, table_ref)
        normed = (norm_parts(mixed)[0] * gain_ref[...]).astype(BF)
        norm_ref[...] = normed.reshape(norm_ref.shape)
        qkv_ref[...] = dot(normed, weight_ref[...]).reshape(qkv_ref.shape)

    real = meta[REAL + step] > 0
    rows = qkv_ref[step]
    width = q_ref.shape[1]
    query = rotated(rows[:, :width], turn_ref[0], turn_ref[1]).astype(BF)
    keys = rotated(rows[:, width : 2 * width], turn_ref[2], turn_ref[3]).astype(BF)
    q_ref[...] = jnp.where(real, query, q_in[...])
    k_ref[...] = jnp.where(real, keys, k_in[...])
    v_ref[...] = jnp.where(real, rows[:, 2 * width :].astype(BF), v_in[...])
    x_ref[...] = jnp.where(real, norm_ref[step], x_in[...])


def project(meta, pieces, weight, turn, before, which):
    rows, depth = pieces[0].shape
    width = weight.shape[1] // 3
    mp = lax.axis_size("mp")
    block = lambda i, m: (m[PART] ^ (which + i), 0)
    outs = [((rows * mp, width), BF, (rows, width), block)] * 3
    outs.append(((rows * mp, depth), BF, (rows, depth), block))
    ins = [(pieces[0],), (pieces[1],), (weight,)]
    ins.append((turn, (4, rows, LANES), lambda i, m: (0, m[PART] ^ (which + i), 0)))
    aliases = {}
    if before is not None:
        for n, array in enumerate(before):
            ins.append((array, None))
            aliases[5 + n] = n
    return call(
        qkv_body_more if before is not None else qkv_body,
        meta,
        (2,),
        ins,
        outs,
        flops=4 * rows * depth * 3 * width,
        aliases=aliases,
    )


def qkv_body_more(meta, near_ref, far_ref, weight_ref, table_ref, *refs):
    qkv_body(meta, near_ref, far_ref, weight_ref, table_ref, *refs[4:])


def turn_tables(length):
    positions = jnp.arange(length, dtype=F32)[:, None]
    lane = jnp.arange(LANES)
    ladder = (lane % (HEAD // 2)).astype(F32)
    angle = positions * jnp.power(10000.0, -2.0 * ladder / HEAD)[None, :]
    decay = (2.0 * ladder + 0.4 * HEAD) / (1.4 * HEAD)
    power = (positions - length // 2) / XPOS_BASE
    sign = jnp.where(lane % HEAD < HEAD // 2, -1.0, 1.0)[None, :]
    cosine, sine = jnp.cos(angle), jnp.sin(angle) * sign
    up = jnp.power(decay[None, :], power)
    down = jnp.power(decay[None, :], -power)
    return jnp.stack([cosine * up, sine * up, cosine * down, sine * down])


def pool_shares_of(query, keys, head):
    lane = lax.broadcasted_iota(jnp.int32, query.shape, 1)
    masked = jnp.where(lane // HEAD == head, query, jnp.zeros_like(query))
    scores = dot(masked, keys, ROWS_BY_ROWS) * 0.125
    top = jnp.max(scores, axis=-1, keepdims=True)
    weights = jnp.exp(scores - top)
    return weights / jnp.sum(weights, axis=-1, keepdims=True)


def pool_body(
    meta, clip_ref, key_w, value_w, query_ref, out_w, key_ref, value_ref, pool_ref, part_ref, scratch, *, images, mp
):
    clip = clip_ref[...]
    key_ref[...] = dot(clip, key_w[...]).astype(BF)
    value_ref[...] = dot(clip, value_w[...]).astype(BF)
    patches = clip.shape[0] // images
    latent = query_ref.shape[0]
    for i in range(images):
        for pair in range(query_ref.shape[1] // LANES):
            lanes = slice(pair * LANES, (pair + 1) * LANES)
            rows = slice(i * patches, (i + 1) * patches)
            query, keys, values = query_ref[:, lanes], key_ref[rows, lanes], value_ref[rows, lanes]
            lane = lax.broadcasted_iota(jnp.int32, query.shape, 1)
            heads = [
                dot(pool_shares_of(query, keys, h).astype(BF), values) for h in range(2)
            ]
            pool_ref[i * latent : (i + 1) * latent, lanes] = jnp.where(
                lane < HEAD, heads[0], heads[1]
            ).astype(BF)
    scratch[...] = dot(pool_ref[...], out_w[...])
    piece = latent // mp
    for j in range(mp):
        for i in range(images):
            start = pl.multiple_of(i * latent + (meta[PART] ^ j) * piece, piece)
            part_ref[j, i] = scratch[pl.ds(start, piece), :].astype(BF)


def copy_body(meta, in_ref, out_ref):
    out_ref[...] = in_ref[...]


def attend_body(meta, q_ref, k_ref, v_ref, out_ref, lse_ref, stat_ref, first, second, lse, *, block):
    length, width = q_ref.shape
    first[...] = jnp.zeros_like(first)
    second[...] = jnp.zeros_like(second)

    def pair(hp, _):
        lanes = pl.ds(pl.multiple_of(hp * LANES, LANES), LANES)
        keys, values = k_ref[:, lanes], v_ref[:, lanes]
        lane = lax.broadcasted_iota(jnp.int32, (block, LANES), 1)
        row = lax.broadcasted_iota(jnp.int32, (block, block), 0)
        col = lax.broadcasted_iota(jnp.int32, (block, block), 1)
        for b in range(length // block):
            rows = slice(b * block, (b + 1) * block)
            end = (b + 1) * block
            query = q_ref[rows, lanes]
            outs = []
            for h in range(2):
                masked = jnp.where(lane // HEAD == h, query, jnp.zeros_like(query))
                scores = dot(masked, keys[:end], ROWS_BY_ROWS) * 0.125
                edge = jnp.where(row >= col, scores[:, b * block :], NEG)
                scores = edge if b == 0 else jnp.concatenate([scores[:, : b * block], edge], axis=1)
                top = jnp.max(scores, axis=-1, keepdims=True)
                weights = jnp.exp(scores - top)
                total = jnp.sum(weights, axis=-1, keepdims=True)
                outs.append(dot(weights.astype(BF), values[:end]) / total)
                lse[rows, :] = jnp.where(lane == 2 * hp + h, top + jnp.log(total), lse[rows, :])
            out = jnp.where(lane < HEAD, outs[0], outs[1])
            first[rows, :] += out
            second[rows, :] += out * out
            out_ref[rows, lanes] = out.astype(BF)
        return 0

    lax.fori_loop(0, width // LANES, pair, 0)
    lse_ref[...] = lse[...].T[: lse_ref.shape[0]]
    stat_ref[...] = two_rows(rows_from(first[...]), rows_from(second[...]))


def total_columns(stats):
    total = stats[0][...]
    for other in stats[1:]:
        total = total + other[...]
    return columns_of(total)


def stat_norm(values, columns, at, width):
    mean = columns[:, at : at + 1] / width
    square = columns[:, at + 1 : at + 2] / width
    inv_std = lax.rsqrt(square - mean * mean + EPS)
    return (values - mean) * inv_std, inv_std


def mid_body(meta, *refs, mp, width):
    att, gain_ref, weight_ref = refs[:2], refs[2], refs[3]
    stats = (refs[4 : 4 + mp], refs[4 + mp : 4 + 2 * mp])
    mids, outs = refs[4 + 2 * mp : 6 + 2 * mp], refs[6 + 2 * mp :]
    for n in range(2):
        normed, _ = stat_norm(att[n][...].astype(F32), total_columns(stats[n]), 0, width)
        mid = (normed * gain_ref[...]).astype(BF)
        mids[n][...] = mid
        outs[n][...] = dot(mid, weight_ref[...]).astype(BF)


def after_body(meta, own_ref, core_ref, far_ref, text_ref, slots_ref, table_ref, gain_ref, after_ref, low_ref):
    mixed = mixed_rows(meta, text_ref, slots_ref, table_ref)
    after = mixed + (
        own_ref[...].astype(F32) + core_ref[...].astype(F32) + far_ref[...].astype(F32)
    )
    after_ref[...] = after
    low_ref[...] = (norm_parts(after)[0] * gain_ref[...]).astype(BF)


def mixed_rows(meta, text_ref, slots_ref, table_ref):
    block = meta[PART] * pl.num_programs(0) + pl.program_id(0)
    filled = meta[BLOCK + block] >= 0
    return (
        jnp.where(filled, slots_ref[0].astype(F32), text_ref[...].astype(F32))
        + kind_of(meta, table_ref)
    )


def slot_index(blocks):
    return lambda i, m: (jnp.maximum(m[BLOCK + m[PART] * blocks + i], 0), 0, 0)


def times_rows_body(meta, *refs):
    pieces, weight_ref, out_ref = refs[:-2], refs[-2], refs[-1]
    rows = pieces[0].shape[0]
    for n, piece in enumerate(pieces):
        out_ref[n * rows : (n + 1) * rows, :] = dot(
            piece[...], weight_ref[...], ROWS_BY_ROWS
        ).astype(out_ref.dtype)


def up_body(meta, a_ref, b_ref, weight_ref, dup_ref, gain_ref, act_ref, slope_ref, stat_ref, *sums):
    step = pl.program_id(0)
    rows = a_ref.shape[0]

    @pl.when(step == 0)
    def _():
        for ref in sums:
            ref[...] = jnp.zeros_like(ref)

    for n, ref in enumerate((a_ref, b_ref)):
        here = slice(n * rows, (n + 1) * rows)
        pre = dot(ref[...], weight_ref[...])
        share = 0.5 + 0.5 * lax.erf(pre * (0.5**0.5))
        density = jnp.exp(pre * pre * -0.5) * ((2.0 * jnp.pi) ** -0.5)
        act = pre * share
        act_ref[here, :] = act.astype(BF)
        slope_ref[here, :] = (share + pre * density).astype(BF)
        scaled = dup_ref[here, :].astype(F32) * gain_ref[...]
        for ref_sum, term in zip(sums, (act, act * act, scaled, scaled * act)):
            ref_sum[here, :] += lane_sums(term)

    @pl.when(step == pl.num_programs(0) - 1)
    def _():
        for n, ref_sum in enumerate(sums):
            stat_ref[n : n + 1, :] = rows_from(ref_sum[...])[:1]
        stat_ref[4:, :] = jnp.zeros_like(stat_ref[4:, :])


def back_body(meta, act_ref, slope_ref, dup_ref, gain_ref, weight_ref, *refs, mp, width):
    stats, outs = refs[:mp], refs[mp:]
    pre_ref, low_ref, first_ref, second_ref, grad_ref = outs
    step = pl.program_id(0)
    columns = total_columns(stats)
    act = act_ref[...].astype(F32)
    normed, inv_std = stat_norm(act, columns, 0, width)
    gain = gain_ref[...]
    low_ref[...] = (normed * gain).astype(BF)
    upstream = dup_ref[...].astype(F32)
    first = columns[:, 2:3] / width
    mean = columns[:, 0:1] / width
    second = (columns[:, 3:4] - mean * columns[:, 2:3]) * inv_std / width
    d_act = inv_std * (upstream * gain - first - normed * second)
    d_pre = (d_act * slope_ref[...].astype(F32)).astype(BF)
    pre_ref[...] = d_pre
    gained = jnp.sum(upstream * normed, axis=0, keepdims=True)

    @pl.when(step == 0)
    def _():
        grad_ref[...] = gained

    @pl.when(step != 0)
    def _():
        grad_ref[...] += gained

    product = dot(d_pre, weight_ref[...], ROWS_BY_ROWS).astype(BF)

    @pl.when(step == 0)
    def _():
        first_ref[...] = product

    @pl.when(step != 0)
    def _():
        second_ref[...] = product


def down_body(meta, near_ref, far_ref, weight_ref, *outs):
    rows = outs[0].shape[0]
    for n, ref in enumerate((near_ref, far_ref)):
        for m in range(2):
            outs[2 * n + m][...] = dot(
                ref[m * rows : (m + 1) * rows, :], weight_ref[...]
            ).astype(BF)


def ffn_back_body(meta, own_ref, core_ref, far_ref, after_ref, cot_ref, gain_ref, out_ref, low_ref, grad_ref):
    upstream = own_ref[...].astype(F32) + core_ref[...].astype(F32) + far_ref[...].astype(F32)
    normed, inv_std = norm_parts(after_ref[...])
    d_after = cot_ref[...].astype(F32) + norm_back(upstream, normed, inv_std, gain_ref[...])
    out_ref[...] = d_after
    low_ref[...] = d_after.astype(BF)
    add_rows(grad_ref, upstream * normed)


def add_rows(ref, values):
    total = jnp.sum(values, axis=0, keepdims=True)

    @pl.when(pl.program_id(0) == 0)
    def _():
        ref[...] = total

    @pl.when(pl.program_id(0) != 0)
    def _():
        ref[...] += total


def d_mid_body(meta, *refs, mp, width):
    pieces, weight_ref, gain_ref, att_ref = refs[:2], refs[2], refs[3], refs[4]
    stats = refs[5 : 5 + mp]
    out_ref, stat_ref, grad_ref = refs[-3:]
    rows = jnp.where(pl.program_id(0) == 0, pieces[0][...], pieces[1][...])
    d_mid = dot(rows, weight_ref[...], ROWS_BY_ROWS)
    out_ref[...] = d_mid.astype(BF)
    normed, _ = stat_norm(att_ref[...].astype(F32), total_columns(stats), 0, width)
    scaled = d_mid * gain_ref[...]
    add_rows(grad_ref, d_mid * normed)
    stat_ref[...] = two_rows(
        rows_from(lane_sums(scaled)), rows_from(lane_sums(scaled * normed))
    )


def d_mid_body_more(meta, *refs, mp, width):
    d_mid_body(meta, *refs[: 5 + mp], *refs[7 + mp :], mp=mp, width=width)


def attend_back_body(
    meta, q_ref, k_ref, v_ref, att_ref, dmid_ref, lse_ref, gain_ref, turn_ref, *refs, mp, width, block
):
    stats, more = refs[:mp], refs[mp : 2 * mp]
    out_ref, d_att, dq, dk, dv = refs[2 * mp :]
    length, wide = q_ref.shape
    columns = total_columns(stats)
    normed, inv_std = stat_norm(att_ref[...].astype(F32), columns, 0, width)
    sums = total_columns(more)
    scaled = dmid_ref[...].astype(F32) * gain_ref[...]
    d_att[...] = (
        inv_std * (scaled - sums[:, 0:1] / width - normed * (sums[:, 1:2] / width))
    ).astype(BF)

    def pair(hp, _):
        lanes = pl.ds(pl.multiple_of(hp * LANES, LANES), LANES)
        keys, values = k_ref[:, lanes], v_ref[:, lanes]
        lane = lax.broadcasted_iota(jnp.int32, (block, LANES), 1)
        row = lax.broadcasted_iota(jnp.int32, (block, block), 0)
        col = lax.broadcasted_iota(jnp.int32, (block, block), 1)
        dk[...] = jnp.zeros_like(dk)
        dv[...] = jnp.zeros_like(dv)
        both = d_att[:, lanes].astype(F32) * att_ref[:, lanes].astype(F32)
        side = lax.broadcasted_iota(jnp.int32, (8, LANES), 1) // HEAD
        pick_head = lax.broadcasted_iota(jnp.int32, (8, LANES), 0) == side
        inner = dot_exact(pick_head.astype(F32), both)
        for b in range(length // block):
            rows = slice(b * block, (b + 1) * block)
            end = (b + 1) * block
            query, grad = q_ref[rows, lanes], d_att[rows, lanes]
            d_query = jnp.zeros((block, LANES), F32)
            for h in range(2):
                keep = lane // HEAD == h
                q_one = jnp.where(keep, query, jnp.zeros_like(query))
                g_one = jnp.where(keep, grad, jnp.zeros_like(grad))
                scores = dot(keys[:end], q_one, ROWS_BY_ROWS) * 0.125
                shares = jnp.exp(scores - lse_ref[pl.ds(2 * hp + h, 1), rows])
                edge = jnp.where(col >= row, shares[b * block :], 0.0)
                shares = edge if b == 0 else jnp.concatenate([shares[: b * block], edge], axis=0)
                d_shares = dot(values[:end], g_one, ROWS_BY_ROWS)
                d_scores = (shares * (d_shares - inner[h : h + 1, rows])).astype(BF)
                dv[:end, :] += dot(shares.astype(BF), g_one)
                dk[:end, :] += dot(d_scores, q_one)
                turned = dot(d_scores, keys[:end], OVER_ROWS)
                d_query = jnp.where(keep, turned, d_query)
            dq[rows, :] = d_query
        at = pl.multiple_of(hp * LANES, LANES)
        out_ref[:, pl.ds(at, LANES)] = rotated(
            dq[...] * 0.125, turn_ref[0], -turn_ref[1]
        ).astype(BF)
        out_ref[:, pl.ds(wide + at, LANES)] = rotated(
            dk[...] * 0.125, turn_ref[2], -turn_ref[3]
        ).astype(BF)
        out_ref[:, pl.ds(2 * wide + at, LANES)] = dv[...].astype(BF)
        return 0

    lax.fori_loop(0, wide // LANES, pair, 0)


def slot_back_body(meta, *refs, slots, mp):
    pieces, weight_ref, out_ref, scratch = refs[:slots], refs[slots], refs[-2], refs[-1]
    rows = jnp.concatenate([p[...] for p in pieces], axis=0)
    scratch[...] = dot(rows, weight_ref[...], ROWS_BY_ROWS)
    latent = pieces[0].shape[0]
    part = latent // mp
    for j in range(mp):
        for s in range(slots):
            start = pl.multiple_of(s * latent + (meta[PART] ^ j) * part, part)
            out_ref[j, s] = scratch[pl.ds(start, part), :].astype(BF)


def row_back_body(meta, a_ref, b_ref, weight_ref, a_out, b_out):
    a_out[...] = dot(a_ref[...], weight_ref[...], ROWS_BY_ROWS).astype(BF)
    b_out[...] = dot(b_ref[...], weight_ref[...], ROWS_BY_ROWS).astype(BF)


def slot_grad_body(meta, *refs, mp, slots, latent):
    own_ref, core_ref, far_ref, slots_ref, table_ref, gain_ref = refs[:6]
    after, out_ref = refs[6:-1], refs[-1]
    part = latent // mp
    start = pl.multiple_of(meta[PART] * part, part)
    for s in range(slots):
        upstream = (
            own_ref[s].astype(F32) + core_ref[s].astype(F32) + far_ref[s].astype(F32)
        )
        mixed = slots_ref[s, pl.ds(start, part), :].astype(F32) + kind_of(meta, table_ref)
        normed, inv_std = norm_parts(mixed)
        block = meta[POS + s]
        blocks = after[0].shape[0] // latent
        rel = (block // blocks) ^ meta[PART]
        row = pl.multiple_of((block % blocks) * latent + start, part)
        d_after = after[0][pl.ds(row, part), :]
        for j in range(1, mp):
            d_after = jnp.where(rel == j, after[j][pl.ds(row, part), :], d_after)
        out_ref[s] = (
            d_after.astype(F32) + norm_back(upstream, normed, inv_std, gain_ref[...])
        ).astype(BF)


def place_body(meta, in_ref, out_ref, *, image_local):
    k = pl.program_id(0)
    image = ((k // image_local) ^ meta[GROUP]) * image_local + k % image_local
    out_ref[...] = jnp.where(meta[RANK + image] >= 0, in_ref[...], jnp.zeros_like(in_ref[...]))


def in_back_body(
    meta, own_ref, core_ref, far_ref, after_ref, text_ref, slots_ref, table_ref, gain_ref, out_ref, gain_grad, type_grad
):
    upstream = own_ref[...].astype(F32) + core_ref[...].astype(F32) + far_ref[...].astype(F32)
    normed, inv_std = norm_parts(mixed_rows(meta, text_ref, slots_ref, table_ref))
    d_mixed = after_ref[...] + norm_back(upstream, normed, inv_std, gain_ref[...])
    block = meta[PART] * pl.num_programs(0) + pl.program_id(0)
    out_ref[...] = jnp.where(meta[BLOCK + block] >= 0, 0.0, d_mixed)
    add_rows(gain_grad, upstream * normed)
    add_rows(type_grad, d_mixed)


def pool_back_body(
    meta, grad_ref, out_w, key_ref, value_ref, query_ref, key_w, value_w, kv_ref, query_grad, clip_ref, scratch, *, images, mp
):
    d_heads = dot(grad_ref[...], out_w[...], ROWS_BY_ROWS).astype(BF)
    patches = key_ref.shape[0] // images
    latent, wide = query_ref.shape
    for pair in range(wide // LANES):
        lanes = slice(pair * LANES, (pair + 1) * LANES)
        query = query_ref[:, lanes]
        lane = lax.broadcasted_iota(jnp.int32, query.shape, 1)
        d_query = jnp.zeros((latent, LANES), F32)
        for i in range(images):
            rows = slice(i * patches, (i + 1) * patches)
            keys, values = key_ref[rows, lanes], value_ref[rows, lanes]
            grad = d_heads[i * latent : (i + 1) * latent, lanes]
            d_keys = jnp.zeros((patches, LANES), F32)
            d_values = jnp.zeros((patches, LANES), F32)
            for h in range(2):
                keep = lane // HEAD == h
                shares = pool_shares_of(query, keys, h)
                g_one = jnp.where(keep, grad, jnp.zeros_like(grad))
                q_one = jnp.where(keep, query, jnp.zeros_like(query))
                d_shares = dot(g_one, values, ROWS_BY_ROWS)
                inner = jnp.sum(shares * d_shares, axis=-1, keepdims=True)
                d_scores = (shares * (d_shares - inner)).astype(BF)
                d_query += jnp.where(keep, dot(d_scores, keys), 0.0)
                d_keys += dot(d_scores, q_one, OVER_ROWS)
                d_values += dot(shares.astype(BF), g_one, OVER_ROWS)
            kv_ref[rows, lanes] = (d_keys * 0.125).astype(BF)
            kv_ref[rows, slice(wide + pair * LANES, wide + (pair + 1) * LANES)] = d_values.astype(BF)
        query_grad[:, lanes] = d_query * 0.125
    scratch[...] = dot(kv_ref[:, :wide], key_w[...], ROWS_BY_ROWS) + dot(
        kv_ref[:, wide:], value_w[...], ROWS_BY_ROWS
    )
    piece = patches // mp
    for j in range(mp):
        for i in range(images):
            start = pl.multiple_of(i * patches + (meta[PART] ^ j) * piece, piece)
            clip_ref[j, i] = scratch[pl.ds(start, piece), :].astype(BF)


def weight_body(meta, *refs, lefts, rights):
    left, right, rest = refs[:lefts], refs[lefts : lefts + rights], refs[lefts + rights :]
    depth = sum(r.shape[0] for r in left)
    total = None
    step = depth // max(lefts, rights)
    for start in range(0, depth, step):
        l_ref, l_at = find(left, start)
        r_ref, r_at = find(right, start)
        term = dot(l_ref[l_at : l_at + step, :], r_ref[r_at : r_at + step, :], OVER_ROWS)
        total = term if total is None else total + term
    if len(rest) == 1:
        rest[0][0] = total.astype(BF)
        return
    got, even, odd = rest
    total = (total + got[0].astype(F32)).astype(BF)
    step = pl.program_id(0)

    @pl.when(step % 2 == 0)
    def _():
        even[0] = total

    @pl.when(step % 2 == 1)
    def _():
        odd[0] = total


def find(refs, start):
    for ref in refs:
        if start < ref.shape[0]:
            return ref, start
        start -= ref.shape[0]
    return None


def weight_grads(meta, left, right):
    size = lax.axis_size("dp")
    rows, width = sum(a.shape[0] for a in left), left[0].shape[1]
    inner = right[0].shape[1]
    part = width // size
    bits = bits_of(size)
    if part % LANES or size < 4:
        whole = dot(jnp.concatenate(left), jnp.concatenate(right), OVER_ROWS).astype(BF)
        whole = whole.reshape(size, part, inner)
        me = lax.axis_index("dp")
        return scatter_dp(pick(whole, [me ^ k for k in range(size)]), bits, F32)
    half = size // 2

    def run(odd, got):
        ins = [
            (a, (a.shape[0], part), lambda i, m: (0, m[GROUP] ^ (2 * i + odd))) for a in left
        ] + [(a,) for a in right]
        if got is None:
            outs = [((half, part, inner), BF, (1, part, inner), lambda i, m: (i, 0, 0))]
        else:
            ins.append((got, (1, part, inner), lambda i, m: (i, 0, 0)))
            outs = [
                ((half // 2, part, inner), BF, (1, part, inner), lambda i, m: (i // 2, 0, 0))
            ] * 2
        return call(
            functools.partial(weight_body, lefts=len(left), rights=len(right)),
            meta,
            (half,),
            ins,
            outs,
            flops=rows * width * inner,
        )

    send = run(1, None)[0]
    keep, send = run(0, swap(send, "dp", 1))
    for bit in bits[1:]:
        got = swap(send, "dp", bit)
        if bit == bits[-1]:
            return (keep.astype(F32) + got.astype(F32))[0]
        values = add_low(keep, got)
        values = values.reshape((-1, 2) + values.shape[1:])
        keep, send = halve(values, 1)


def shards(
    text_embed,
    clip_feats,
    type_table,
    gain_attn_in,
    qkv_weight,
    gain_attn_out,
    out_weight,
    gain_ffn_in,
    up_weight,
    gain_ffn_out,
    down_weight,
    res_query,
    res_key,
    res_value,
    res_out,
    cotangent,
    owner_count,
    image_seq,
    slot_block,
    seq_kind,
):
    mp = lax.axis_size("mp")
    dp = lax.axis_size("dp")
    rows, width = text_embed.shape
    length = rows * mp
    latent = res_query.shape[0]
    slots = slot_block.shape[1]
    images, patches, clip_width = clip_feats.shape
    wide = qkv_weight.shape[2]
    heads = wide // HEAD
    ff = up_weight.shape[1]
    ff_all = ff * mp
    here = rows // latent
    part = latent // mp
    tile = 512

    meta = make_meta(owner_count, image_seq, slot_block, seq_kind, images)
    table = type_table.astype(F32)
    gain_in, gain_out = gain_attn_in[None], gain_attn_out[None]
    gain_ffn, gain_ff = gain_ffn_in[None], gain_ffn_out[None]
    row_block = lambda i, m: (i, 0)

    text_in = call(
        text_body,
        meta,
        (4,),
        [(text_embed, (rows // 4, width), row_block), (table,), (gain_in,)],
        [((rows, width), BF, (rows // 4, width), row_block)],
    )[0]
    text_pieces = gather_rel(text_in)

    clip = clip_feats.reshape(images * patches, clip_width)
    key_proj, value_proj, pool_out, pool_part = call(
        functools.partial(pool_body, images=images, mp=mp),
        meta,
        (1,),
        [(clip,), (res_key,), (res_value,), (res_query,), (res_out,)],
        [
            ((images * patches, wide), BF, None, None),
            ((images * patches, wide), BF, None, None),
            ((images * latent, wide), BF, None, None),
            ((mp, images, part, width), BF, None, None),
        ],
        scratch=[pltpu.VMEM((images * latent, width), F32)],
        flops=4 * images * patches * clip_width * wide,
    )
    pooled = sum_three([pool_part[j] for j in range(mp)]).astype(BF)
    pooled = gather_dp(pooled).reshape(dp * images, part, width)
    slot_piece = call(
        copy_body,
        meta,
        (slots,),
        [(pooled, (1, part, width), lambda i, m: (m[SOURCE + i], 0, 0))],
        [((slots, part, width), BF, (1, part, width), lambda i, m: (i, 0, 0))],
    )[0]
    slot_pieces = gather_rel(slot_piece)
    cot_pieces = gather_rel(cotangent)

    weight = qkv_weight.reshape(width, 3 * wide)
    turn = turn_tables(length)
    state = project(meta, text_pieces[:2], weight, turn, None, 0)
    state = project(meta, text_pieces[2:], weight, turn, state, 2)
    at_slot = lambda i, m: (m[POS + i], 0)
    state = call(
        functools.partial(slot_body, mp=mp, slots=slots, latent=latent),
        meta,
        (slots,),
        [(p,) for p in slot_pieces]
        + [(table,), (gain_in,), (weight,)]
        + [(turn, (4, latent, LANES), lambda i, m: (0, m[POS + i], 0))]
        + [(a, (latent, a.shape[1]), at_slot) for a in state],
        [(a.shape, BF, (latent, a.shape[1]), at_slot) for a in state]
        + [((slots, latent, width), BF, None, None)],
        scratch=[
            pltpu.VMEM((slots, latent, width), F32),
            pltpu.VMEM((slots, latent, 3 * wide), F32),
            pltpu.VMEM((slots, latent, width), BF),
        ],
        flops=6 * slots * latent * width * wide,
        aliases={mp + 5 + n: n for n in range(4)},
    )
    query, keys, values, in_full, slot_rows = state

    att, lse, att_stats = call(
        functools.partial(attend_body, block=rows),
        meta,
        (1,),
        [(query,), (keys,), (values,)],
        [
            ((length, wide), BF, None, None),
            ((heads, length), F32, None, None),
            ((8, length), F32, None, None),
        ],
        scratch=[pltpu.VMEM((length, LANES), F32)] * 3,
        flops=4 * length * length * wide,
    )
    att_stats = spread_stats(att_stats)

    def mid_terms(which):
        places = [which, which + 1]
        block = [lambda i, m, j=j: (m[PART] ^ j, 0) for j in places]
        lane_block = [lambda i, m, j=j: (0, m[PART] ^ j) for j in places]
        return call(
            functools.partial(mid_body, mp=mp, width=width),
            meta,
            (1,),
            [(att, (rows, wide), block[n]) for n in range(2)]
            + [(gain_out,), (out_weight,)]
            + [(s, (8, rows), lane_block[n]) for n in range(2) for s in att_stats],
            [((rows, wide), BF, None, None)] * 2 + [((rows, width), BF, None, None)] * 2,
            flops=4 * rows * wide * width,
        )

    mid_2, mid_3, out_2, out_3 = mid_terms(2)
    mid_0, mid_1, out_0, out_1 = mid_terms(0)
    mids = [mid_0, mid_1, mid_2, mid_3]
    out_terms = scatter_rel([out_0, out_1, out_2, out_3])
    few = (latent, width)
    after_attn, ffn_in = call(
        after_body,
        meta,
        (here,),
        [(t, few, row_block) for t in out_terms]
        + [(text_embed, few, row_block), (slot_rows, (1,) + few, slot_index(here))]
        + [(table,), (gain_ffn,)],
        [((rows, width), F32, few, row_block), ((rows, width), BF, few, row_block)],
    )
    ffn_pieces = gather_rel(ffn_in)

    d_up = call(
        times_rows_body,
        meta,
        (ff // tile,),
        [(p,) for p in cot_pieces] + [(down_weight, (tile, width), row_block)],
        [((length, ff), BF, (length, tile), lambda i, m: (0, i))],
        flops=2 * length * width * ff,
    )[0]

    def up_half(which):
        return call(
            up_body,
            meta,
            (ff // tile,),
            [(ffn_pieces[which],), (ffn_pieces[which + 1],)]
            + [(up_weight, (width, tile), lambda i, m: (0, i))]
            + [(d_up, (2 * rows, tile), lambda i, m: (which // 2, i))]
            + [(gain_ff, (1, tile), lambda i, m: (0, i))],
            [
                ((2 * rows, ff), BF, (2 * rows, tile), lambda i, m: (0, i)),
                ((2 * rows, ff), BF, (2 * rows, tile), lambda i, m: (0, i)),
                ((8, 2 * rows), F32, None, None),
            ],
            scratch=[pltpu.VMEM((2 * rows, LANES), F32)] * 4,
            flops=4 * rows * width * ff,
        )

    act_near, slope_near, stat_near = up_half(0)
    act_far, slope_far, stat_far = up_half(2)
    ff_stats = spread_stats(jnp.concatenate([stat_near, stat_far], axis=1))

    def back_half(act, slope, which):
        block = (rows, ff)
        flip = lambda i, m: (1 - i, 0)
        return call(
            functools.partial(back_body, mp=mp, width=ff_all),
            meta,
            (2,),
            [(act, block, flip), (slope, block, flip)]
            + [(d_up, block, lambda i, m: (which + 1 - i, 0)), (gain_ff,), (up_weight,)]
            + [
                (s, (8, rows), lambda i, m, b=b: (0, (which + 1 - i) ^ b))
                for b, s in enumerate(ff_stats)
            ],
            [((2 * rows, ff), BF, block, flip)] * 2
            + [((rows, width), BF, None, None)] * 2
            + [((1, ff), F32, None, None)],
            flops=4 * rows * width * ff,
        )

    pre_far, low_far, back_3, back_2, gain_far = back_half(act_far, slope_far, 2)
    pre_near, low_near, back_1, back_0, gain_near = back_half(act_near, slope_near, 0)
    ffn_terms = scatter_rel([back_0, back_1, back_2, back_3])
    down_grad = weight_grads(meta, cot_pieces, [low_near, low_far]).T
    up_grad = weight_grads(meta, ffn_pieces, [pre_near, pre_far])
    d_after, d_after_low, gain_ffn_local = call(
        ffn_back_body,
        meta,
        (here,),
        [(t, few, row_block) for t in ffn_terms]
        + [(after_attn, few, row_block), (cotangent, few, row_block), (gain_ffn,)],
        [
            ((rows, width), F32, few, row_block),
            ((rows, width), BF, few, row_block),
            ((1, width), F32, None, None),
        ],
    )
    after_pieces = gather_rel(d_after_low)

    down_terms = call(
        down_body,
        meta,
        (width // tile,),
        [(low_near,), (low_far,), (down_weight, (ff, tile), lambda i, m: (0, i))],
        [((rows, width), BF, (rows, tile), lambda i, m: (0, i))] * mp,
        flops=2 * length * width * ff,
    )
    layer_out = after_attn + sum_three(down_terms)

    def d_mid_half(which, before):
        block = lambda i, m: (m[PART] ^ (which + i), 0)
        lane_block = lambda i, m: (0, m[PART] ^ (which + i))
        body, aliases = d_mid_body, {}
        ins = [(after_pieces[which],), (after_pieces[which + 1],), (out_weight,), (gain_out,)]
        ins += [(att, (rows, wide), block)] + [(s, (8, rows), lane_block) for s in att_stats]
        if before is not None:
            body = d_mid_body_more
            aliases = {len(ins) + 1 + n: n for n in range(2)}
            ins += [(a, None) for a in before]
        return call(
            functools.partial(body, mp=mp, width=width),
            meta,
            (2,),
            ins,
            [
                ((length, wide), BF, (rows, wide), block),
                ((8, length), F32, (8, rows), lane_block),
                ((1, wide), F32, None, None),
            ],
            flops=4 * rows * wide * width,
            aliases=aliases,
        )

    d_mid, mid_stats, gain_mid_near = d_mid_half(0, None)
    d_mid, mid_stats, gain_mid_far = d_mid_half(2, (d_mid, mid_stats))
    mid_stats = spread_stats(mid_stats)
    out_grad = weight_grads(meta, after_pieces, mids).T
    d_qkv = call(
        functools.partial(attend_back_body, mp=mp, width=width, block=rows),
        meta,
        (1,),
        [(a,) for a in (query, keys, values, att, d_mid, lse, gain_out, turn)]
        + [(s,) for s in att_stats]
        + [(s,) for s in mid_stats],
        [((length, 3 * wide), BF, None, None)],
        scratch=[pltpu.VMEM((length, wide), BF)] + [pltpu.VMEM((length, LANES), F32)] * 3,
        flops=10 * length * length * wide,
    )[0]

    slot_terms = call(
        functools.partial(slot_back_body, slots=slots, mp=mp),
        meta,
        (1,),
        [
            (d_qkv, (latent, 3 * wide), lambda i, m, s=s: (m[POS + s], 0))
            for s in range(slots)
        ]
        + [(weight,)],
        [((mp, slots, part, width), BF, None, None)],
        scratch=[pltpu.VMEM((slots * latent, width), F32)],
        flops=6 * slots * latent * width * wide,
    )[0]
    slot_terms = scatter_rel([slot_terms[j] for j in range(mp)])
    slot_grad = call(
        functools.partial(slot_grad_body, mp=mp, slots=slots, latent=latent),
        meta,
        (1,),
        [(t,) for t in slot_terms]
        + [(slot_rows,), (table,), (gain_in,)]
        + [(a,) for a in after_pieces],
        [((slots, part, width), BF, None, None)],
    )[0]
    image_of = lambda k, m: ((k // images) ^ m[GROUP]) * images + k % images
    image_grad = call(
        functools.partial(place_body, image_local=images),
        meta,
        (dp * images,),
        [
            (
                slot_grad,
                (1, part, width),
                lambda k, m: (jnp.maximum(m[RANK + image_of(k, m)], 0), 0, 0),
            )
        ],
        [((dp * images, part, width), BF, (1, part, width), lambda k, m: (k, 0, 0))],
    )[0]
    owned = scatter_dp(image_grad.reshape(dp, images, part, width), bits_of(dp), BF)
    pool_grad = jnp.swapaxes(by_mp(jnp.stack(gather_rel(owned))), 0, 1).reshape(
        images * latent, width
    )
    d_kv, query_local, clip_terms = call(
        functools.partial(pool_back_body, images=images, mp=mp),
        meta,
        (1,),
        [(a,) for a in (pool_grad, res_out, key_proj, value_proj, res_query, res_key, res_value)],
        [
            ((images * patches, 2 * wide), BF, None, None),
            ((latent, wide), F32, None, None),
            ((mp, images, patches // mp, clip_width), BF, None, None),
        ],
        scratch=[pltpu.VMEM((images * patches, clip_width), F32)],
        flops=4 * images * patches * clip_width * wide,
    )
    res_out_grad = weight_grads(meta, [pool_grad], [pool_out]).T
    kv_grad = weight_grads(meta, [clip], [d_kv])
    clip_grad = sum_three([clip_terms[j] for j in range(mp)])

    def row_terms(which):
        return call(
            row_back_body,
            meta,
            (1,),
            [
                (d_qkv, (rows, 3 * wide), lambda i, m, j=j: (m[PART] ^ j, 0))
                for j in (which, which + 1)
            ]
            + [(weight,)],
            [((rows, width), BF, None, None)] * 2,
            flops=12 * rows * width * wide,
        )

    in_2, in_3 = row_terms(2)
    in_0, in_1 = row_terms(0)
    in_terms = scatter_rel([in_0, in_1, in_2, in_3])
    qkv_grad = weight_grads(meta, [in_full], [d_qkv]).reshape(-1, 3, wide)
    text_grad, gain_in_local, type_local = call(
        in_back_body,
        meta,
        (here,),
        [(t, few, row_block) for t in in_terms]
        + [(d_after, few, row_block), (text_embed, few, row_block)]
        + [(slot_rows, (1,) + few, slot_index(here)), (table,), (gain_in,)],
        [
            ((rows, width), F32, few, row_block),
            ((1, width), F32, None, None),
            ((1, width), F32, None, None),
        ],
    )
    kind = (jnp.arange(3) == meta[KIND]).astype(F32)[:, None]
    sums, parts = sum_small(
        jnp.concatenate([kind * type_local, gain_in_local, gain_ffn_local]),
        jnp.concatenate(
            [
                (gain_mid_near + gain_mid_far)[0],
                (gain_near + gain_far)[0],
                query_local.reshape(-1),
            ]
        ),
    )
    query_grad = jnp.swapaxes(parts[:, wide + ff :].reshape(mp, latent, wide), 0, 1)
    return (
        layer_out,
        text_grad,
        clip_grad,
        sums[:3],
        sums[3],
        qkv_grad,
        parts[:, :wide].reshape(-1),
        out_grad,
        sums[4],
        up_grad,
        parts[:, wide : wide + ff].reshape(-1),
        down_grad,
        query_grad.reshape(latent, width),
        kv_grad[:, :wide],
        kv_grad[:, wide:],
        res_out_grad,
    )


def solution(mesh):
    return jax.shard_map(
        shards,
        mesh=mesh,
        in_specs=(
            P(("dp", "mp"), None),
            P("dp", None, None),
            P(),
            P(),
            P(None, None, "mp"),
            P("mp"),
            P("mp", None),
            P(),
            P(None, "mp"),
            P("mp"),
            P("mp", None),
            P(None, "mp"),
            P(None, "mp"),
            P(None, "mp"),
            P("mp", None),
            P(("dp", "mp"), None),
            P(),
            P(),
            P(),
            P(),
        ),
        out_specs=(
            P(("dp", "mp"), None),
            P(("dp", "mp"), None),
            P("dp", "mp", None),
            P(),
            P(),
            P("dp", None, "mp"),
            P(),
            P("mp", "dp"),
            P(),
            P("dp", "mp"),
            P(),
            P("mp", "dp"),
            P(),
            P("dp", "mp"),
            P("dp", "mp"),
            P("mp", "dp"),
        ),
        check_vma=False,
    )
```

```python
import functools

import jax
import jax.numpy as jnp
from jax import lax
from jax.experimental import pallas as pl
from jax.experimental.pallas import tpu as pltpu
from jax.sharding import PartitionSpec as P

HEAD = 64
LANES = 128
EPS = 1e-05
NEG = -1e30
XPOS_BASE = 512.0
BF = jnp.bfloat16
F32 = jnp.float32
ROWS_BY_ROWS = (((1,), (1,)), ((), ()))
PLAIN = (((1,), (0,)), ((), ()))
OVER_ROWS = (((0,), (0,)), ((), ()))
KIND, PART, GROUP, REAL, POS, SOURCE, BLOCK, RANK = 0, 1, 2, 4, 8, 12, 16, 32
VMEM_BYTES = 28 * 1024 * 1024


def dot(left, right, form=PLAIN):
    return lax.dot_general(left, right, form, preferred_element_type=F32)


def dot_exact(left, right, form=ROWS_BY_ROWS):
    return lax.dot_general(
        left, right, form, precision=lax.Precision.HIGHEST, preferred_element_type=F32
    )


def swap(values, axis, bit):
    size = lax.axis_size(axis)
    return lax.ppermute(values, axis, [(i, i ^ bit) for i in range(size)])


def bits_of(size):
    return [1 << i for i in range(size.bit_length() - 1)]


def gather_rel(values):
    size = lax.axis_size("mp")
    pieces = {0: values}
    for bit in reversed(bits_of(size)):
        pieces[bit] = swap(values, "mp", bit)
    for j in range(size):
        if j not in pieces:
            low = j & -j
            pieces[j] = swap(pieces[j ^ low], "mp", low)
    return [pieces[j] for j in range(size)]


def add_low(first, second):
    return (first.astype(F32) + second.astype(F32)).astype(BF)


def scatter_pairs(even, odd):
    near = add_low(even, swap(odd, "mp", 1))
    return near[0], swap(near[1], "mp", 2), near


def sum_pairs(even, odd):
    own, far, _ = scatter_pairs(even, odd)
    return own.astype(F32) + far.astype(F32)


def pick(values, indices):
    return jnp.stack([lax.dynamic_index_in_dim(values, i, 0, keepdims=False) for i in indices])


def by_mp(values):
    me = lax.axis_index("mp")
    return pick(values, [me ^ j for j in range(lax.axis_size("mp"))])


def halve(values, axis):
    return (
        lax.index_in_dim(values, 0, axis, keepdims=False),
        lax.index_in_dim(values, 1, axis, keepdims=False),
    )


def scatter_dp(values, bits, last):
    for bit in bits:
        values = values.reshape((-1, 2) + values.shape[1:])
        keep, send = halve(values, 1)
        got = swap(send, "dp", bit)
        total = keep.astype(F32) + got.astype(F32)
        values = total.astype(last if bit == bits[-1] else BF)
    return values[0]


class Order:
    mark = None
    channel = 0


def call(body, meta, grid, ins, outs, scratch=(), aliases=None, remote=False, after=(), cost=1):
    arrays, specs = [], []
    for item in ins:
        arrays.append(item[0])
        if len(item) == 1:
            dims = item[0].ndim
            specs.append(
                pl.BlockSpec(
                    item[0].shape,
                    lambda *_, dims=dims: (0,) * dims,
                    pipeline_mode=pl.Buffered(1),
                )
            )
        elif item[1] is None:
            specs.append(pl.BlockSpec(memory_space=pl.ANY))
        else:
            specs.append(pl.BlockSpec(item[1], item[2]))
    shapes, out_specs = [], []
    for shape, dtype, block, index in list(outs) + [((8, LANES), F32, None, None)]:
        shapes.append(jax.ShapeDtypeStruct(shape, dtype))
        if index == "any":
            out_specs.append(pl.BlockSpec(memory_space=pl.ANY))
        elif block is None:
            dims = len(shape)
            out_specs.append(pl.BlockSpec(shape, lambda *_, dims=dims: (0,) * dims))
        else:
            out_specs.append(pl.BlockSpec(block, index))
    count, after = len(ins), list(after)
    if Order.mark is not None:
        after.append(Order.mark)
    specs += [pl.BlockSpec(memory_space=pl.ANY)] * len(after)

    params = pltpu.CompilerParams(vmem_limit_bytes=VMEM_BYTES)
    if remote:
        Order.channel += 1
        params = pltpu.CompilerParams(
            vmem_limit_bytes=VMEM_BYTES, collective_id=Order.channel, has_side_effects=True
        )

    def marked(meta_ref, *refs):
        refs = refs[:count] + refs[count + len(after) :]
        place = count + len(outs)
        refs[place][...] = jnp.zeros((8, LANES), F32)
        body(meta_ref, *refs[:place], *refs[place + 1 :])

    result = pl.pallas_call(
        marked,
        out_shape=shapes,
        grid_spec=pltpu.PrefetchScalarGridSpec(
            num_scalar_prefetch=1,
            grid=grid,
            in_specs=specs,
            out_specs=out_specs,
            scratch_shapes=list(scratch),
        ),
        input_output_aliases=aliases or {},
        compiler_params=params,
        cost_estimate=pl.CostEstimate(
            flops=cost * 40000000, bytes_accessed=1024, transcendentals=0
        ),
        name=getattr(body, "func", body).__name__,
    )(meta, *arrays, *after)
    Order.mark = result[-1]
    return result[:-1]


def norm_parts(values):
    width = values.shape[-1]
    mean = jnp.sum(values, axis=-1, keepdims=True) / width
    square = jnp.sum(values * values, axis=-1, keepdims=True) / width
    inv_std = lax.rsqrt(square - mean * mean + EPS)
    return (values - mean) * inv_std, inv_std


def norm_back(upstream, normed, inv_std, gain):
    width = upstream.shape[-1]
    scaled = upstream * gain
    first = jnp.sum(scaled, axis=-1, keepdims=True) / width
    second = jnp.sum(scaled * normed, axis=-1, keepdims=True) / width
    return inv_std * (scaled - first - normed * second)


def columns_of(rows):
    count, length = rows.shape
    full = jnp.concatenate([rows, jnp.zeros((LANES - count, length), F32)], axis=0)
    return full.T


def lane_sums(values):
    total = values[:, :LANES]
    for start in range(LANES, values.shape[1], LANES):
        total = total + values[:, start : start + LANES]
    return total


def rows_from(partials):
    return dot_exact(jnp.ones((8, LANES), F32), partials)


def two_rows(first, second):
    row = lax.broadcasted_iota(jnp.int32, first.shape, 0)
    return jnp.where(row == 0, first, jnp.where(row == 1, second, 0.0))


def meta_body(count_ref, seq_ref, slot_ref, kind_ref, me_ref, out_ref, *, image_local, slots, images):
    me_m, me_d = me_ref[0], me_ref[1]

    def clear(i, _):
        out_ref[i] = 0
        return 0

    lax.fori_loop(0, BLOCK, clear, 0)

    def absent(i, _):
        out_ref[BLOCK + i] = -1
        return 0

    lax.fori_loop(0, RANK - BLOCK + images, absent, 0)
    out_ref[KIND] = kind_ref[me_d]
    out_ref[PART] = me_m
    out_ref[GROUP] = me_d
    for s in range(slots):
        out_ref[POS + s] = slot_ref[me_d, s]

    def one(i, found):
        owner = i // image_local
        inside = i - owner * image_local
        here = jnp.logical_and(inside < count_ref[owner], seq_ref[i] == me_d)
        rank = jnp.minimum(found, slots - 1)

        @pl.when(here)
        def _():
            out_ref[REAL + rank] = 1
            out_ref[SOURCE + rank] = (owner ^ me_d) * image_local + inside
            out_ref[BLOCK + slot_ref[me_d, rank]] = rank
            out_ref[RANK + i] = rank

        return found + here.astype(jnp.int32)

    lax.fori_loop(0, images, one, jnp.int32(0))


def make_meta(owner_count, image_seq, slot_block, seq_kind, image_local):
    me = jnp.stack([lax.axis_index("mp"), lax.axis_index("dp")]).astype(jnp.int32)
    images = image_seq.shape[0]
    smem = pl.BlockSpec(memory_space=pltpu.SMEM)
    return pl.pallas_call(
        functools.partial(
            meta_body, image_local=image_local, slots=slot_block.shape[1], images=images
        ),
        out_shape=jax.ShapeDtypeStruct((RANK + images,), jnp.int32),
        in_specs=[smem] * 5,
        out_specs=smem,
    )(owner_count, image_seq, slot_block, seq_kind, me)


def other_of(me, j):
    return [me, me + 1 - 2 * (me % 2), (me + 2) % 4, 3 - me][j]


def pair_sums(terms, out_refs, scratch):
    sent, came, kept, send_sem, recv_sem = scratch
    step, steps = pl.program_id(0), pl.num_programs(0)
    partner = {"mp": other_of(lax.axis_index("mp"), 1)}

    @pl.when(step == 0)
    def _():
        barrier = pltpu.get_barrier_semaphore()
        pl.semaphore_signal(barrier, inc=1, device_id=partner)
        pl.semaphore_wait(barrier, 1)

    def move(n, place):
        return pltpu.make_async_remote_copy(
            src_ref=sent.at[n, place],
            dst_ref=came.at[n, place],
            send_sem=send_sem.at[n, place],
            recv_sem=recv_sem.at[n, place],
            device_id=partner,
        )

    for n, (mine, theirs) in enumerate(terms):
        sent[n, step] = theirs().astype(BF)
        move(n, step).start()
        kept[n, step] = mine()

    @pl.when(step == steps - 1)
    def _():
        tile = sent.shape[-1]
        for n, out_ref in enumerate(out_refs):
            for place in range(sent.shape[1]):
                move(n, place).wait()
                total = kept[n, place] + came[n, place].astype(F32)
                out_ref[:, place * tile : (place + 1) * tile] = total.astype(BF)


def flipped(me, bit):
    return me + bit * (1 - 2 * ((me // bit) % 2))


def exchange(meta, *items):
    places = sorted({(axis, bit) for _, axis, bit in items})
    count = len(items)

    def body(meta_ref, *refs):
        sources, targets, (send_sem, recv_sem) = refs[:count], refs[count : 2 * count], refs[-2:]

        def partner(axis, bit):
            me = lax.axis_index(axis)
            for one in bits_of(lax.axis_size(axis)):
                if bit & one:
                    me = flipped(me, one)
            return {axis: me}

        barrier = pltpu.get_barrier_semaphore()
        for axis, bit in places:
            pl.semaphore_signal(barrier, inc=1, device_id=partner(axis, bit))
        pl.semaphore_wait(barrier, len(places))
        copies = [
            pltpu.make_async_remote_copy(
                src_ref=sources[n],
                dst_ref=targets[n],
                send_sem=send_sem.at[n],
                recv_sem=recv_sem.at[n],
                device_id=partner(axis, bit),
            )
            for n, (_, axis, bit) in enumerate(items)
        ]
        for copy in copies:
            copy.start()
        for copy in copies:
            copy.wait()

    return call(
        body,
        meta,
        (1,),
        [(array, None) for array, _, _ in items],
        [(array.shape, array.dtype, None, "any") for array, _, _ in items],
        scratch=[pltpu.SemaphoreType.DMA((count,)), pltpu.SemaphoreType.DMA((count,))],
        remote=True,
    )


def spread_stats(meta, values):
    others = range(1, lax.axis_size("mp"))
    return [values] + list(exchange(meta, *[(values, "mp", b) for b in others]))


def gather_now(meta, values):
    far, near = exchange(meta, (values, "mp", 2), (values, "mp", 1))
    return [values, near, far, exchange(meta, (far, "mp", 1))[0]]


def scatter_now(meta, even, odd):
    near = add_low(even, exchange(meta, (odd, "mp", 1))[0])
    return near[0], exchange(meta, (near[1], "mp", 2))[0]


def pair_scratch(count, steps, rows, tile):
    shape = (count, steps, rows, tile)
    return [
        pltpu.VMEM(shape, BF),
        pltpu.VMEM(shape, BF),
        pltpu.VMEM(shape, F32),
        pltpu.SemaphoreType.DMA((count, steps)),
        pltpu.SemaphoreType.DMA((count, steps)),
    ]


def kind_of(meta, table_ref):
    return table_ref[pl.ds(meta[KIND], 1), :]


def text_body(meta, text_ref, table_ref, gain_ref, out_ref):
    mixed = text_ref[...].astype(F32) + kind_of(meta, table_ref)
    out_ref[...] = (norm_parts(mixed)[0] * gain_ref[...]).astype(BF)


def rotated(values, cosine, sine):
    width = values.shape[1]
    lane = lax.broadcasted_iota(jnp.int32, values.shape, 1)
    other = jnp.where(
        lane % HEAD < HEAD // 2,
        pltpu.roll(values, width - HEAD // 2, 1),
        pltpu.roll(values, HEAD // 2, 1),
    )
    repeat = width // LANES
    cosine = jnp.concatenate([cosine] * repeat, axis=1)
    sine = jnp.concatenate([sine] * repeat, axis=1)
    return values * cosine + other * sine


def qkv_body(meta, near_ref, far_ref, weight_ref, turn_ref, *refs, which):
    out_ref, in_ref = refs[-2:]
    rows = near_ref.shape[0]
    for n, ref in enumerate((near_ref, far_ref)):
        at = pl.ds(pl.multiple_of(((meta[PART] ^ (which + n)) % 2) * rows, rows), rows)
        product = dot(ref[...], weight_ref[0])
        out_ref[at, :] = rotated(product, turn_ref[0, 0, at, :], turn_ref[0, 1, at, :]).astype(BF)
        in_ref[at, :] = ref[...]


def project(meta, pieces, weight, turn, before, which, after=()):
    rows, depth = pieces[0].shape
    width = weight.shape[2]
    length = rows * lax.axis_size("mp")
    pair = lambda m: (m[PART] ^ which) // 2
    ins = [(pieces[0],), (pieces[1],), (weight, (1, depth, width), lambda i, m: (i, 0, 0))]
    ins.append((turn, (1, 2, 2 * rows, LANES), lambda i, m: (i, 0, pair(m), 0)))
    aliases = {}
    if before is not None:
        for n, array in enumerate(before):
            ins.append((array, None))
            aliases[5 + n] = n
    return call(
        functools.partial(qkv_body, which=which),
        meta,
        (3,),
        ins,
        [
            ((length, 3 * width), BF, (2 * rows, width), lambda i, m: (pair(m), i)),
            ((length, depth), BF, (2 * rows, depth), lambda i, m: (pair(m), 0)),
        ],
        aliases=aliases,
        after=after,
    )


def slot_body(meta, *refs, mp, slots, latent):
    pieces = refs[:mp]
    table_ref, gain_ref, weight_ref, turn_ref, qkv_in, x_in = refs[mp : mp + 6]
    qkv_ref, x_ref, slots_ref, rows_ref, new_ref, norm_ref = refs[mp + 6 :]
    step = pl.program_id(0)
    part = latent // mp

    @pl.when(step == 0)
    def _():
        for j in range(mp):
            place = pl.multiple_of((meta[PART] ^ j) * part, part)
            for s in range(slots):
                rows_ref[s, pl.ds(place, part), :] = pieces[j][s].astype(F32)
        mixed = rows_ref[...].reshape(slots * latent, -1)
        slots_ref[...] = mixed.astype(BF).reshape(slots_ref.shape)
        mixed = mixed + kind_of(meta, table_ref)
        normed = (norm_parts(mixed)[0] * gain_ref[...]).astype(BF)
        norm_ref[...] = normed.reshape(norm_ref.shape)

    @pl.when(step < 3)
    def _():
        product = dot(norm_ref[...].reshape(slots * latent, -1), weight_ref[0])
        new_ref[step] = product.reshape(new_ref.shape[1:])

    @pl.when(step >= 3)
    def _():
        slot = step - 3
        real = meta[REAL + slot] > 0
        width = new_ref.shape[-1]
        for c in range(3):
            at = slice(c * width, (c + 1) * width)
            value = rotated(new_ref[c, slot], turn_ref[c, 0], turn_ref[c, 1]).astype(BF)
            qkv_ref[:, at] = jnp.where(real, value, qkv_in[:, at])
        x_ref[...] = jnp.where(real, norm_ref[slot], x_in[...])


def turn_tables(length):
    positions = jnp.arange(length, dtype=F32)[:, None]
    lane = jnp.arange(LANES)
    ladder = (lane % (HEAD // 2)).astype(F32)
    angle = positions * jnp.power(10000.0, -2.0 * ladder / HEAD)[None, :]
    decay = (2.0 * ladder + 0.4 * HEAD) / (1.4 * HEAD)
    power = (positions - length // 2) / XPOS_BASE
    sign = jnp.where(lane % HEAD < HEAD // 2, -1.0, 1.0)[None, :]
    cosine, sine = jnp.cos(angle), jnp.sin(angle) * sign
    up = jnp.power(decay[None, :], power)
    down = jnp.power(decay[None, :], -power)
    one, zero = jnp.ones_like(cosine), jnp.zeros_like(cosine)
    return jnp.stack(
        [
            jnp.stack([cosine * up, sine * up]),
            jnp.stack([cosine * down, sine * down]),
            jnp.stack([one, zero]),
        ]
    )


def pool_shares_of(query, keys, head):
    lane = lax.broadcasted_iota(jnp.int32, query.shape, 1)
    masked = jnp.where(lane // HEAD == head, query, jnp.zeros_like(query))
    scores = dot(masked, keys, ROWS_BY_ROWS) * 0.125
    top = jnp.max(scores, axis=-1, keepdims=True)
    weights = jnp.exp(scores - top)
    return weights / jnp.sum(weights, axis=-1, keepdims=True)


def pool_body(
    meta, clip_ref, key_w, value_w, query_ref, key_ref, value_ref, pool_ref, *, images
):
    clip = clip_ref[...]
    key_ref[...] = dot(clip, key_w[...]).astype(BF)
    value_ref[...] = dot(clip, value_w[...]).astype(BF)
    patches = clip.shape[0] // images
    latent = query_ref.shape[0]
    for i in range(images):
        for pair in range(query_ref.shape[1] // LANES):
            lanes = slice(pair * LANES, (pair + 1) * LANES)
            rows = slice(i * patches, (i + 1) * patches)
            query, keys, values = query_ref[:, lanes], key_ref[rows, lanes], value_ref[rows, lanes]
            lane = lax.broadcasted_iota(jnp.int32, query.shape, 1)
            heads = [
                dot(pool_shares_of(query, keys, h).astype(BF), values) for h in range(2)
            ]
            pool_ref[i * latent : (i + 1) * latent, lanes] = jnp.where(
                lane < HEAD, heads[0], heads[1]
            ).astype(BF)


def pooled_body(meta, *refs, slots, mp):
    pieces, out_w, even_ref, odd_ref, scratch = refs[:slots], refs[slots], *refs[slots + 1 :]
    rows = jnp.concatenate([p[...] for p in pieces], axis=0)
    scratch[...] = dot(rows, out_w[...])
    latent = pieces[0].shape[0]
    part = latent // mp
    for j in range(mp):
        for s in range(slots):
            start = pl.multiple_of(s * latent + (meta[PART] ^ j) * part, part)
            (odd_ref if j % 2 else even_ref)[j // 2, s] = scratch[pl.ds(start, part), :].astype(BF)


def copy_body(meta, in_ref, out_ref):
    out_ref[...] = in_ref[...]


def head_lanes(pair, width):
    return [
        pl.ds(pl.multiple_of(c * width + pair * LANES, LANES), LANES) for c in range(3)
    ]


def attend_body(meta, qkv_ref, out_ref, lse_ref, stat_ref, first, second, lse, *, block):
    length, width = out_ref.shape
    first[...] = jnp.zeros_like(first)
    second[...] = jnp.zeros_like(second)

    def pair(hp, _):
        lanes, k_lanes, v_lanes = head_lanes(hp, width)
        keys, values = qkv_ref[:, k_lanes], qkv_ref[:, v_lanes]
        lane = lax.broadcasted_iota(jnp.int32, (block, LANES), 1)
        row = lax.broadcasted_iota(jnp.int32, (block, block), 0)
        col = lax.broadcasted_iota(jnp.int32, (block, block), 1)
        for b in range(length // block):
            rows = slice(b * block, (b + 1) * block)
            end = (b + 1) * block
            query = qkv_ref[rows, lanes]
            outs = []
            for h in range(2):
                masked = jnp.where(lane // HEAD == h, query, jnp.zeros_like(query))
                scores = dot(masked, keys[:end], ROWS_BY_ROWS) * 0.125
                edge = jnp.where(row >= col, scores[:, b * block :], NEG)
                scores = edge if b == 0 else jnp.concatenate([scores[:, : b * block], edge], axis=1)
                top = jnp.max(scores, axis=-1, keepdims=True)
                weights = jnp.exp(scores - top)
                total = jnp.sum(weights, axis=-1, keepdims=True)
                outs.append(dot(weights.astype(BF), values[:end]) / total)
                lse[rows, :] = jnp.where(lane == 2 * hp + h, top + jnp.log(total), lse[rows, :])
            out = jnp.where(lane < HEAD, outs[0], outs[1])
            first[rows, :] += out
            second[rows, :] += out * out
            out_ref[rows, lanes] = out.astype(BF)
        return 0

    lax.fori_loop(0, width // LANES, pair, 0)
    lse_ref[...] = lse[...].T[: lse_ref.shape[0]]
    stat_ref[...] = two_rows(rows_from(first[...]), rows_from(second[...]))


def total_columns(stats):
    total = stats[0][...]
    for other in stats[1:]:
        total = total + other[...]
    return columns_of(total)


def stat_norm(values, columns, at, width):
    mean = columns[:, at : at + 1] / width
    square = columns[:, at + 1 : at + 2] / width
    inv_std = lax.rsqrt(square - mean * mean + EPS)
    return (values - mean) * inv_std, inv_std


def mid_body(meta, att_ref, gain_ref, *refs, mp, width):
    normed, _ = stat_norm(att_ref[...].astype(F32), total_columns(refs[:mp]), 0, width)
    refs[mp][...] = (normed * gain_ref[...]).astype(BF)


def out_body(meta, rows_ref, weight_ref, out_ref, *scratch):
    rows = out_ref.shape[0]
    pair_sums(
        [
            (
                lambda: dot(rows_ref[:rows, :], weight_ref[...]),
                lambda: dot(rows_ref[rows:, :], weight_ref[...]),
            )
        ],
        [out_ref],
        scratch,
    )


def back_body(meta, rows_ref, weight_ref, out_ref, *scratch):
    rows = out_ref.shape[0]
    pair_sums(
        [
            (
                lambda: dot(rows_ref[:rows, :], weight_ref[...], ROWS_BY_ROWS),
                lambda: dot(rows_ref[rows:, :], weight_ref[...], ROWS_BY_ROWS),
            )
        ],
        [out_ref],
        scratch,
    )


def after_body(meta, own_ref, far_ref, text_ref, slots_ref, table_ref, gain_ref, after_ref, low_ref):
    mixed = mixed_rows(meta, text_ref, slots_ref, table_ref)
    after = mixed + (own_ref[...].astype(F32) + far_ref[...].astype(F32))
    after_ref[...] = after
    low_ref[...] = (norm_parts(after)[0] * gain_ref[...]).astype(BF)


def mixed_rows(meta, text_ref, slots_ref, table_ref):
    block = meta[PART] * pl.num_programs(0) + pl.program_id(0)
    filled = meta[BLOCK + block] >= 0
    return (
        jnp.where(filled, slots_ref[0].astype(F32), text_ref[...].astype(F32))
        + kind_of(meta, table_ref)
    )


def slot_index(blocks):
    return lambda i, m: (jnp.maximum(m[BLOCK + m[PART] * blocks + i], 0), 0, 0)


def times_rows_body(meta, *refs, count):
    pieces, weight_ref, outs = refs[:count], refs[count], refs[-count:]
    for piece, out_ref in zip(pieces, outs):
        out_ref[...] = dot(piece[...], weight_ref[...], ROWS_BY_ROWS).astype(out_ref.dtype)


def up_body(meta, a_ref, b_ref, weight_ref, dup_a, dup_b, gain_ref, *refs):
    act_ref, slope_ref, stat_ref = refs[-7:-4]
    sums = refs[-4:]
    step = pl.program_id(0)
    rows = a_ref.shape[0]

    @pl.when(step == 0)
    def _():
        for ref in sums:
            ref[...] = jnp.zeros_like(ref)

    for n, (ref, dup_ref) in enumerate(((a_ref, dup_a), (b_ref, dup_b))):
        here = slice(n * rows, (n + 1) * rows)
        pre = dot(ref[...], weight_ref[...])
        share = 0.5 + 0.5 * lax.erf(pre * (0.5**0.5))
        density = jnp.exp(pre * pre * -0.5) * ((2.0 * jnp.pi) ** -0.5)
        act = pre * share
        act_ref[here, :] = act.astype(BF)
        slope_ref[here, :] = (share + pre * density).astype(BF)
        scaled = dup_ref[...].astype(F32) * gain_ref[...]
        for ref_sum, term in zip(sums, (act, act * act, scaled, scaled * act)):
            ref_sum[here, :] += lane_sums(term)

    @pl.when(step == pl.num_programs(0) - 1)
    def _():
        rows_of = [rows_from(ref_sum[...]) for ref_sum in sums]
        row = lax.broadcasted_iota(jnp.int32, rows_of[0].shape, 0)
        total = jnp.zeros_like(rows_of[0])
        for n, value in enumerate(rows_of):
            total = jnp.where(row == n, value, total)
        stat_ref[...] = total


def spread_body(meta, act_ref, slope_ref, dup_0, dup_1, dup_2, dup_3, gain_ref, *refs, mp, width):
    stats = refs[:mp]
    pre_ref, low_ref, grad_ref = refs[mp:]
    columns = total_columns(stats)
    act = act_ref[...].astype(F32)
    normed, inv_std = stat_norm(act, columns, 0, width)
    gain = gain_ref[...]
    low_ref[...] = (normed * gain).astype(BF)
    step = pl.program_id(0) // (pl.num_programs(0) // 4)
    upstream = jnp.where(
        step < 2,
        jnp.where(step == 0, dup_0[...], dup_1[...]),
        jnp.where(step == 2, dup_2[...], dup_3[...]),
    ).astype(F32)
    first = columns[:, 2:3] / width
    mean = columns[:, 0:1] / width
    second = (columns[:, 3:4] - mean * columns[:, 2:3]) * inv_std / width
    d_act = inv_std * (upstream * gain - first - normed * second)
    pre_ref[...] = (d_act * slope_ref[...].astype(F32)).astype(BF)
    add_rows(grad_ref, upstream * normed)


def down_body(meta, low_ref, weight_ref, near_ref, far_ref, *scratch):
    rows = near_ref.shape[0]

    def term(j):
        return lambda: dot(low_ref[j * rows : (j + 1) * rows, :], weight_ref[...])

    pair_sums([(term(2), term(3)), (term(0), term(1))], [far_ref, near_ref], scratch)


def sum_body(meta, first_ref, second_ref, third_ref, out_ref):
    out_ref[...] = first_ref[...] + (second_ref[...].astype(F32) + third_ref[...].astype(F32))


def ffn_back_body(meta, own_ref, far_ref, after_ref, cot_ref, gain_ref, out_ref, low_ref, grad_ref):
    upstream = own_ref[...].astype(F32) + far_ref[...].astype(F32)
    normed, inv_std = norm_parts(after_ref[...])
    d_after = cot_ref[...].astype(F32) + norm_back(upstream, normed, inv_std, gain_ref[...])
    out_ref[...] = d_after
    low_ref[...] = d_after.astype(BF)
    add_rows(grad_ref, upstream * normed)


def add_rows(ref, values):
    total = jnp.sum(values, axis=0, keepdims=True)

    @pl.when(pl.program_id(0) == 0)
    def _():
        ref[...] = total

    @pl.when(pl.program_id(0) != 0)
    def _():
        ref[...] += total


def d_mid_body(meta, *refs, mp, width):
    pieces, weight_ref, gain_ref, att_ref = refs[:2], refs[2], refs[3], refs[4]
    stats = refs[5 : 5 + mp]
    out_ref, stat_ref, grad_ref = refs[-3:]
    rows = jnp.where(pl.program_id(0) == 0, pieces[0][...], pieces[1][...])
    d_mid = dot(rows, weight_ref[...], ROWS_BY_ROWS)
    out_ref[...] = d_mid.astype(BF)
    normed, _ = stat_norm(att_ref[...].astype(F32), total_columns(stats), 0, width)
    scaled = d_mid * gain_ref[...]
    add_rows(grad_ref, d_mid * normed)
    stat_ref[...] = two_rows(
        rows_from(lane_sums(scaled)), rows_from(lane_sums(scaled * normed))
    )


def attend_back_body(
    meta, qkv_ref, att_ref, dmid_ref, lse_ref, gain_ref, turn_ref, *refs, mp, width, block
):
    stats, more = refs[:mp], refs[mp : 2 * mp]
    out_ref, d_att, dq, dk, dv = refs[2 * mp :]
    length, wide = att_ref.shape
    columns = total_columns(stats)
    normed, inv_std = stat_norm(att_ref[...].astype(F32), columns, 0, width)
    sums = total_columns(more)
    scaled = dmid_ref[...].astype(F32) * gain_ref[...]
    d_att[...] = (
        inv_std * (scaled - sums[:, 0:1] / width - normed * (sums[:, 1:2] / width))
    ).astype(BF)

    def pair(hp, _):
        lanes, k_lanes, v_lanes = head_lanes(hp, wide)
        keys, values = qkv_ref[:, k_lanes], qkv_ref[:, v_lanes]
        lane = lax.broadcasted_iota(jnp.int32, (block, LANES), 1)
        row = lax.broadcasted_iota(jnp.int32, (block, block), 0)
        col = lax.broadcasted_iota(jnp.int32, (block, block), 1)
        dk[...] = jnp.zeros_like(dk)
        dv[...] = jnp.zeros_like(dv)
        both = d_att[:, lanes].astype(F32) * att_ref[:, lanes].astype(F32)
        side = lax.broadcasted_iota(jnp.int32, (8, LANES), 1) // HEAD
        pick_head = lax.broadcasted_iota(jnp.int32, (8, LANES), 0) == side
        inner = dot_exact(pick_head.astype(F32), both)
        for b in range(length // block):
            rows = slice(b * block, (b + 1) * block)
            end = (b + 1) * block
            query, grad = qkv_ref[rows, lanes], d_att[rows, lanes]
            d_query = jnp.zeros((block, LANES), F32)
            for h in range(2):
                keep = lane // HEAD == h
                q_one = jnp.where(keep, query, jnp.zeros_like(query))
                g_one = jnp.where(keep, grad, jnp.zeros_like(grad))
                scores = dot(keys[:end], q_one, ROWS_BY_ROWS) * 0.125
                shares = jnp.exp(scores - lse_ref[pl.ds(2 * hp + h, 1), rows])
                edge = jnp.where(col >= row, shares[b * block :], 0.0)
                shares = edge if b == 0 else jnp.concatenate([shares[: b * block], edge], axis=0)
                d_shares = dot(values[:end], g_one, ROWS_BY_ROWS)
                d_scores = (shares * (d_shares - inner[h : h + 1, rows])).astype(BF)
                dv[:end, :] += dot(shares.astype(BF), g_one)
                dk[:end, :] += dot(d_scores, q_one)
                turned = dot(d_scores, keys[:end], OVER_ROWS)
                d_query = jnp.where(keep, turned, d_query)
            dq[rows, :] = d_query
        out_ref[:, lanes] = rotated(
            dq[...] * 0.125, turn_ref[0, 0], -turn_ref[0, 1]
        ).astype(BF)
        out_ref[:, k_lanes] = rotated(
            dk[...] * 0.125, turn_ref[1, 0], -turn_ref[1, 1]
        ).astype(BF)
        out_ref[:, v_lanes] = dv[...].astype(BF)
        return 0

    lax.fori_loop(0, wide // LANES, pair, 0)


def three_dots(rows, weight_ref):
    width = weight_ref.shape[2]
    total = None
    for c in range(3):
        term = dot(rows[:, c * width : (c + 1) * width], weight_ref[c], ROWS_BY_ROWS)
        total = term if total is None else total + term
    return total


def slot_back_body(meta, *refs, slots, mp):
    pieces, weight_ref, even_ref, odd_ref, scratch = refs[:slots], refs[slots], *refs[-3:]
    rows = jnp.concatenate([p[...] for p in pieces], axis=0)
    scratch[...] = three_dots(rows, weight_ref)
    latent = pieces[0].shape[0]
    part = latent // mp
    for j in range(mp):
        for s in range(slots):
            start = pl.multiple_of(s * latent + (meta[PART] ^ j) * part, part)
            (odd_ref if j % 2 else even_ref)[j // 2, s] = scratch[pl.ds(start, part), :].astype(BF)


def row_back_body(meta, rows_ref, weight_ref, out_ref, *scratch, which):
    rows = out_ref.shape[0]
    me = lax.axis_index("mp")

    def term(j):
        at = pl.ds(pl.multiple_of(other_of(me, j) * rows, rows), rows)
        return lambda: three_dots(rows_ref[at, :], weight_ref)

    pair_sums([(term(which), term(which + 1))], [out_ref], scratch)


def slot_grad_body(meta, *refs, mp, slots, latent, images, groups):
    own_ref, far_ref, slots_ref, table_ref, gain_ref = refs[:5]
    after, (keep_ref, send_ref, grad_ref) = refs[5:-3], refs[-3:]
    part = latent // mp
    start = pl.multiple_of(meta[PART] * part, part)
    for s in range(slots):
        upstream = own_ref[s].astype(F32) + far_ref[s].astype(F32)
        mixed = slots_ref[s, pl.ds(start, part), :].astype(F32) + kind_of(meta, table_ref)
        normed, inv_std = norm_parts(mixed)
        block = meta[POS + s]
        blocks = after[0].shape[0] // latent
        rel = (block // blocks) ^ meta[PART]
        row = pl.multiple_of((block % blocks) * latent + start, part)
        d_after = after[0][pl.ds(row, part), :]
        for j in range(1, mp):
            d_after = jnp.where(rel == j, after[j][pl.ds(row, part), :], d_after)
        grad_ref[s] = (
            d_after.astype(F32) + norm_back(upstream, normed, inv_std, gain_ref[...])
        ).astype(BF)
    for k in range(groups):
        for i in range(images):
            rank = meta[RANK + (k ^ meta[GROUP]) * images + i]
            value = grad_ref[jnp.maximum(rank, 0)]
            value = jnp.where(rank >= 0, value, jnp.zeros_like(value))
            (send_ref if k % 2 else keep_ref)[k // 2, i * part : (i + 1) * part, :] = value


def in_back_body(
    meta, own_ref, far_ref, after_ref, text_ref, slots_ref, table_ref, gain_ref, out_ref, gain_grad, type_grad
):
    upstream = own_ref[...].astype(F32) + far_ref[...].astype(F32)
    normed, inv_std = norm_parts(mixed_rows(meta, text_ref, slots_ref, table_ref))
    d_mixed = after_ref[...] + norm_back(upstream, normed, inv_std, gain_ref[...])
    block = meta[PART] * pl.num_programs(0) + pl.program_id(0)
    out_ref[...] = jnp.where(meta[BLOCK + block] >= 0, 0.0, d_mixed)
    add_rows(gain_grad, upstream * normed)
    add_rows(type_grad, d_mixed)


def pool_back_body(
    meta, *refs, images, mp
):
    pieces, out_w, key_ref, value_ref, query_ref, key_w, value_w = refs[:mp], *refs[mp : mp + 6]
    kv_ref, query_grad, clip_even, clip_odd, grad_ref, scratch = refs[mp + 6 :]
    part = pieces[0].shape[1]
    for j in range(mp):
        for i in range(images):
            start = pl.multiple_of(i * part * mp + (meta[PART] ^ j) * part, part)
            grad_ref[pl.ds(start, part), :] = pieces[j][i]
    d_heads = dot(grad_ref[...], out_w[...], ROWS_BY_ROWS).astype(BF)
    patches = key_ref.shape[0] // images
    latent, wide = query_ref.shape
    for pair in range(wide // LANES):
        lanes = slice(pair * LANES, (pair + 1) * LANES)
        query = query_ref[:, lanes]
        lane = lax.broadcasted_iota(jnp.int32, query.shape, 1)
        d_query = jnp.zeros((latent, LANES), F32)
        for i in range(images):
            rows = slice(i * patches, (i + 1) * patches)
            keys, values = key_ref[rows, lanes], value_ref[rows, lanes]
            grad = d_heads[i * latent : (i + 1) * latent, lanes]
            d_keys = jnp.zeros((patches, LANES), F32)
            d_values = jnp.zeros((patches, LANES), F32)
            for h in range(2):
                keep = lane // HEAD == h
                shares = pool_shares_of(query, keys, h)
                g_one = jnp.where(keep, grad, jnp.zeros_like(grad))
                q_one = jnp.where(keep, query, jnp.zeros_like(query))
                d_shares = dot(g_one, values, ROWS_BY_ROWS)
                inner = jnp.sum(shares * d_shares, axis=-1, keepdims=True)
                d_scores = (shares * (d_shares - inner)).astype(BF)
                d_query += jnp.where(keep, dot(d_scores, keys), 0.0)
                d_keys += dot(d_scores, q_one, OVER_ROWS)
                d_values += dot(shares.astype(BF), g_one, OVER_ROWS)
            kv_ref[rows, lanes] = (d_keys * 0.125).astype(BF)
            kv_ref[rows, slice(wide + pair * LANES, wide + (pair + 1) * LANES)] = d_values.astype(BF)
        query_grad[:, lanes] = d_query * 0.125
    scratch[...] = dot(kv_ref[:, :wide], key_w[...], ROWS_BY_ROWS) + dot(
        kv_ref[:, wide:], value_w[...], ROWS_BY_ROWS
    )
    piece = patches // mp
    for j in range(mp):
        for i in range(images):
            start = pl.multiple_of(i * patches + (meta[PART] ^ j) * piece, piece)
            (clip_odd if j % 2 else clip_even)[j // 2, i] = scratch[
                pl.ds(start, piece), :
            ].astype(BF)


def weight_body(meta, *refs, lefts, rights, before, has_got, split):
    left, right = refs[:lefts], refs[lefts : lefts + rights]
    rest = refs[lefts + rights :]
    depth = sum(r.shape[0] for r in left)
    total = None
    step = depth // max(lefts, rights)
    for start in range(0, depth, step):
        l_ref, l_at = find(left, start)
        r_ref, r_at = find(right, start)
        term = dot(l_ref[l_at : l_at + step, :], r_ref[r_at : r_at + step, :], OVER_ROWS)
        total = term if total is None else total + term
    if split:
        wide = total.shape[1] // 2
        total = jnp.concatenate([total[:, :wide], total[:, wide:]], axis=0)
    if not has_got:
        rest[-1][0] = total.astype(BF)
        return
    even, odd = rest[-2:]
    total = (total + rest[0][0].astype(F32)).astype(BF)
    step = pl.program_id(0)

    @pl.when(step % 2 == 0)
    def _():
        even[0] = total

    @pl.when(step % 2 == 1)
    def _():
        odd[0] = total


def find(refs, start):
    for ref in refs:
        if start < ref.shape[0]:
            return ref, start
        start -= ref.shape[0]
    return None


def add_body(meta, keep_ref, got_ref, keep_out, send_out):
    keep_out[0] = (keep_ref[0].astype(F32) + got_ref[0].astype(F32)).astype(BF)
    send_out[0] = (keep_ref[1].astype(F32) + got_ref[1].astype(F32)).astype(BF)


def gathered_body(meta, left_ref, right_ref, out_ref):
    out_ref[...] = dot(left_ref[...], right_ref[...], OVER_ROWS)


def last_body(meta, keep_ref, got_ref, out_ref):
    out_ref[...] = (keep_ref[...].astype(F32) + got_ref[...].astype(F32)).astype(out_ref.dtype)


def plus(meta, first, second, dtype):
    shape = first.shape
    steps = 2 if shape[-2] % 32 == 0 and len(shape) == 2 else 1
    block = (shape[-2] // steps,) + shape[-1:]
    if len(shape) == 3:
        block = shape
    index = lambda i, m: (i,) + (0,) * (len(shape) - 1)
    return call(
        last_body,
        meta,
        (steps,),
        [(first, block, index), (second, block, index)],
        [(shape, dtype, block, index)],
    )[0]


def split_sum(meta, keep, got):
    count, *dims = keep.shape
    pair, one = (2,) + tuple(dims), (1,) + tuple(dims)
    at = lambda i, m: (i, 0, 0)
    return call(
        add_body,
        meta,
        (count // 2,),
        [(keep, pair, at), (got, pair, at)],
        [((count // 2,) + tuple(dims), BF, one, at)] * 2,
    )


def stack_body(meta, first_ref, second_ref, out_ref):
    out_ref[:, 0] = first_ref[...]
    out_ref[:, 1] = second_ref[...]


class GatherDp:
    def __init__(self, meta, values):
        self.meta, self.values = meta, values[None]
        self.pending = list(reversed(bits_of(lax.axis_size("dp"))))
        self.got = swap(self.values, "dp", self.pending.pop(0))

    def step(self):
        count, *dims = self.values.shape
        stacked = call(
            stack_body,
            self.meta,
            (1,),
            [(self.values,), (self.got,)],
            [((count, 2) + tuple(dims), self.values.dtype, None, None)],
        )[0]
        self.values = stacked.reshape((2 * count,) + tuple(dims))
        if self.pending:
            self.got = swap(self.values, "dp", self.pending.pop(0))

    def end(self):
        while self.pending:
            self.step()
        self.step()
        return self.values


class WeightGrads:
    def __init__(self, meta, members, shape, first=1, cost=1):
        self.meta, self.members, self.shape = meta, members, shape
        self.size = lax.axis_size("dp")
        bits = bits_of(self.size)
        widths = [left[0].shape[1] // self.size for left, *_ in members]
        self.plain = any(w % LANES for w in widths) or self.size < 8
        self.first, self.cost = first, cost
        self.order = [first] + [b for b in bits if b != first]
        self.pending = list(self.order)

    def run(self, side, got):
        half, first = self.size // 2, self.first
        before = None
        for left, right, split, at in self.members:
            part = left[0].shape[1] // self.size
            inner = right[0].shape[1]
            block = (1, 2 * part, inner // 2) if split else (1, part, inner)
            place = lambda i, m, at=at: (i,) + at
            pair_place = lambda i, m, at=at: (i // 2,) + at
            column = lambda i, m: (
                0,
                m[GROUP] ^ ((i // first) * 2 * first + side * first + i % first),
            )
            ins = [(a, (a.shape[0], part), column) for a in left] + [(a,) for a in right]
            if got is not None:
                ins.append((got, block, place))
                outs = [((half // 2,) + self.shape, BF, block, pair_place)] * 2
            else:
                outs = [((half,) + self.shape, BF, block, place)]
            aliases = {}
            if before is not None:
                aliases = {len(ins) + 1 + n: n for n in range(len(outs))}
                ins += [(a, None) for a in before]
            before = call(
                functools.partial(
                    weight_body,
                    lefts=len(left),
                    rights=len(right),
                    before=before is not None,
                    has_got=got is not None,
                    split=split,
                ),
                self.meta,
                (half,),
                ins,
                outs,
                aliases=aliases,
                cost=self.cost,
            )
        return before

    def start(self):
        if not self.plain:
            self.got = swap(self.run(1, None)[0], "dp", self.pending.pop(0))

    def step(self):
        if self.plain:
            return
        if len(self.pending) == len(self.order) - 1:
            self.keep, send = self.run(0, self.got)
        else:
            self.keep, send = split_sum(self.meta, self.keep, self.got)
        self.got = swap(send, "dp", self.pending.pop(0))

    def finish(self):
        if not self.plain:
            while self.pending:
                self.step()
            self.total = plus(self.meta, self.keep[0], self.got[0], F32)

    def end(self):
        me = lax.axis_index("dp")
        results = []
        if self.plain:
            for left, right, split, at in self.members:
                whole = dot(jnp.concatenate(left), jnp.concatenate(right), OVER_ROWS).astype(BF)
                whole = whole.reshape(self.size, -1, whole.shape[1])
                whole = pick(whole, [me ^ k for k in range(self.size)])
                results.append(scatter_dp(whole, bits_of(self.size), F32))
            return results
        for left, right, split, at in self.members:
            part = left[0].shape[1] // self.size
            inner = right[0].shape[1]
            high, wide = (2 * part, inner // 2) if split else (part, inner)
            cut = (slice(at[0] * high, (at[0] + 1) * high), slice(at[1] * wide, (at[1] + 1) * wide))
            value = self.total[cut]
            if split:
                value = jnp.concatenate([value[:part], value[part:]], axis=1)
            results.append(value)
        return results


def shards(
    text_embed,
    clip_feats,
    type_table,
    gain_attn_in,
    qkv_weight,
    gain_attn_out,
    out_weight,
    gain_ffn_in,
    up_weight,
    gain_ffn_out,
    down_weight,
    res_query,
    res_key,
    res_value,
    res_out,
    cotangent,
    owner_count,
    image_seq,
    slot_block,
    seq_kind,
):
    mp = lax.axis_size("mp")
    dp = lax.axis_size("dp")
    rows, width = text_embed.shape
    length = rows * mp
    latent = res_query.shape[0]
    slots = slot_block.shape[1]
    images, patches, clip_width = clip_feats.shape
    wide = qkv_weight.shape[2]
    heads = wide // HEAD
    ff = up_weight.shape[1]
    ff_all = ff * mp
    here = rows // latent
    part = latent // mp
    tile = 512

    Order.mark, Order.channel = None, 0
    meta = make_meta(owner_count, image_seq, slot_block, seq_kind, images)
    table = type_table.astype(F32)
    gain_in, gain_out = gain_attn_in[None], gain_attn_out[None]
    gain_ffn, gain_ff = gain_ffn_in[None], gain_ffn_out[None]
    row_block = lambda i, m: (i, 0)
    few = (latent, width)
    weight = jnp.moveaxis(qkv_weight, 1, 0)
    turn = turn_tables(length)

    text_in = call(
        text_body,
        meta,
        (4,),
        [(text_embed, (rows // 4, width), row_block), (table,), (gain_in,)],
        [((rows, width), BF, (rows // 4, width), row_block)],
    )[0]
    text_pieces = gather_rel(text_in)


    clip = clip_feats.reshape(images * patches, clip_width)
    key_proj, value_proj, pool_out = call(
        functools.partial(pool_body, images=images),
        meta,
        (1,),
        [(clip,), (res_key,), (res_value,), (res_query,)],
        [
            ((images * patches, wide), BF, None, None),
            ((images * patches, wide), BF, None, None),
            ((images * latent, wide), BF, None, None),
        ],
    )
    gathering = GatherDp(meta, pool_out)
    cot = call(
        copy_body,
        meta,
        (2,),
        [(cotangent, (rows // 2, width), row_block)],
        [((rows, width), BF, (rows // 2, width), row_block)],
    )[0]
    cot_pieces = gather_rel(cot)

    state = project(meta, text_pieces[:2], weight, turn, None, 0)
    gathering.step()
    state = project(meta, text_pieces[2:], weight, turn, state, 2)
    gathering.step()

    def d_up_half(which):
        return call(
            functools.partial(times_rows_body, count=2),
            meta,
            (ff // tile,),
            [(cot_pieces[which + n],) for n in range(2)]
            + [(down_weight, (tile, width), row_block)],
            [((rows, ff), BF, (rows, tile), lambda i, m: (0, i))] * 2,
        )

    d_up_near = d_up_half(0)
    pool_rows = gathering.end().reshape(dp * images * latent, wide)
    slot_terms = call(
        functools.partial(pooled_body, slots=slots, mp=mp),
        meta,
        (1,),
        [
            (pool_rows, (latent, wide), lambda i, m, s=s: (m[SOURCE + s], 0))
            for s in range(slots)
        ]
        + [(res_out,)],
        [((mp // 2, slots, part, width), BF, None, None)] * 2,
        scratch=[pltpu.VMEM((slots * latent, width), F32)],
    )
    slot_own, slot_far = scatter_now(meta, *slot_terms)
    slot_pieces = gather_now(meta, add_low(slot_own, slot_far))

    at_slot = lambda i, m: (m[POS + jnp.maximum(i - 3, 0)], 0)
    state = call(
        functools.partial(slot_body, mp=mp, slots=slots, latent=latent),
        meta,
        (3 + slots,),
        [(p,) for p in slot_pieces]
        + [(table,), (gain_in,)]
        + [(weight, (1, width, wide), lambda i, m: (jnp.minimum(i, 2), 0, 0))]
        + [(turn, (3, 2, latent, LANES), lambda i, m: (0, 0) + at_slot(i, m))]
        + [(a, (latent, a.shape[1]), at_slot) for a in state],
        [(a.shape, BF, (latent, a.shape[1]), at_slot) for a in state]
        + [((slots, latent, width), BF, None, None)],
        scratch=[
            pltpu.VMEM((slots, latent, width), F32),
            pltpu.VMEM((3, slots, latent, wide), F32),
            pltpu.VMEM((slots, latent, width), BF),
        ],
        aliases={mp + 5 + n: n for n in range(2)},
    )
    qkv, in_full, slot_rows = state

    att, lse, att_stats = call(
        functools.partial(attend_body, block=rows),
        meta,
        (1,),
        [(qkv,)],
        [
            ((length, wide), BF, None, None),
            ((heads, length), F32, None, None),
            ((8, length), F32, None, None),
        ],
        scratch=[pltpu.VMEM((length, LANES), F32)] * 3,
    )
    att_stats = spread_stats(meta, att_stats)

    mids = call(
        functools.partial(mid_body, mp=mp, width=width),
        meta,
        (mp,),
        [(att, (rows, wide), lambda j, m: (m[PART] ^ j, 0)), (gain_out,)]
        + [(s, (8, rows), lambda j, m: (0, m[PART] ^ j)) for s in att_stats],
        [((length, wide), BF, (rows, wide), lambda j, m: (j, 0))],
    )[0]
    steps = width // tile

    def summed(body, array, weights, which):
        return call(
            body,
            meta,
            (steps,),
            [(array, (2 * rows, array.shape[1]), lambda i, m: (which // 2, 0)), weights],
            [((rows, width), BF, None, None)],
            scratch=pair_scratch(1, steps, rows, tile),
            remote=True,
        )[0]

    out_w = (out_weight, (wide, tile), lambda i, m: (0, i))
    out_far = swap(summed(out_body, mids, out_w, 2), "mp", 2)
    out_terms = [summed(out_body, mids, out_w, 0), out_far]
    d_up = d_up_near + d_up_half(2)
    after_attn, ffn_in = call(
        after_body,
        meta,
        (here,),
        [(t, few, row_block) for t in out_terms]
        + [(text_embed, few, row_block), (slot_rows, (1,) + few, slot_index(here))]
        + [(table,), (gain_ffn,)],
        [((rows, width), F32, few, row_block), ((rows, width), BF, few, row_block)],
    )
    ffn_pieces = gather_rel(ffn_in)

    def up_half(which, before):
        lanes_of = lambda i, m: (0, i)
        half = lambda i, m: (which // 2, i)
        ins = [(ffn_pieces[which],), (ffn_pieces[which + 1],)]
        ins += [(up_weight, (width, tile), lanes_of)]
        ins += [(d_up[which + n], (rows, tile), lanes_of) for n in range(2)]
        ins += [(gain_ff, (1, tile), lanes_of)]
        aliases = {}
        if before is not None:
            aliases = {len(ins) + 1 + n: n for n in range(3)}
            ins += [(a, None) for a in before]
        return call(
            up_body,
            meta,
            (ff // tile,),
            ins,
            [
                ((length, ff), BF, (2 * rows, tile), half),
                ((length, ff), BF, (2 * rows, tile), half),
                ((8, length), F32, (8, 2 * rows), lambda i, m: (0, which // 2)),
            ],
            scratch=[pltpu.VMEM((2 * rows, LANES), F32)] * 4,
            aliases=aliases,
        )

    state = up_half(0, None)
    act, slope, ff_stats = up_half(2, state)
    ff_stats = spread_stats(meta, ff_stats)
    cut = rows // 2
    fine = lambda i, m: (i, 0)
    pre, low, gain_ff_local = call(
        functools.partial(spread_body, mp=mp, width=ff_all),
        meta,
        (length // cut,),
        [(act, (cut, ff), fine), (slope, (cut, ff), fine)]
        + [
            (d_up[j], (cut, ff), lambda i, m, j=j: (jnp.clip(i - 2 * j, 0, 1), 0))
            for j in range(mp)
        ]
        + [(gain_ff,)]
        + [
            (s, (8, cut), lambda i, m, b=b: (0, (((i // 2) ^ b) * 2) + i % 2))
            for b, s in enumerate(ff_stats)
        ],
        [((length, ff), BF, (cut, ff), fine)] * 2 + [((1, ff), F32, None, None)],
    )

    up_w = (up_weight, (tile, ff), row_block)
    down_grad = WeightGrads(meta, [(cot_pieces, [low], False, (0, 0))], (width // dp, ff))
    up_grad = WeightGrads(meta, [(ffn_pieces, [pre], False, (0, 0))], (width // dp, ff), 2)
    down_grad.start()
    back_far = swap(summed(back_body, pre, up_w, 2), "mp", 2)
    ffn_terms = [summed(back_body, pre, up_w, 0), back_far]
    d_after, d_after_low, gain_ffn_local = call(
        ffn_back_body,
        meta,
        (here,),
        [(t, few, row_block) for t in ffn_terms]
        + [(after_attn, few, row_block), (cotangent, few, row_block), (gain_ffn,)],
        [
            ((rows, width), F32, few, row_block),
            ((rows, width), BF, few, row_block),
            ((1, width), F32, None, None),
        ],
    )
    after_pieces = gather_rel(d_after_low)
    up_grad.start()

    down_near, down_far = call(
        down_body,
        meta,
        (steps,),
        [(low,), (down_weight, (ff, tile), lambda i, m: (0, i))],
        [((rows, width), BF, None, None)] * 2,
        scratch=pair_scratch(2, steps, rows, tile),
        remote=True,
    )
    down_far = swap(down_far, "mp", 2)
    def d_mid_half(which, before):
        block = lambda i, m: (m[PART] ^ (which + i), 0)
        lane_block = lambda i, m: (0, m[PART] ^ (which + i))
        aliases = {}
        ins = [(after_pieces[which],), (after_pieces[which + 1],), (out_weight,), (gain_out,)]
        ins += [(att, (rows, wide), block)] + [(s, (8, rows), lane_block) for s in att_stats]
        if before is not None:
            aliases = {len(ins) + 1 + n: n for n in range(2)}
            ins += [(a, None) for a in before]
        return call(
            functools.partial(d_mid_body, mp=mp, width=width),
            meta,
            (2,),
            ins,
            [
                ((length, wide), BF, (rows, wide), block),
                ((8, length), F32, (8, rows), lane_block),
                ((1, wide), F32, None, None),
            ],
            aliases=aliases,
        )

    d_mid, mid_stats, gain_mid_near = d_mid_half(0, None)
    d_mid, mid_stats, gain_mid_far = d_mid_half(2, (d_mid, mid_stats))
    mid_stats = spread_stats(meta, mid_stats)
    out_grad = WeightGrads(meta, [(after_pieces, [mids], False, (0, 0))], (width // dp, wide))
    out_grad.start()
    layer_out = call(
        sum_body,
        meta,
        (here,),
        [(after_attn, few, row_block), (down_near, few, row_block), (down_far, few, row_block)],
        [((rows, width), F32, few, row_block)],
    )[0]
    down_grad.step()
    d_qkv = call(
        functools.partial(attend_back_body, mp=mp, width=width, block=rows),
        meta,
        (1,),
        [(a,) for a in (qkv, att, d_mid, lse, gain_out, turn)]
        + [(s,) for s in att_stats]
        + [(s,) for s in mid_stats],
        [((length, 3 * wide), BF, None, None)],
        scratch=[pltpu.VMEM((length, wide), BF)] + [pltpu.VMEM((length, LANES), F32)] * 3,
    )[0]

    slot_terms = call(
        functools.partial(slot_back_body, slots=slots, mp=mp),
        meta,
        (1,),
        [
            (d_qkv, (latent, 3 * wide), lambda i, m, s=s: (m[POS + s], 0))
            for s in range(slots)
        ]
        + [(weight,)],
        [((mp // 2, slots, part, width), BF, None, None)] * 2,
        scratch=[pltpu.VMEM((slots * latent, width), F32)],
    )
    slot_terms = scatter_now(meta, *slot_terms)
    image_keep, image_send, _ = call(
        functools.partial(
            slot_grad_body, mp=mp, slots=slots, latent=latent, images=images, groups=dp
        ),
        meta,
        (1,),
        [(t,) for t in slot_terms]
        + [(slot_rows,), (table,), (gain_in,)]
        + [(a,) for a in after_pieces],
        [((dp // 2, images * part, width), BF, None, None)] * 2
        + [((slots, part, width), BF, None, None)],
    )
    image_got = exchange(meta, (image_send, "dp", 1))[0]
    in_grad = WeightGrads(meta, [([in_full], [d_qkv], False, (0, 0))], (width // dp, 3 * wide))
    def row_terms(which):
        return call(
            functools.partial(row_back_body, which=which),
            meta,
            (steps,),
            [(d_qkv,), (weight, (3, tile, wide), lambda i, m: (0, i, 0))],
            [((rows, width), BF, None, None)],
            scratch=pair_scratch(1, steps, rows, tile),
            remote=True,
        )[0]

    for bit in bits_of(dp)[1:]:
        image_keep, image_send = split_sum(meta, image_keep, image_got)
        image_got = exchange(meta, (image_send, "dp", bit))[0]
        if bit == 2:
            up_grad.step()
            in_grad.start()
            in_far = swap(row_terms(2), "mp", 2)
            down_grad.step()
            out_grad.step()
    owned = plus(meta, image_keep, image_got, BF).reshape(images, part, width)
    owned_pieces = gather_now(meta, owned)
    d_kv, query_local, clip_even, clip_odd, pool_grad = call(
        functools.partial(pool_back_body, images=images, mp=mp),
        meta,
        (1,),
        [(a,) for a in owned_pieces]
        + [(a,) for a in (res_out, key_proj, value_proj, res_query, res_key, res_value)],
        [
            ((images * patches, 2 * wide), BF, None, None),
            ((latent, wide), F32, None, None),
            ((mp // 2, images, patches // mp, clip_width), BF, None, None),
            ((mp // 2, images, patches // mp, clip_width), BF, None, None),
            ((images * latent, width), BF, None, None),
        ],
        scratch=[pltpu.VMEM((images * patches, clip_width), F32)],
    )
    pool_grads = WeightGrads(
        meta, [([clip], [d_kv], False, (0, 0))], (clip_width // dp, 2 * wide)
    )
    pool_grads.start()
    up_grad.step()
    in_terms = [row_terms(0), in_far]
    text_grad, gain_in_local, type_local = call(
        in_back_body,
        meta,
        (here,),
        [(t, few, row_block) for t in in_terms]
        + [(d_after, few, row_block), (text_embed, few, row_block)]
        + [(slot_rows, (1,) + few, slot_index(here)), (table,), (gain_in,)],
        [
            ((rows, width), F32, few, row_block),
            ((1, width), F32, None, None),
            ((1, width), F32, None, None),
        ],
    )
    kind = (jnp.arange(3) == meta[KIND]).astype(F32)[:, None]
    over_all = jnp.concatenate([kind * type_local, gain_in_local, gain_ffn_local])
    flat = jnp.concatenate(
        [
            over_all.reshape(-1),
            (gain_mid_near + gain_mid_far)[0],
            gain_ff_local[0],
            query_local.reshape(-1),
        ]
    ).reshape(-1, LANES)
    group = lax.axis_index("dp")
    columns = pool_grad.reshape(images * latent, dp, width // dp).swapaxes(0, 1)
    columns = pick(columns, [group ^ k for k in range(dp)])
    hops = bits_of(dp)[1:] + [1]
    for bit in hops:
        cut = columns.reshape((-1, 2, bit) + columns.shape[1:])
        stay, send = halve(cut, 1)
        got, flat_got = exchange(meta, (send, "dp", bit), (flat, "dp", bit))
        flat = plus(meta, flat, flat_got, F32)
        columns = jnp.stack([stay, got], axis=1).reshape(columns.shape)
        if bit == hops[-2]:
            in_grad.step()
            out_grad.step()
            pool_grads.step()
    clip_even = add_low(clip_even, exchange(meta, (clip_odd, "mp", 1))[0])
    clip_far, flat_far, flat_near = exchange(
        meta, (clip_even[1], "mp", 2), (flat, "mp", 2), (flat, "mp", 1)
    )
    flat_last = exchange(meta, (flat_far, "mp", 1))[0]
    res_out_grad = call(
        gathered_body,
        meta,
        (1,),
        [(pool_rows,), (columns.reshape(dp * images * latent, width // dp),)],
        [((wide, width // dp), F32, None, None)],
    )[0]
    in_grad.step()
    pool_grads.step()
    down_grad.finish()
    up_grad.finish()
    out_grad.finish()
    pool_grads.finish()
    in_grad.finish()
    clip_grad = clip_even[0].astype(F32) + clip_far.astype(F32)
    flat = by_mp(jnp.stack([flat, flat_near, flat_far, flat_last])).reshape(mp, -1)
    sums = jnp.sum(flat[:, : 5 * width].reshape(mp, 5, width), axis=0)
    parts = flat[:, 5 * width :]
    query_grad = jnp.swapaxes(parts[:, wide + ff :].reshape(mp, latent, wide), 0, 1)
    kv_grad = pool_grads.end()[0]
    qkv_grad, out_grad = in_grad.end()[0], out_grad.end()[0]
    return (
        layer_out,
        text_grad,
        clip_grad,
        sums[:3],
        sums[3],
        qkv_grad.reshape(-1, 3, wide),
        parts[:, :wide].reshape(-1),
        out_grad.T,
        sums[4],
        up_grad.end()[0],
        parts[:, wide : wide + ff].reshape(-1),
        down_grad.end()[0].T,
        query_grad.reshape(latent, width),
        kv_grad[:, :wide],
        kv_grad[:, wide:],
        res_out_grad,
    )


def solution(mesh):
    return jax.shard_map(
        shards,
        mesh=mesh,
        in_specs=(
            P(("dp", "mp"), None),
            P("dp", None, None),
            P(),
            P(),
            P(None, None, "mp"),
            P("mp"),
            P("mp", None),
            P(),
            P(None, "mp"),
            P("mp"),
            P("mp", None),
            P(None, "mp"),
            P(None, "mp"),
            P(None, "mp"),
            P("mp", None),
            P(("dp", "mp"), None),
            P(),
            P(),
            P(),
            P(),
        ),
        out_specs=(
            P(("dp", "mp"), None),
            P(("dp", "mp"), None),
            P("dp", "mp", None),
            P(),
            P(),
            P("dp", None, "mp"),
            P(),
            P("mp", "dp"),
            P(),
            P("dp", "mp"),
            P(),
            P("mp", "dp"),
            P(),
            P("dp", "mp"),
            P("dp", "mp"),
            P("mp", "dp"),
        ),
        check_vma=False,
    )
```

```python
import functools

import jax
import jax.numpy as jnp
from jax import lax
from jax.experimental import pallas as pl
from jax.experimental.pallas import tpu as pltpu
from jax.sharding import PartitionSpec as P

HEAD = 64
LANES = 128
EPS = 1e-05
NEG = -1e30
XPOS_BASE = 512.0
BF = jnp.bfloat16
F32 = jnp.float32
ROWS_BY_ROWS = (((1,), (1,)), ((), ()))
PLAIN = (((1,), (0,)), ((), ()))
OVER_ROWS = (((0,), (0,)), ((), ()))
KIND, PART, GROUP, REAL, POS, SOURCE, BLOCK, RANK = 0, 1, 2, 4, 8, 12, 16, 32
VMEM_BYTES = 14 * 1024 * 1024


def dot(left, right, form=PLAIN):
    return lax.dot_general(left, right, form, preferred_element_type=F32)


def dot_exact(left, right, form=ROWS_BY_ROWS):
    return lax.dot_general(
        left, right, form, precision=lax.Precision.HIGHEST, preferred_element_type=F32
    )


def swap(values, axis, bit):
    size = lax.axis_size(axis)
    return lax.ppermute(values, axis, [(i, i ^ bit) for i in range(size)])


def bits_of(size):
    return [1 << i for i in range(size.bit_length() - 1)]


def gather_start(values):
    far, near = swap(values, "mp", 2), swap(values, "mp", 1)
    return [values, near, far]


def gather_end(meta, pieces):
    pieces.append(exchange(meta, (pieces[2], "mp", 1))[0])


def add_low(first, second):
    return (first.astype(F32) + second.astype(F32)).astype(BF)


def scatter_pairs(even, odd):
    near = add_low(even, swap(odd, "mp", 1))
    return near[0], swap(near[1], "mp", 2), near


def sum_pairs(even, odd):
    own, far, _ = scatter_pairs(even, odd)
    return own.astype(F32) + far.astype(F32)


def pick(values, indices):
    return jnp.stack([lax.dynamic_index_in_dim(values, i, 0, keepdims=False) for i in indices])


def by_mp(values):
    me = lax.axis_index("mp")
    return pick(values, [me ^ j for j in range(lax.axis_size("mp"))])


def halve(values, axis):
    return (
        lax.index_in_dim(values, 0, axis, keepdims=False),
        lax.index_in_dim(values, 1, axis, keepdims=False),
    )


def scatter_dp(values, bits, last):
    for bit in bits:
        values = values.reshape((-1, 2) + values.shape[1:])
        keep, send = halve(values, 1)
        got = swap(send, "dp", bit)
        total = keep.astype(F32) + got.astype(F32)
        values = total.astype(last if bit == bits[-1] else BF)
    return values[0]


class Order:
    mark = None
    channel = 0


def call(body, meta, grid, ins, outs, scratch=(), aliases=None, remote=False, after=(), cost=1, room=VMEM_BYTES):
    arrays, specs = [], []
    for item in ins:
        arrays.append(item[0])
        if len(item) == 1:
            dims = item[0].ndim
            specs.append(
                pl.BlockSpec(
                    item[0].shape,
                    lambda *_, dims=dims: (0,) * dims,
                    pipeline_mode=pl.Buffered(1),
                )
            )
        elif item[1] is None:
            specs.append(pl.BlockSpec(memory_space=pl.ANY))
        else:
            specs.append(pl.BlockSpec(item[1], item[2]))
    shapes, out_specs = [], []
    for shape, dtype, block, index in list(outs) + [((8, LANES), F32, None, None)]:
        shapes.append(jax.ShapeDtypeStruct(shape, dtype))
        if index == "any":
            out_specs.append(pl.BlockSpec(memory_space=pl.ANY))
        elif block is None:
            dims = len(shape)
            out_specs.append(pl.BlockSpec(shape, lambda *_, dims=dims: (0,) * dims))
        else:
            out_specs.append(pl.BlockSpec(block, index))
    count, after = len(ins), list(after)
    if Order.mark is not None:
        after.append(Order.mark)
    specs += [pl.BlockSpec(memory_space=pl.ANY)] * len(after)

    params = pltpu.CompilerParams(vmem_limit_bytes=room)
    if remote:
        Order.channel += 1
        params = pltpu.CompilerParams(
            vmem_limit_bytes=room, collective_id=Order.channel, has_side_effects=True
        )

    def marked(meta_ref, *refs):
        refs = refs[:count] + refs[count + len(after) :]
        place = count + len(outs)
        refs[place][...] = jnp.zeros((8, LANES), F32)
        body(meta_ref, *refs[:place], *refs[place + 1 :])

    result = pl.pallas_call(
        marked,
        out_shape=shapes,
        grid_spec=pltpu.PrefetchScalarGridSpec(
            num_scalar_prefetch=1,
            grid=grid,
            in_specs=specs,
            out_specs=out_specs,
            scratch_shapes=list(scratch),
        ),
        input_output_aliases=aliases or {},
        compiler_params=params,
        cost_estimate=pl.CostEstimate(
            flops=cost * 1000000, bytes_accessed=1024, transcendentals=0
        ),
        name=getattr(body, "func", body).__name__,
    )(meta, *arrays, *after)
    Order.mark = result[-1]
    return result[:-1]


def norm_parts(values):
    width = values.shape[-1]
    mean = jnp.sum(values, axis=-1, keepdims=True) / width
    square = jnp.sum(values * values, axis=-1, keepdims=True) / width
    inv_std = lax.rsqrt(square - mean * mean + EPS)
    return (values - mean) * inv_std, inv_std


def norm_back(upstream, normed, inv_std, gain):
    width = upstream.shape[-1]
    scaled = upstream * gain
    first = jnp.sum(scaled, axis=-1, keepdims=True) / width
    second = jnp.sum(scaled * normed, axis=-1, keepdims=True) / width
    return inv_std * (scaled - first - normed * second)


def columns_of(rows):
    count, length = rows.shape
    full = jnp.concatenate([rows, jnp.zeros((LANES - count, length), F32)], axis=0)
    return full.T


def lane_sums(values):
    total = values[:, :LANES]
    for start in range(LANES, values.shape[1], LANES):
        total = total + values[:, start : start + LANES]
    return total


def rows_from(partials):
    return dot_exact(jnp.ones((8, LANES), F32), partials)


def two_rows(first, second):
    row = lax.broadcasted_iota(jnp.int32, first.shape, 0)
    return jnp.where(row == 0, first, jnp.where(row == 1, second, 0.0))


def meta_body(count_ref, seq_ref, slot_ref, kind_ref, me_ref, out_ref, *, image_local, slots, images):
    me_m, me_d = me_ref[0], me_ref[1]

    def clear(i, _):
        out_ref[i] = 0
        return 0

    lax.fori_loop(0, BLOCK, clear, 0)

    def absent(i, _):
        out_ref[BLOCK + i] = -1
        return 0

    lax.fori_loop(0, RANK - BLOCK + images, absent, 0)
    out_ref[KIND] = kind_ref[me_d]
    out_ref[PART] = me_m
    out_ref[GROUP] = me_d
    for s in range(slots):
        out_ref[POS + s] = slot_ref[me_d, s]

    def one(i, found):
        owner = i // image_local
        inside = i - owner * image_local
        here = jnp.logical_and(inside < count_ref[owner], seq_ref[i] == me_d)
        rank = jnp.minimum(found, slots - 1)

        @pl.when(here)
        def _():
            out_ref[REAL + rank] = 1
            out_ref[SOURCE + rank] = (owner ^ me_d) * image_local + inside
            out_ref[BLOCK + slot_ref[me_d, rank]] = rank
            out_ref[RANK + i] = rank

        return found + here.astype(jnp.int32)

    lax.fori_loop(0, images, one, jnp.int32(0))


def make_meta(owner_count, image_seq, slot_block, seq_kind, image_local):
    me = jnp.stack([lax.axis_index("mp"), lax.axis_index("dp")]).astype(jnp.int32)
    images = image_seq.shape[0]
    smem = pl.BlockSpec(memory_space=pltpu.SMEM)
    return pl.pallas_call(
        functools.partial(
            meta_body, image_local=image_local, slots=slot_block.shape[1], images=images
        ),
        out_shape=jax.ShapeDtypeStruct((RANK + images,), jnp.int32),
        in_specs=[smem] * 5,
        out_specs=smem,
    )(owner_count, image_seq, slot_block, seq_kind, me)


def other_of(me, j):
    return [me, me + 1 - 2 * (me % 2), (me + 2) % 4, 3 - me][j]


def pair_sums(terms, out_refs, scratch):
    sent, came, kept, send_sem, recv_sem = scratch
    step, steps = pl.program_id(0), pl.num_programs(0)
    partner = {"mp": other_of(lax.axis_index("mp"), 1)}

    @pl.when(step == 0)
    def _():
        barrier = pltpu.get_barrier_semaphore()
        pl.semaphore_signal(barrier, inc=1, device_id=partner)
        pl.semaphore_wait(barrier, 1)

    def move(n, place):
        return pltpu.make_async_remote_copy(
            src_ref=sent.at[n, place],
            dst_ref=came.at[n, place],
            send_sem=send_sem.at[n, place],
            recv_sem=recv_sem.at[n, place],
            device_id=partner,
        )

    for n, (mine, theirs) in enumerate(terms):
        sent[n, step] = theirs().astype(BF)
        move(n, step).start()
        kept[n, step] = mine()

    @pl.when(step == steps - 1)
    def _():
        tile = sent.shape[-1]
        for n, out_ref in enumerate(out_refs):
            for place in range(sent.shape[1]):
                move(n, place).wait()
                total = kept[n, place] + came[n, place].astype(F32)
                out_ref[:, place * tile : (place + 1) * tile] = total.astype(BF)


def flipped(me, bit):
    return me + bit * (1 - 2 * ((me // bit) % 2))


def exchange(meta, *items):
    places = sorted({(axis, bit) for _, axis, bit in items})
    count = len(items)

    def body(meta_ref, *refs):
        sources, targets, (send_sem, recv_sem) = refs[:count], refs[count : 2 * count], refs[-2:]

        def partner(axis, bit):
            me = lax.axis_index(axis)
            for one in bits_of(lax.axis_size(axis)):
                if bit & one:
                    me = flipped(me, one)
            return {axis: me}

        barrier = pltpu.get_barrier_semaphore()
        for axis, bit in places:
            pl.semaphore_signal(barrier, inc=1, device_id=partner(axis, bit))
        pl.semaphore_wait(barrier, len(places))
        copies = [
            pltpu.make_async_remote_copy(
                src_ref=sources[n],
                dst_ref=targets[n],
                send_sem=send_sem.at[n],
                recv_sem=recv_sem.at[n],
                device_id=partner(axis, bit),
            )
            for n, (_, axis, bit) in enumerate(items)
        ]
        for copy in copies:
            copy.start()
        for copy in copies:
            copy.wait()

    return call(
        body,
        meta,
        (1,),
        [(array, None) for array, _, _ in items],
        [(array.shape, array.dtype, None, "any") for array, _, _ in items],
        scratch=[pltpu.SemaphoreType.DMA((count,)), pltpu.SemaphoreType.DMA((count,))],
        remote=True,
    )


def spread_stats(meta, values):
    others = range(1, lax.axis_size("mp"))
    return [values] + list(exchange(meta, *[(values, "mp", b) for b in others]))


def gather_now(meta, values):
    far, near = exchange(meta, (values, "mp", 2), (values, "mp", 1))
    return [values, near, far, exchange(meta, (far, "mp", 1))[0]]


def scatter_now(meta, even, odd):
    near = add_low(even, exchange(meta, (odd, "mp", 1))[0])
    return near[0], exchange(meta, (near[1], "mp", 2))[0]


def pair_scratch(count, steps, rows, tile):
    shape = (count, steps, rows, tile)
    return [
        pltpu.VMEM(shape, BF),
        pltpu.VMEM(shape, BF),
        pltpu.VMEM(shape, F32),
        pltpu.SemaphoreType.DMA((count, steps)),
        pltpu.SemaphoreType.DMA((count, steps)),
    ]


def kind_of(meta, table_ref):
    return table_ref[pl.ds(meta[KIND], 1), :]


def text_body(meta, text_ref, table_ref, gain_ref, out_ref):
    mixed = text_ref[...].astype(F32) + kind_of(meta, table_ref)
    out_ref[...] = (norm_parts(mixed)[0] * gain_ref[...]).astype(BF)


def rotated(values, cosine, sine):
    width = values.shape[1]
    lane = lax.broadcasted_iota(jnp.int32, values.shape, 1)
    other = jnp.where(
        lane % HEAD < HEAD // 2,
        pltpu.roll(values, width - HEAD // 2, 1),
        pltpu.roll(values, HEAD // 2, 1),
    )
    repeat = width // LANES
    cosine = jnp.concatenate([cosine] * repeat, axis=1)
    sine = jnp.concatenate([sine] * repeat, axis=1)
    return values * cosine + other * sine


def qkv_body(meta, near_ref, far_ref, weight_ref, turn_ref, *refs, which):
    out_ref, in_ref = refs[-2:]
    rows = near_ref.shape[0]
    for n, ref in enumerate((near_ref, far_ref)):
        at = pl.ds(pl.multiple_of(((meta[PART] ^ (which + n)) % 2) * rows, rows), rows)
        product = dot(ref[...], weight_ref[0])
        out_ref[at, :] = rotated(product, turn_ref[0, 0, at, :], turn_ref[0, 1, at, :]).astype(BF)
        in_ref[at, :] = ref[...]


def project(meta, pieces, weight, turn, before, which, after=()):
    rows, depth = pieces[0].shape
    width = weight.shape[2]
    length = rows * lax.axis_size("mp")
    pair = lambda m: (m[PART] ^ which) // 2
    ins = [(pieces[0],), (pieces[1],), (weight, (1, depth, width), lambda i, m: (i, 0, 0))]
    ins.append((turn, (1, 2, 2 * rows, LANES), lambda i, m: (i, 0, pair(m), 0)))
    aliases = {}
    if before is not None:
        for n, array in enumerate(before):
            ins.append((array, None))
            aliases[5 + n] = n
    return call(
        functools.partial(qkv_body, which=which),
        meta,
        (3,),
        ins,
        [
            ((length, 3 * width), BF, (2 * rows, width), lambda i, m: (pair(m), i)),
            ((length, depth), BF, (2 * rows, depth), lambda i, m: (pair(m), 0)),
        ],
        aliases=aliases,
        after=after,
    )


def slot_body(meta, *refs, mp, slots, latent):
    pieces = refs[:mp]
    table_ref, gain_ref, weight_ref, turn_ref, qkv_in, x_in = refs[mp : mp + 6]
    qkv_ref, x_ref, slots_ref, rows_ref, new_ref, norm_ref = refs[mp + 6 :]
    step = pl.program_id(0)
    part = latent // mp

    @pl.when(step == 0)
    def _():
        for j in range(mp):
            place = pl.multiple_of((meta[PART] ^ j) * part, part)
            for s in range(slots):
                rows_ref[s, pl.ds(place, part), :] = pieces[j][s].astype(F32)
        mixed = rows_ref[...].reshape(slots * latent, -1)
        slots_ref[...] = mixed.astype(BF).reshape(slots_ref.shape)
        mixed = mixed + kind_of(meta, table_ref)
        normed = (norm_parts(mixed)[0] * gain_ref[...]).astype(BF)
        norm_ref[...] = normed.reshape(norm_ref.shape)

    @pl.when(step < 3)
    def _():
        product = dot(norm_ref[...].reshape(slots * latent, -1), weight_ref[0])
        new_ref[step] = product.reshape(new_ref.shape[1:])

    @pl.when(step >= 3)
    def _():
        slot = step - 3
        real = meta[REAL + slot] > 0
        width = new_ref.shape[-1]
        for c in range(3):
            at = slice(c * width, (c + 1) * width)
            value = rotated(new_ref[c, slot], turn_ref[c, 0], turn_ref[c, 1]).astype(BF)
            qkv_ref[:, at] = jnp.where(real, value, qkv_in[:, at])
        x_ref[...] = jnp.where(real, norm_ref[slot], x_in[...])


def turn_tables(length):
    positions = jnp.arange(length, dtype=F32)[:, None]
    lane = jnp.arange(LANES)
    ladder = (lane % (HEAD // 2)).astype(F32)
    angle = positions * jnp.power(10000.0, -2.0 * ladder / HEAD)[None, :]
    decay = (2.0 * ladder + 0.4 * HEAD) / (1.4 * HEAD)
    power = (positions - length // 2) / XPOS_BASE
    sign = jnp.where(lane % HEAD < HEAD // 2, -1.0, 1.0)[None, :]
    cosine, sine = jnp.cos(angle), jnp.sin(angle) * sign
    up = jnp.power(decay[None, :], power)
    down = jnp.power(decay[None, :], -power)
    one, zero = jnp.ones_like(cosine), jnp.zeros_like(cosine)
    return jnp.stack(
        [
            jnp.stack([cosine * up, sine * up]),
            jnp.stack([cosine * down, sine * down]),
            jnp.stack([one, zero]),
        ]
    )


def pool_shares_of(query, keys, head):
    lane = lax.broadcasted_iota(jnp.int32, query.shape, 1)
    masked = jnp.where(lane // HEAD == head, query, jnp.zeros_like(query))
    scores = dot(masked, keys, ROWS_BY_ROWS) * 0.125
    top = jnp.max(scores, axis=-1, keepdims=True)
    weights = jnp.exp(scores - top)
    return weights / jnp.sum(weights, axis=-1, keepdims=True)


def pool_body(
    meta, clip_ref, key_w, value_w, query_ref, key_ref, value_ref, pool_ref, *, images
):
    clip = clip_ref[...]
    key_ref[...] = dot(clip, key_w[...]).astype(BF)
    value_ref[...] = dot(clip, value_w[...]).astype(BF)
    patches = clip.shape[0] // images
    latent = query_ref.shape[0]
    for i in range(images):
        for pair in range(query_ref.shape[1] // LANES):
            lanes = slice(pair * LANES, (pair + 1) * LANES)
            rows = slice(i * patches, (i + 1) * patches)
            query, keys, values = query_ref[:, lanes], key_ref[rows, lanes], value_ref[rows, lanes]
            lane = lax.broadcasted_iota(jnp.int32, query.shape, 1)
            heads = [
                dot(pool_shares_of(query, keys, h).astype(BF), values) for h in range(2)
            ]
            pool_ref[i * latent : (i + 1) * latent, lanes] = jnp.where(
                lane < HEAD, heads[0], heads[1]
            ).astype(BF)


def pooled_body(meta, *refs, slots, mp):
    pieces, out_w, even_ref, odd_ref, scratch = refs[:slots], refs[slots], *refs[slots + 1 :]
    rows = jnp.concatenate([p[...] for p in pieces], axis=0)
    scratch[...] = dot(rows, out_w[...])
    latent = pieces[0].shape[0]
    part = latent // mp
    for j in range(mp):
        for s in range(slots):
            start = pl.multiple_of(s * latent + (meta[PART] ^ j) * part, part)
            (odd_ref if j % 2 else even_ref)[j // 2, s] = scratch[pl.ds(start, part), :].astype(BF)


def copy_body(meta, in_ref, out_ref):
    out_ref[...] = in_ref[...]


def head_lanes(pair, width):
    return [
        pl.ds(pl.multiple_of(c * width + pair * LANES, LANES), LANES) for c in range(3)
    ]


def attend_body(meta, qkv_ref, out_ref, lse_ref, stat_ref, first, second, lse, *, block):
    length, width = out_ref.shape
    first[...] = jnp.zeros_like(first)
    second[...] = jnp.zeros_like(second)

    def pair(hp, _):
        lanes, k_lanes, v_lanes = head_lanes(hp, width)
        keys, values = qkv_ref[:, k_lanes], qkv_ref[:, v_lanes]
        lane = lax.broadcasted_iota(jnp.int32, (block, LANES), 1)
        row = lax.broadcasted_iota(jnp.int32, (block, block), 0)
        col = lax.broadcasted_iota(jnp.int32, (block, block), 1)
        for b in range(length // block):
            rows = slice(b * block, (b + 1) * block)
            end = (b + 1) * block
            query = qkv_ref[rows, lanes]
            outs = []
            for h in range(2):
                masked = jnp.where(lane // HEAD == h, query, jnp.zeros_like(query))
                scores = dot(masked, keys[:end], ROWS_BY_ROWS) * 0.125
                edge = jnp.where(row >= col, scores[:, b * block :], NEG)
                scores = edge if b == 0 else jnp.concatenate([scores[:, : b * block], edge], axis=1)
                top = jnp.max(scores, axis=-1, keepdims=True)
                weights = jnp.exp(scores - top)
                total = jnp.sum(weights, axis=-1, keepdims=True)
                outs.append(dot(weights.astype(BF), values[:end]) / total)
                lse[rows, :] = jnp.where(lane == 2 * hp + h, top + jnp.log(total), lse[rows, :])
            out = jnp.where(lane < HEAD, outs[0], outs[1])
            first[rows, :] += out
            second[rows, :] += out * out
            out_ref[rows, lanes] = out.astype(BF)
        return 0

    lax.fori_loop(0, width // LANES, pair, 0)
    lse_ref[...] = lse[...].T[: lse_ref.shape[0]]
    stat_ref[...] = two_rows(rows_from(first[...]), rows_from(second[...]))


def total_columns(stats):
    total = stats[0][...]
    for other in stats[1:]:
        total = total + other[...]
    return columns_of(total)


def stat_norm(values, columns, at, width):
    mean = columns[:, at : at + 1] / width
    square = columns[:, at + 1 : at + 2] / width
    inv_std = lax.rsqrt(square - mean * mean + EPS)
    return (values - mean) * inv_std, inv_std


def mid_body(meta, att_ref, gain_ref, *refs, mp, width):
    normed, _ = stat_norm(att_ref[...].astype(F32), total_columns(refs[:mp]), 0, width)
    refs[mp][...] = (normed * gain_ref[...]).astype(BF)


def out_body(meta, rows_ref, weight_ref, out_ref, *scratch):
    rows = out_ref.shape[0]
    pair_sums(
        [
            (
                lambda: dot(rows_ref[:rows, :], weight_ref[...]),
                lambda: dot(rows_ref[rows:, :], weight_ref[...]),
            )
        ],
        [out_ref],
        scratch,
    )


def back_body(meta, rows_ref, weight_ref, out_ref, *scratch):
    rows = out_ref.shape[0]
    pair_sums(
        [
            (
                lambda: dot(rows_ref[:rows, :], weight_ref[...], ROWS_BY_ROWS),
                lambda: dot(rows_ref[rows:, :], weight_ref[...], ROWS_BY_ROWS),
            )
        ],
        [out_ref],
        scratch,
    )


def after_body(meta, own_ref, far_ref, text_ref, slots_ref, table_ref, gain_ref, after_ref, low_ref):
    mixed = mixed_rows(meta, text_ref, slots_ref, table_ref)
    after = mixed + (own_ref[...].astype(F32) + far_ref[...].astype(F32))
    after_ref[...] = after
    low_ref[...] = (norm_parts(after)[0] * gain_ref[...]).astype(BF)


def mixed_rows(meta, text_ref, slots_ref, table_ref):
    block = meta[PART] * pl.num_programs(0) + pl.program_id(0)
    filled = meta[BLOCK + block] >= 0
    return (
        jnp.where(filled, slots_ref[0].astype(F32), text_ref[...].astype(F32))
        + kind_of(meta, table_ref)
    )


def slot_index(blocks):
    return lambda i, m: (jnp.maximum(m[BLOCK + m[PART] * blocks + i], 0), 0, 0)


def times_rows_body(meta, *refs, count):
    pieces, weight_ref, outs = refs[:count], refs[count], refs[-count:]
    for piece, out_ref in zip(pieces, outs):
        out_ref[...] = dot(piece[...], weight_ref[...], ROWS_BY_ROWS).astype(out_ref.dtype)


def up_body(meta, a_ref, b_ref, weight_ref, dup_a, dup_b, gain_ref, *refs):
    act_ref, slope_ref, stat_ref = refs[-7:-4]
    sums = refs[-4:]
    step = pl.program_id(0)
    rows = a_ref.shape[0]

    @pl.when(step == 0)
    def _():
        for ref in sums:
            ref[...] = jnp.zeros_like(ref)

    for n, (ref, dup_ref) in enumerate(((a_ref, dup_a), (b_ref, dup_b))):
        here = slice(n * rows, (n + 1) * rows)
        pre = dot(ref[...], weight_ref[...])
        share = 0.5 + 0.5 * lax.erf(pre * (0.5**0.5))
        density = jnp.exp(pre * pre * -0.5) * ((2.0 * jnp.pi) ** -0.5)
        act = pre * share
        act_ref[here, :] = act.astype(BF)
        slope_ref[here, :] = (share + pre * density).astype(BF)
        scaled = dup_ref[...].astype(F32) * gain_ref[...]
        for ref_sum, term in zip(sums, (act, act * act, scaled, scaled * act)):
            ref_sum[here, :] += lane_sums(term)

    @pl.when(step == pl.num_programs(0) - 1)
    def _():
        rows_of = [rows_from(ref_sum[...]) for ref_sum in sums]
        row = lax.broadcasted_iota(jnp.int32, rows_of[0].shape, 0)
        total = jnp.zeros_like(rows_of[0])
        for n, value in enumerate(rows_of):
            total = jnp.where(row == n, value, total)
        stat_ref[...] = total


def spread_body(meta, act_ref, slope_ref, dup_0, dup_1, dup_2, dup_3, gain_ref, *refs, mp, width):
    stats = refs[:mp]
    pre_ref, low_ref, grad_ref = refs[mp:]
    columns = total_columns(stats)
    act = act_ref[...].astype(F32)
    normed, inv_std = stat_norm(act, columns, 0, width)
    gain = gain_ref[...]
    low_ref[...] = (normed * gain).astype(BF)
    step = pl.program_id(0) // (pl.num_programs(0) // 4)
    upstream = jnp.where(
        step < 2,
        jnp.where(step == 0, dup_0[...], dup_1[...]),
        jnp.where(step == 2, dup_2[...], dup_3[...]),
    ).astype(F32)
    first = columns[:, 2:3] / width
    mean = columns[:, 0:1] / width
    second = (columns[:, 3:4] - mean * columns[:, 2:3]) * inv_std / width
    d_act = inv_std * (upstream * gain - first - normed * second)
    pre_ref[...] = (d_act * slope_ref[...].astype(F32)).astype(BF)
    add_rows(grad_ref, upstream * normed)


def down_body(meta, low_ref, weight_ref, near_ref, far_ref, *scratch):
    rows = near_ref.shape[0]

    def term(j):
        return lambda: dot(low_ref[j * rows : (j + 1) * rows, :], weight_ref[...])

    pair_sums([(term(2), term(3)), (term(0), term(1))], [far_ref, near_ref], scratch)


def sum_body(meta, first_ref, second_ref, third_ref, out_ref):
    out_ref[...] = first_ref[...] + (second_ref[...].astype(F32) + third_ref[...].astype(F32))


def ffn_back_body(meta, own_ref, far_ref, after_ref, cot_ref, gain_ref, out_ref, low_ref, grad_ref):
    upstream = own_ref[...].astype(F32) + far_ref[...].astype(F32)
    normed, inv_std = norm_parts(after_ref[...])
    d_after = cot_ref[...].astype(F32) + norm_back(upstream, normed, inv_std, gain_ref[...])
    out_ref[...] = d_after
    low_ref[...] = d_after.astype(BF)
    add_rows(grad_ref, upstream * normed)


def add_rows(ref, values):
    total = jnp.sum(values, axis=0, keepdims=True)

    @pl.when(pl.program_id(0) == 0)
    def _():
        ref[...] = total

    @pl.when(pl.program_id(0) != 0)
    def _():
        ref[...] += total


def d_mid_body(meta, *refs, mp, width):
    pieces, weight_ref, gain_ref, att_ref = refs[:2], refs[2], refs[3], refs[4]
    stats = refs[5 : 5 + mp]
    out_ref, stat_ref, grad_ref = refs[-3:]
    rows = jnp.where(pl.program_id(0) == 0, pieces[0][...], pieces[1][...])
    d_mid = dot(rows, weight_ref[...], ROWS_BY_ROWS)
    out_ref[...] = d_mid.astype(BF)
    normed, _ = stat_norm(att_ref[...].astype(F32), total_columns(stats), 0, width)
    scaled = d_mid * gain_ref[...]
    add_rows(grad_ref, d_mid * normed)
    stat_ref[...] = two_rows(
        rows_from(lane_sums(scaled)), rows_from(lane_sums(scaled * normed))
    )


def attend_back_body(
    meta, qkv_ref, att_ref, dmid_ref, lse_ref, gain_ref, turn_ref, *refs, mp, width, block
):
    stats, more = refs[:mp], refs[mp : 2 * mp]
    out_ref, d_att, dq, dk, dv = refs[2 * mp :]
    length, wide = att_ref.shape
    columns = total_columns(stats)
    normed, inv_std = stat_norm(att_ref[...].astype(F32), columns, 0, width)
    sums = total_columns(more)
    scaled = dmid_ref[...].astype(F32) * gain_ref[...]
    d_att[...] = (
        inv_std * (scaled - sums[:, 0:1] / width - normed * (sums[:, 1:2] / width))
    ).astype(BF)

    def pair(hp, _):
        lanes, k_lanes, v_lanes = head_lanes(hp, wide)
        keys, values = qkv_ref[:, k_lanes], qkv_ref[:, v_lanes]
        lane = lax.broadcasted_iota(jnp.int32, (block, LANES), 1)
        row = lax.broadcasted_iota(jnp.int32, (block, block), 0)
        col = lax.broadcasted_iota(jnp.int32, (block, block), 1)
        dk[...] = jnp.zeros_like(dk)
        dv[...] = jnp.zeros_like(dv)
        both = d_att[:, lanes].astype(F32) * att_ref[:, lanes].astype(F32)
        side = lax.broadcasted_iota(jnp.int32, (8, LANES), 1) // HEAD
        pick_head = lax.broadcasted_iota(jnp.int32, (8, LANES), 0) == side
        inner = dot_exact(pick_head.astype(F32), both)
        for b in range(length // block):
            rows = slice(b * block, (b + 1) * block)
            end = (b + 1) * block
            query, grad = qkv_ref[rows, lanes], d_att[rows, lanes]
            d_query = jnp.zeros((block, LANES), F32)
            for h in range(2):
                keep = lane // HEAD == h
                q_one = jnp.where(keep, query, jnp.zeros_like(query))
                g_one = jnp.where(keep, grad, jnp.zeros_like(grad))
                scores = dot(keys[:end], q_one, ROWS_BY_ROWS) * 0.125
                shares = jnp.exp(scores - lse_ref[pl.ds(2 * hp + h, 1), rows])
                edge = jnp.where(col >= row, shares[b * block :], 0.0)
                shares = edge if b == 0 else jnp.concatenate([shares[: b * block], edge], axis=0)
                d_shares = dot(values[:end], g_one, ROWS_BY_ROWS)
                d_scores = (shares * (d_shares - inner[h : h + 1, rows])).astype(BF)
                dv[:end, :] += dot(shares.astype(BF), g_one)
                dk[:end, :] += dot(d_scores, q_one)
                turned = dot(d_scores, keys[:end], OVER_ROWS)
                d_query = jnp.where(keep, turned, d_query)
            dq[rows, :] = d_query
        out_ref[:, lanes] = rotated(
            dq[...] * 0.125, turn_ref[0, 0], -turn_ref[0, 1]
        ).astype(BF)
        out_ref[:, k_lanes] = rotated(
            dk[...] * 0.125, turn_ref[1, 0], -turn_ref[1, 1]
        ).astype(BF)
        out_ref[:, v_lanes] = dv[...].astype(BF)
        return 0

    lax.fori_loop(0, wide // LANES, pair, 0)


def three_dots(rows, weight_ref):
    width = weight_ref.shape[2]
    total = None
    for c in range(3):
        term = dot(rows[:, c * width : (c + 1) * width], weight_ref[c], ROWS_BY_ROWS)
        total = term if total is None else total + term
    return total


def slot_back_body(meta, *refs, slots, mp):
    pieces, weight_ref, even_ref, odd_ref, scratch = refs[:slots], refs[slots], *refs[-3:]
    rows = jnp.concatenate([p[...] for p in pieces], axis=0)
    scratch[...] = three_dots(rows, weight_ref)
    latent = pieces[0].shape[0]
    part = latent // mp
    for j in range(mp):
        for s in range(slots):
            start = pl.multiple_of(s * latent + (meta[PART] ^ j) * part, part)
            (odd_ref if j % 2 else even_ref)[j // 2, s] = scratch[pl.ds(start, part), :].astype(BF)


def row_back_body(meta, rows_ref, weight_ref, out_ref, *scratch, which):
    rows = out_ref.shape[0]
    me = lax.axis_index("mp")

    def term(j):
        at = pl.ds(pl.multiple_of(other_of(me, j) * rows, rows), rows)
        return lambda: three_dots(rows_ref[at, :], weight_ref)

    pair_sums([(term(which), term(which + 1))], [out_ref], scratch)


def slot_grad_body(meta, *refs, mp, slots, latent, images, groups):
    own_ref, far_ref, slots_ref, table_ref, gain_ref = refs[:5]
    after, (keep_ref, send_ref, grad_ref) = refs[5:-3], refs[-3:]
    part = latent // mp
    start = pl.multiple_of(meta[PART] * part, part)
    for s in range(slots):
        upstream = own_ref[s].astype(F32) + far_ref[s].astype(F32)
        mixed = slots_ref[s, pl.ds(start, part), :].astype(F32) + kind_of(meta, table_ref)
        normed, inv_std = norm_parts(mixed)
        block = meta[POS + s]
        blocks = after[0].shape[0] // latent
        rel = (block // blocks) ^ meta[PART]
        row = pl.multiple_of((block % blocks) * latent + start, part)
        d_after = after[0][pl.ds(row, part), :]
        for j in range(1, mp):
            d_after = jnp.where(rel == j, after[j][pl.ds(row, part), :], d_after)
        grad_ref[s] = (
            d_after.astype(F32) + norm_back(upstream, normed, inv_std, gain_ref[...])
        ).astype(BF)
    for k in range(groups):
        for i in range(images):
            rank = meta[RANK + (k ^ meta[GROUP]) * images + i]
            value = grad_ref[jnp.maximum(rank, 0)]
            value = jnp.where(rank >= 0, value, jnp.zeros_like(value))
            (send_ref if k % 2 else keep_ref)[k // 2, i * part : (i + 1) * part, :] = value


def in_back_body(
    meta, own_ref, far_ref, after_ref, text_ref, slots_ref, table_ref, gain_ref, out_ref, gain_grad, type_grad
):
    upstream = own_ref[...].astype(F32) + far_ref[...].astype(F32)
    normed, inv_std = norm_parts(mixed_rows(meta, text_ref, slots_ref, table_ref))
    d_mixed = after_ref[...] + norm_back(upstream, normed, inv_std, gain_ref[...])
    block = meta[PART] * pl.num_programs(0) + pl.program_id(0)
    out_ref[...] = jnp.where(meta[BLOCK + block] >= 0, 0.0, d_mixed)
    add_rows(gain_grad, upstream * normed)
    add_rows(type_grad, d_mixed)


def pool_back_body(
    meta, *refs, images, mp
):
    pieces, out_w, key_ref, value_ref, query_ref, key_w, value_w = refs[:mp], *refs[mp : mp + 6]
    kv_ref, query_grad, clip_even, clip_odd, grad_ref, scratch = refs[mp + 6 :]
    part = pieces[0].shape[1]
    for j in range(mp):
        for i in range(images):
            start = pl.multiple_of(i * part * mp + (meta[PART] ^ j) * part, part)
            grad_ref[pl.ds(start, part), :] = pieces[j][i]
    d_heads = dot(grad_ref[...], out_w[...], ROWS_BY_ROWS).astype(BF)
    patches = key_ref.shape[0] // images
    latent, wide = query_ref.shape
    for pair in range(wide // LANES):
        lanes = slice(pair * LANES, (pair + 1) * LANES)
        query = query_ref[:, lanes]
        lane = lax.broadcasted_iota(jnp.int32, query.shape, 1)
        d_query = jnp.zeros((latent, LANES), F32)
        for i in range(images):
            rows = slice(i * patches, (i + 1) * patches)
            keys, values = key_ref[rows, lanes], value_ref[rows, lanes]
            grad = d_heads[i * latent : (i + 1) * latent, lanes]
            d_keys = jnp.zeros((patches, LANES), F32)
            d_values = jnp.zeros((patches, LANES), F32)
            for h in range(2):
                keep = lane // HEAD == h
                shares = pool_shares_of(query, keys, h)
                g_one = jnp.where(keep, grad, jnp.zeros_like(grad))
                q_one = jnp.where(keep, query, jnp.zeros_like(query))
                d_shares = dot(g_one, values, ROWS_BY_ROWS)
                inner = jnp.sum(shares * d_shares, axis=-1, keepdims=True)
                d_scores = (shares * (d_shares - inner)).astype(BF)
                d_query += jnp.where(keep, dot(d_scores, keys), 0.0)
                d_keys += dot(d_scores, q_one, OVER_ROWS)
                d_values += dot(shares.astype(BF), g_one, OVER_ROWS)
            kv_ref[rows, lanes] = (d_keys * 0.125).astype(BF)
            kv_ref[rows, slice(wide + pair * LANES, wide + (pair + 1) * LANES)] = d_values.astype(BF)
        query_grad[:, lanes] = d_query * 0.125
    scratch[...] = dot(kv_ref[:, :wide], key_w[...], ROWS_BY_ROWS) + dot(
        kv_ref[:, wide:], value_w[...], ROWS_BY_ROWS
    )
    piece = patches // mp
    for j in range(mp):
        for i in range(images):
            start = pl.multiple_of(i * patches + (meta[PART] ^ j) * piece, piece)
            (clip_odd if j % 2 else clip_even)[j // 2, i] = scratch[
                pl.ds(start, piece), :
            ].astype(BF)


def weight_body(meta, *refs, lefts, rights, before, has_got, split):
    left, right = refs[:lefts], refs[lefts : lefts + rights]
    rest = refs[lefts + rights :]
    depth = sum(r.shape[0] for r in left)
    total = None
    step = depth // max(lefts, rights)
    for start in range(0, depth, step):
        l_ref, l_at = find(left, start)
        r_ref, r_at = find(right, start)
        term = dot(l_ref[l_at : l_at + step, :], r_ref[r_at : r_at + step, :], OVER_ROWS)
        total = term if total is None else total + term
    if split:
        wide = total.shape[1] // 2
        total = jnp.concatenate([total[:, :wide], total[:, wide:]], axis=0)
    if not has_got:
        rest[-1][0] = total.astype(BF)
        return
    even, odd = rest[-2:]
    total = (total + rest[0][0].astype(F32)).astype(BF)
    step = pl.program_id(0)

    @pl.when(step % 2 == 0)
    def _():
        even[0] = total

    @pl.when(step % 2 == 1)
    def _():
        odd[0] = total


def find(refs, start):
    for ref in refs:
        if start < ref.shape[0]:
            return ref, start
        start -= ref.shape[0]
    return None


def add_body(meta, keep_ref, got_ref, keep_out, send_out):
    keep_out[0] = (keep_ref[0].astype(F32) + got_ref[0].astype(F32)).astype(BF)
    send_out[0] = (keep_ref[1].astype(F32) + got_ref[1].astype(F32)).astype(BF)


def flat_body(meta, kinds, gain_in, gain_ffn, mid_near, mid_far, gain_ff, query_ref, flat_ref, rows_ref):
    rows_ref[...] = jnp.zeros_like(rows_ref)
    line = 0
    lines = [jnp.where(meta[KIND] == c, kinds[...], 0.0) for c in range(3)]
    lines += [gain_in[...], gain_ffn[...], mid_near[...] + mid_far[...], gain_ff[...]]
    for value in lines:
        for start in range(0, value.shape[1], LANES):
            rows_ref[line : line + 1, :] = value[:, start : start + LANES]
            line += 1
    latent, wide = query_ref.shape
    line = rows_ref.shape[0] - latent * wide // LANES
    for start in range(0, wide, LANES):
        rows_ref[line : line + latent, :] = query_ref[:, start : start + LANES]
        line += latent
    flat_ref[...] = rows_ref[...].astype(BF)


def last_body(meta, keep_ref, got_ref, out_ref):
    out_ref[...] = (keep_ref[...].astype(F32) + got_ref[...].astype(F32)).astype(out_ref.dtype)


def plus(meta, first, second, dtype):
    shape = first.shape
    steps = 2 if shape[-2] % 32 == 0 and len(shape) == 2 else 1
    block = (shape[-2] // steps,) + shape[-1:]
    if len(shape) == 3:
        block = shape
    index = lambda i, m: (i,) + (0,) * (len(shape) - 1)
    return call(
        last_body,
        meta,
        (steps,),
        [(first, block, index), (second, block, index)],
        [(shape, dtype, block, index)],
    )[0]


def split_sum(meta, keep, got):
    count, *dims = keep.shape
    pair, one = (2,) + tuple(dims), (1,) + tuple(dims)
    at = lambda i, m: (i, 0, 0)
    return call(
        add_body,
        meta,
        (count // 2,),
        [(keep, pair, at), (got, pair, at)],
        [((count // 2,) + tuple(dims), BF, one, at)] * 2,
    )


def stack_body(meta, first_ref, second_ref, out_ref):
    out_ref[:, 0] = first_ref[...]
    out_ref[:, 1] = second_ref[...]


class GatherDp:
    def __init__(self, meta, values):
        self.meta, self.values = meta, values[None]
        self.pending = list(reversed(bits_of(lax.axis_size("dp"))))
        self.got = swap(self.values, "dp", self.pending.pop(0))

    def step(self):
        count, *dims = self.values.shape
        stacked = call(
            stack_body,
            self.meta,
            (1,),
            [(self.values,), (self.got,)],
            [((count, 2) + tuple(dims), self.values.dtype, None, None)],
        )[0]
        self.values = stacked.reshape((2 * count,) + tuple(dims))
        if self.pending:
            self.got = swap(self.values, "dp", self.pending.pop(0))

    def end(self):
        while self.pending:
            self.step()
        self.step()
        return self.values


class WeightGrads:
    def __init__(self, meta, members, shape, first=1, cost=1):
        self.meta, self.members, self.shape = meta, members, shape
        self.size = lax.axis_size("dp")
        bits = bits_of(self.size)
        widths = [left[0].shape[1] // self.size for left, *_ in members]
        self.plain = any(w % LANES for w in widths) or self.size < 8
        self.first, self.cost = first, cost
        self.order = [first] + [b for b in bits if b != first]
        self.pending = list(self.order)

    def run(self, side, got):
        half, first = self.size // 2, self.first
        before = None
        for left, right, split, at in self.members:
            part = left[0].shape[1] // self.size
            inner = right[0].shape[1]
            block = (1, 2 * part, inner // 2) if split else (1, part, inner)
            place = lambda i, m, at=at: (i,) + at
            pair_place = lambda i, m, at=at: (i // 2,) + at
            column = lambda i, m: (
                0,
                m[GROUP] ^ ((i // first) * 2 * first + side * first + i % first),
            )
            ins = [(a, (a.shape[0], part), column) for a in left] + [(a,) for a in right]
            if got is not None:
                ins.append((got, block, place))
                outs = [((half // 2,) + self.shape, BF, block, pair_place)] * 2
            else:
                outs = [((half,) + self.shape, BF, block, place)]
            aliases = {}
            if before is not None:
                aliases = {len(ins) + 1 + n: n for n in range(len(outs))}
                ins += [(a, None) for a in before]
            before = call(
                functools.partial(
                    weight_body,
                    lefts=len(left),
                    rights=len(right),
                    before=before is not None,
                    has_got=got is not None,
                    split=split,
                ),
                self.meta,
                (half,),
                ins,
                outs,
                aliases=aliases,
                cost=self.cost,
            )
        return before

    def start(self):
        if not self.plain:
            self.got = swap(self.run(1, None)[0], "dp", self.pending.pop(0))

    def step(self):
        if self.plain:
            return
        if len(self.pending) == len(self.order) - 1:
            self.keep, send = self.run(0, self.got)
        else:
            self.keep, send = split_sum(self.meta, self.keep, self.got)
        self.got = swap(send, "dp", self.pending.pop(0))

    def finish(self):
        if not self.plain:
            while self.pending:
                self.step()
            self.total = plus(self.meta, self.keep[0], self.got[0], F32)

    def end(self):
        me = lax.axis_index("dp")
        results = []
        if self.plain:
            for left, right, split, at in self.members:
                whole = dot(jnp.concatenate(left), jnp.concatenate(right), OVER_ROWS).astype(BF)
                whole = whole.reshape(self.size, -1, whole.shape[1])
                whole = pick(whole, [me ^ k for k in range(self.size)])
                results.append(scatter_dp(whole, bits_of(self.size), F32))
            return results
        for left, right, split, at in self.members:
            part = left[0].shape[1] // self.size
            inner = right[0].shape[1]
            high, wide = (2 * part, inner // 2) if split else (part, inner)
            cut = (slice(at[0] * high, (at[0] + 1) * high), slice(at[1] * wide, (at[1] + 1) * wide))
            value = self.total[cut]
            if split:
                value = jnp.concatenate([value[:part], value[part:]], axis=1)
            results.append(value)
        return results


def shards(
    text_embed,
    clip_feats,
    type_table,
    gain_attn_in,
    qkv_weight,
    gain_attn_out,
    out_weight,
    gain_ffn_in,
    up_weight,
    gain_ffn_out,
    down_weight,
    res_query,
    res_key,
    res_value,
    res_out,
    cotangent,
    owner_count,
    image_seq,
    slot_block,
    seq_kind,
):
    mp = lax.axis_size("mp")
    dp = lax.axis_size("dp")
    rows, width = text_embed.shape
    length = rows * mp
    latent = res_query.shape[0]
    slots = slot_block.shape[1]
    images, patches, clip_width = clip_feats.shape
    wide = qkv_weight.shape[2]
    heads = wide // HEAD
    ff = up_weight.shape[1]
    ff_all = ff * mp
    here = rows // latent
    part = latent // mp
    tile = 512

    Order.mark, Order.channel = None, 0
    meta = make_meta(owner_count, image_seq, slot_block, seq_kind, images)
    table = type_table.astype(F32)
    gain_in, gain_out = gain_attn_in[None], gain_attn_out[None]
    gain_ffn, gain_ff = gain_ffn_in[None], gain_ffn_out[None]
    row_block = lambda i, m: (i, 0)
    few = (latent, width)
    weight = jnp.moveaxis(qkv_weight, 1, 0)
    turn = turn_tables(length)

    text_in = call(
        text_body,
        meta,
        (4,),
        [(text_embed, (rows // 4, width), row_block), (table,), (gain_in,)],
        [((rows, width), BF, (rows // 4, width), row_block)],
    )[0]
    text_pieces = gather_start(text_in)


    clip = clip_feats.reshape(images * patches, clip_width)
    key_proj, value_proj, pool_out = call(
        functools.partial(pool_body, images=images),
        meta,
        (1,),
        [(clip,), (res_key,), (res_value,), (res_query,)],
        [
            ((images * patches, wide), BF, None, None),
            ((images * patches, wide), BF, None, None),
            ((images * latent, wide), BF, None, None),
        ],
    )
    gathering = GatherDp(meta, pool_out)
    state = project(meta, text_pieces[:2], weight, turn, None, 0)
    gathering.step()
    gather_end(meta, text_pieces)
    state = project(meta, text_pieces[2:], weight, turn, state, 2)
    gathering.step()

    def d_up_half(which):
        return call(
            functools.partial(times_rows_body, count=2),
            meta,
            (ff // tile,),
            [(cot_pieces[which + n],) for n in range(2)]
            + [(down_weight, (tile, width), row_block)],
            [((rows, ff), BF, (rows, tile), lambda i, m: (0, i))] * 2,
        )

    pool_rows = gathering.end().reshape(dp * images * latent, wide)
    slot_terms = call(
        functools.partial(pooled_body, slots=slots, mp=mp),
        meta,
        (1,),
        [
            (pool_rows, (latent, wide), lambda i, m, s=s: (m[SOURCE + s], 0))
            for s in range(slots)
        ]
        + [(res_out,)],
        [((mp // 2, slots, part, width), BF, None, None)] * 2,
        scratch=[pltpu.VMEM((slots * latent, width), F32)],
    )
    slot_own, slot_far = scatter_now(meta, *slot_terms)
    slot_pieces = gather_now(meta, add_low(slot_own, slot_far))

    cot = call(
        copy_body,
        meta,
        (2,),
        [(cotangent, (rows // 2, width), row_block)],
        [((rows, width), BF, (rows // 2, width), row_block)],
    )[0]
    cot_pieces = gather_start(cot)

    at_slot = lambda i, m: (m[POS + jnp.maximum(i - 3, 0)], 0)
    state = call(
        functools.partial(slot_body, mp=mp, slots=slots, latent=latent),
        meta,
        (3 + slots,),
        [(p,) for p in slot_pieces]
        + [(table,), (gain_in,)]
        + [(weight, (1, width, wide), lambda i, m: (jnp.minimum(i, 2), 0, 0))]
        + [(turn, (3, 2, latent, LANES), lambda i, m: (0, 0) + at_slot(i, m))]
        + [(a, (latent, a.shape[1]), at_slot) for a in state],
        [(a.shape, BF, (latent, a.shape[1]), at_slot) for a in state]
        + [((slots, latent, width), BF, None, None)],
        scratch=[
            pltpu.VMEM((slots, latent, width), F32),
            pltpu.VMEM((3, slots, latent, wide), F32),
            pltpu.VMEM((slots, latent, width), BF),
        ],
        aliases={mp + 5 + n: n for n in range(2)},
    )
    qkv, in_full, slot_rows = state

    att, lse, att_stats = call(
        functools.partial(attend_body, block=rows),
        meta,
        (1,),
        [(qkv,)],
        [
            ((length, wide), BF, None, None),
            ((heads, length), F32, None, None),
            ((8, length), F32, None, None),
        ],
        scratch=[pltpu.VMEM((length, LANES), F32)] * 3,
    )
    att_stats = spread_stats(meta, att_stats)

    mids = call(
        functools.partial(mid_body, mp=mp, width=width),
        meta,
        (mp,),
        [(att, (rows, wide), lambda j, m: (m[PART] ^ j, 0)), (gain_out,)]
        + [(s, (8, rows), lambda j, m: (0, m[PART] ^ j)) for s in att_stats],
        [((length, wide), BF, (rows, wide), lambda j, m: (j, 0))],
    )[0]
    steps = width // tile

    def summed(body, array, weights, which):
        return call(
            body,
            meta,
            (steps,),
            [(array, (2 * rows, array.shape[1]), lambda i, m: (which // 2, 0)), weights],
            [((rows, width), BF, None, None)],
            scratch=pair_scratch(1, steps, rows, tile),
            remote=True,
        )[0]

    out_w = (out_weight, (wide, tile), lambda i, m: (0, i))
    out_far = swap(summed(out_body, mids, out_w, 2), "mp", 2)
    out_terms = [summed(out_body, mids, out_w, 0), out_far]
    d_up_near = d_up_half(0)
    gather_end(meta, cot_pieces)
    d_up = d_up_near + d_up_half(2)
    after_attn, ffn_in = call(
        after_body,
        meta,
        (here,),
        [(t, few, row_block) for t in out_terms]
        + [(text_embed, few, row_block), (slot_rows, (1,) + few, slot_index(here))]
        + [(table,), (gain_ffn,)],
        [((rows, width), F32, few, row_block), ((rows, width), BF, few, row_block)],
    )
    ffn_pieces = gather_start(ffn_in)

    def up_half(which, before):
        lanes_of = lambda i, m: (0, i)
        half = lambda i, m: (which // 2, i)
        ins = [(ffn_pieces[which],), (ffn_pieces[which + 1],)]
        ins += [(up_weight, (width, tile), lanes_of)]
        ins += [(d_up[which + n], (rows, tile), lanes_of) for n in range(2)]
        ins += [(gain_ff, (1, tile), lanes_of)]
        aliases = {}
        if before is not None:
            aliases = {len(ins) + 1 + n: n for n in range(3)}
            ins += [(a, None) for a in before]
        return call(
            up_body,
            meta,
            (ff // tile,),
            ins,
            [
                ((length, ff), BF, (2 * rows, tile), half),
                ((length, ff), BF, (2 * rows, tile), half),
                ((8, length), F32, (8, 2 * rows), lambda i, m: (0, which // 2)),
            ],
            scratch=[pltpu.VMEM((2 * rows, LANES), F32)] * 4,
            aliases=aliases,
        )

    state = up_half(0, None)
    gather_end(meta, ffn_pieces)
    act, slope, ff_stats = up_half(2, state)
    ff_stats = spread_stats(meta, ff_stats)
    cut = rows // 2
    fine = lambda i, m: (i, 0)
    pre, low, gain_ff_local = call(
        functools.partial(spread_body, mp=mp, width=ff_all),
        meta,
        (length // cut,),
        [(act, (cut, ff), fine), (slope, (cut, ff), fine)]
        + [
            (d_up[j], (cut, ff), lambda i, m, j=j: (jnp.clip(i - 2 * j, 0, 1), 0))
            for j in range(mp)
        ]
        + [(gain_ff,)]
        + [
            (s, (8, cut), lambda i, m, b=b: (0, (((i // 2) ^ b) * 2) + i % 2))
            for b, s in enumerate(ff_stats)
        ],
        [((length, ff), BF, (cut, ff), fine)] * 2 + [((1, ff), F32, None, None)],
    )

    up_w = (up_weight, (tile, ff), row_block)
    down_grad = WeightGrads(meta, [(cot_pieces, [low], False, (0, 0))], (width // dp, ff))
    up_grad = WeightGrads(meta, [(ffn_pieces, [pre], False, (0, 0))], (width // dp, ff), 2)
    down_grad.start()
    up_grad.start()
    back_far = swap(summed(back_body, pre, up_w, 2), "mp", 2)
    ffn_terms = [summed(back_body, pre, up_w, 0), back_far]
    d_after, d_after_low, gain_ffn_local = call(
        ffn_back_body,
        meta,
        (here,),
        [(t, few, row_block) for t in ffn_terms]
        + [(after_attn, few, row_block), (cotangent, few, row_block), (gain_ffn,)],
        [
            ((rows, width), F32, few, row_block),
            ((rows, width), BF, few, row_block),
            ((1, width), F32, None, None),
        ],
    )
    after_pieces = gather_start(d_after_low)

    def d_mid_half(which, before):
        block = lambda i, m: (m[PART] ^ (which + i), 0)
        lane_block = lambda i, m: (0, m[PART] ^ (which + i))
        aliases = {}
        ins = [(after_pieces[which],), (after_pieces[which + 1],), (out_weight,), (gain_out,)]
        ins += [(att, (rows, wide), block)] + [(s, (8, rows), lane_block) for s in att_stats]
        if before is not None:
            aliases = {len(ins) + 1 + n: n for n in range(2)}
            ins += [(a, None) for a in before]
        return call(
            functools.partial(d_mid_body, mp=mp, width=width),
            meta,
            (2,),
            ins,
            [
                ((length, wide), BF, (rows, wide), block),
                ((8, length), F32, (8, rows), lane_block),
                ((1, wide), F32, None, None),
            ],
            aliases=aliases,
        )

    d_mid, mid_stats, gain_mid_near = d_mid_half(0, None)
    down_near, down_far = call(
        down_body,
        meta,
        (steps,),
        [(low,), (down_weight, (ff, tile), lambda i, m: (0, i))],
        [((rows, width), BF, None, None)] * 2,
        scratch=pair_scratch(2, steps, rows, tile),
        remote=True,
    )
    gather_end(meta, after_pieces)
    d_mid, mid_stats, gain_mid_far = d_mid_half(2, (d_mid, mid_stats))
    mid_stats = spread_stats(meta, mid_stats)
    down_far = swap(
        call(
            copy_body,
            meta,
            (2,),
            [(down_far, (rows // 2, width), row_block)],
            [((rows, width), BF, (rows // 2, width), row_block)],
        )[0],
        "mp",
        2,
    )
    out_grad = WeightGrads(meta, [(after_pieces, [mids], False, (0, 0))], (width // dp, wide))
    out_grad.start()
    down_grad.step()
    d_qkv = call(
        functools.partial(attend_back_body, mp=mp, width=width, block=rows),
        meta,
        (1,),
        [(a,) for a in (qkv, att, d_mid, lse, gain_out, turn)]
        + [(s,) for s in att_stats]
        + [(s,) for s in mid_stats],
        [((length, 3 * wide), BF, None, None)],
        scratch=[pltpu.VMEM((length, wide), BF)] + [pltpu.VMEM((length, LANES), F32)] * 3,
    )[0]

    slot_terms = call(
        functools.partial(slot_back_body, slots=slots, mp=mp),
        meta,
        (1,),
        [
            (d_qkv, (latent, 3 * wide), lambda i, m, s=s: (m[POS + s], 0))
            for s in range(slots)
        ]
        + [(weight,)],
        [((mp // 2, slots, part, width), BF, None, None)] * 2,
        scratch=[pltpu.VMEM((slots * latent, width), F32)],
    )
    slot_terms = scatter_now(meta, *slot_terms)
    image_keep, image_send, _ = call(
        functools.partial(
            slot_grad_body, mp=mp, slots=slots, latent=latent, images=images, groups=dp
        ),
        meta,
        (1,),
        [(t,) for t in slot_terms]
        + [(slot_rows,), (table,), (gain_in,)]
        + [(a,) for a in after_pieces],
        [((dp // 2, images * part, width), BF, None, None)] * 2
        + [((slots, part, width), BF, None, None)],
    )
    image_got = exchange(meta, (image_send, "dp", 1))[0]
    in_grad = WeightGrads(meta, [([in_full], [d_qkv], False, (0, 0))], (width // dp, 3 * wide))
    def row_terms(which):
        return call(
            functools.partial(row_back_body, which=which),
            meta,
            (steps,),
            [(d_qkv,), (weight, (3, tile, wide), lambda i, m: (0, i, 0))],
            [((rows, width), BF, None, None)],
            scratch=pair_scratch(1, steps, rows, tile),
            remote=True,
        )[0]

    for bit in bits_of(dp)[1:]:
        image_keep, image_send = split_sum(meta, image_keep, image_got)
        image_got = exchange(meta, (image_send, "dp", bit))[0]
        if bit == 2:
            layer_out = call(
                sum_body,
                meta,
                (here,),
                [(after_attn, few, row_block), (down_near, few, row_block), (down_far, few, row_block)],
                [((rows, width), F32, few, row_block)],
            )[0]
            out_grad.step()
            up_grad.step()
            in_grad.start()
            in_far = swap(row_terms(2), "mp", 2)
    down_grad.step()
    out_grad.step()
    owned = plus(meta, image_keep, image_got, BF).reshape(images, part, width)
    owned_pieces = gather_now(meta, owned)
    d_kv, query_local, clip_even, clip_odd, pool_grad = call(
        functools.partial(pool_back_body, images=images, mp=mp),
        meta,
        (1,),
        [(a,) for a in owned_pieces]
        + [(a,) for a in (res_out, key_proj, value_proj, res_query, res_key, res_value)],
        [
            ((images * patches, 2 * wide), BF, None, None),
            ((latent, wide), F32, None, None),
            ((mp // 2, images, patches // mp, clip_width), BF, None, None),
            ((mp // 2, images, patches // mp, clip_width), BF, None, None),
            ((images * latent, width), BF, None, None),
        ],
        scratch=[pltpu.VMEM((images * patches, clip_width), F32)],
    )
    pool_grads = WeightGrads(
        meta,
        [
            ([pool_grad], [pool_out], False, (0, 0)),
            ([clip], [d_kv], True, (1, 0)),
        ],
        (width // dp + 2 * (clip_width // dp), wide),
    )
    down_grad.finish()
    in_grad.step()
    pool_grads.start()
    in_terms = [row_terms(0), in_far]
    text_grad, gain_in_local, type_local = call(
        in_back_body,
        meta,
        (here,),
        [(t, few, row_block) for t in in_terms]
        + [(d_after, few, row_block), (text_embed, few, row_block)]
        + [(slot_rows, (1,) + few, slot_index(here)), (table,), (gain_in,)],
        [
            ((rows, width), F32, few, row_block),
            ((1, width), F32, None, None),
            ((1, width), F32, None, None),
        ],
    )
    down_grad.finish()
    hops = bits_of(dp)[1:] + [1]
    small = (type_local, gain_in_local, gain_ffn_local, gain_mid_near, gain_mid_far, gain_ff_local)
    sizes = 5 * width + wide + ff
    lines = -(-sizes // (16 * LANES)) * 16 + latent * wide // LANES
    flat = call(
        flat_body,
        meta,
        (1,),
        [(x,) for x in small] + [(query_local,)],
        [((lines, LANES), BF, None, None)],
        scratch=[pltpu.VMEM((lines, LANES), F32)],
    )[0]
    for n, bit in enumerate(hops):
        got = swap(flat, "dp", bit)
        if n == 0:
            up_grad.step()
            clip_even = add_low(clip_even, exchange(meta, (clip_odd, "mp", 1))[0])
            clip_far = exchange(meta, (clip_even[1], "mp", 2))[0]
        elif n == len(hops) - 2:
            pool_grads.step()
            in_grad.step()
        elif n == len(hops) - 1:
            up_grad.finish()
            pool_grads.step()
        flat = plus(meta, flat, got, BF)
    flat_far, flat_near = exchange(meta, (flat, "mp", 2), (flat, "mp", 1))
    flat_last = exchange(meta, (flat_far, "mp", 1))[0]
    out_grad.finish()
    pool_grads.finish()
    in_grad.finish()
    clip_grad = clip_even[0].astype(F32) + clip_far.astype(F32)
    flat = by_mp(jnp.stack([flat, flat_near, flat_far, flat_last])).astype(F32)
    edge = flat.shape[1] - latent * wide // LANES
    parts = flat[:, :edge].reshape(mp, -1)
    sums = jnp.sum(parts[:, : 5 * width].reshape(mp, 5, width), axis=0)
    parts = parts[:, 5 * width :]
    query_grad = flat[:, edge:].reshape(mp, wide // LANES, latent, LANES).swapaxes(1, 2)
    query_grad = jnp.swapaxes(query_grad.reshape(mp, latent, wide), 0, 1)
    res_out_grad, kv_grad = pool_grads.end()
    qkv_grad, out_grad = in_grad.end()[0], out_grad.end()[0]
    return (
        layer_out,
        text_grad,
        clip_grad,
        sums[:3],
        sums[3],
        qkv_grad.reshape(-1, 3, wide),
        parts[:, :wide].reshape(-1),
        out_grad.T,
        sums[4],
        up_grad.end()[0],
        parts[:, wide : wide + ff].reshape(-1),
        down_grad.end()[0].T,
        query_grad.reshape(latent, width),
        kv_grad[:, :wide],
        kv_grad[:, wide:],
        res_out_grad.T,
    )


def solution(mesh):
    return jax.shard_map(
        shards,
        mesh=mesh,
        in_specs=(
            P(("dp", "mp"), None),
            P("dp", None, None),
            P(),
            P(),
            P(None, None, "mp"),
            P("mp"),
            P("mp", None),
            P(),
            P(None, "mp"),
            P("mp"),
            P("mp", None),
            P(None, "mp"),
            P(None, "mp"),
            P(None, "mp"),
            P("mp", None),
            P(("dp", "mp"), None),
            P(),
            P(),
            P(),
            P(),
        ),
        out_specs=(
            P(("dp", "mp"), None),
            P(("dp", "mp"), None),
            P("dp", "mp", None),
            P(),
            P(),
            P("dp", None, "mp"),
            P(),
            P("mp", "dp"),
            P(),
            P("dp", "mp"),
            P(),
            P("mp", "dp"),
            P(),
            P("dp", "mp"),
            P("dp", "mp"),
            P("mp", "dp"),
        ),
        check_vma=False,
    )
```

```python
import functools

import jax
import jax.numpy as jnp
from jax import lax
from jax.experimental import pallas as pl
from jax.experimental.pallas import tpu as pltpu
from jax.sharding import PartitionSpec as P

HEAD = 64
LANES = 128
EPS = 1e-05
NEG = -1e30
XPOS_BASE = 512.0
BF = jnp.bfloat16
F32 = jnp.float32
ROWS_BY_ROWS = (((1,), (1,)), ((), ()))
PLAIN = (((1,), (0,)), ((), ()))
OVER_ROWS = (((0,), (0,)), ((), ()))
KIND, PART, GROUP, REAL, POS, SOURCE, BLOCK, RANK = 0, 1, 2, 4, 8, 12, 16, 32
VMEM_BYTES = 14 * 1024 * 1024


def dot(left, right, form=PLAIN):
    return lax.dot_general(left, right, form, preferred_element_type=F32)


def dot_exact(left, right, form=ROWS_BY_ROWS):
    return lax.dot_general(
        left, right, form, precision=lax.Precision.HIGHEST, preferred_element_type=F32
    )


def swap(values, axis, bit):
    size = lax.axis_size(axis)
    return lax.ppermute(values, axis, [(i, i ^ bit) for i in range(size)])


def bits_of(size):
    return [1 << i for i in range(size.bit_length() - 1)]


def gather_start(values):
    far, near = swap(values, "mp", 2), swap(values, "mp", 1)
    return [values, near, far]


def gather_end(meta, pieces):
    pieces.append(exchange(meta, (pieces[2], "mp", 1))[0])


def add_low(first, second):
    return (first.astype(F32) + second.astype(F32)).astype(BF)


def scatter_pairs(even, odd):
    near = add_low(even, swap(odd, "mp", 1))
    return near[0], swap(near[1], "mp", 2), near


def sum_pairs(even, odd):
    own, far, _ = scatter_pairs(even, odd)
    return own.astype(F32) + far.astype(F32)


def pick(values, indices):
    return jnp.stack([lax.dynamic_index_in_dim(values, i, 0, keepdims=False) for i in indices])


def by_mp(values):
    me = lax.axis_index("mp")
    return pick(values, [me ^ j for j in range(lax.axis_size("mp"))])


def halve(values, axis):
    return (
        lax.index_in_dim(values, 0, axis, keepdims=False),
        lax.index_in_dim(values, 1, axis, keepdims=False),
    )


def scatter_dp(values, bits, last):
    for bit in bits:
        values = values.reshape((-1, 2) + values.shape[1:])
        keep, send = halve(values, 1)
        got = swap(send, "dp", bit)
        total = keep.astype(F32) + got.astype(F32)
        values = total.astype(last if bit == bits[-1] else BF)
    return values[0]


class Order:
    mark = None
    channel = 0


def call(body, meta, grid, ins, outs, scratch=(), aliases=None, remote=False, after=(), cost=1, room=VMEM_BYTES):
    arrays, specs = [], []
    for item in ins:
        arrays.append(item[0])
        if len(item) == 1:
            dims = item[0].ndim
            specs.append(
                pl.BlockSpec(
                    item[0].shape,
                    lambda *_, dims=dims: (0,) * dims,
                    pipeline_mode=pl.Buffered(1),
                )
            )
        elif item[1] is None:
            specs.append(pl.BlockSpec(memory_space=pl.ANY))
        else:
            specs.append(pl.BlockSpec(item[1], item[2]))
    shapes, out_specs = [], []
    for shape, dtype, block, index in list(outs) + [((8, LANES), F32, None, None)]:
        shapes.append(jax.ShapeDtypeStruct(shape, dtype))
        if index == "any":
            out_specs.append(pl.BlockSpec(memory_space=pl.ANY))
        elif block is None:
            dims = len(shape)
            out_specs.append(pl.BlockSpec(shape, lambda *_, dims=dims: (0,) * dims))
        else:
            out_specs.append(pl.BlockSpec(block, index))
    count, after = len(ins), list(after)
    if Order.mark is not None:
        after.append(Order.mark)
    specs += [pl.BlockSpec(memory_space=pl.ANY)] * len(after)

    params = pltpu.CompilerParams(vmem_limit_bytes=room)
    if remote:
        Order.channel += 1
        params = pltpu.CompilerParams(
            vmem_limit_bytes=room, collective_id=Order.channel, has_side_effects=True
        )

    def marked(meta_ref, *refs):
        refs = refs[:count] + refs[count + len(after) :]
        place = count + len(outs)
        refs[place][...] = jnp.zeros((8, LANES), F32)
        body(meta_ref, *refs[:place], *refs[place + 1 :])

    result = pl.pallas_call(
        marked,
        out_shape=shapes,
        grid_spec=pltpu.PrefetchScalarGridSpec(
            num_scalar_prefetch=1,
            grid=grid,
            in_specs=specs,
            out_specs=out_specs,
            scratch_shapes=list(scratch),
        ),
        input_output_aliases=aliases or {},
        compiler_params=params,
        cost_estimate=pl.CostEstimate(
            flops=cost * 1000000, bytes_accessed=1024, transcendentals=0
        ),
        name=getattr(body, "func", body).__name__,
    )(meta, *arrays, *after)
    Order.mark = result[-1]
    return result[:-1]


def norm_parts(values):
    width = values.shape[-1]
    mean = jnp.sum(values, axis=-1, keepdims=True) / width
    square = jnp.sum(values * values, axis=-1, keepdims=True) / width
    inv_std = lax.rsqrt(square - mean * mean + EPS)
    return (values - mean) * inv_std, inv_std


def norm_back(upstream, normed, inv_std, gain):
    width = upstream.shape[-1]
    scaled = upstream * gain
    first = jnp.sum(scaled, axis=-1, keepdims=True) / width
    second = jnp.sum(scaled * normed, axis=-1, keepdims=True) / width
    return inv_std * (scaled - first - normed * second)


def columns_of(rows):
    count, length = rows.shape
    full = jnp.concatenate([rows, jnp.zeros((LANES - count, length), F32)], axis=0)
    return full.T


def lane_sums(values):
    total = values[:, :LANES]
    for start in range(LANES, values.shape[1], LANES):
        total = total + values[:, start : start + LANES]
    return total


def rows_from(partials):
    return dot_exact(jnp.ones((8, LANES), F32), partials)


def two_rows(first, second):
    row = lax.broadcasted_iota(jnp.int32, first.shape, 0)
    return jnp.where(row == 0, first, jnp.where(row == 1, second, 0.0))


def meta_body(count_ref, seq_ref, slot_ref, kind_ref, me_ref, out_ref, *, image_local, slots, images):
    me_m, me_d = me_ref[0], me_ref[1]

    def clear(i, _):
        out_ref[i] = 0
        return 0

    lax.fori_loop(0, BLOCK, clear, 0)

    def absent(i, _):
        out_ref[BLOCK + i] = -1
        return 0

    lax.fori_loop(0, RANK - BLOCK + images, absent, 0)
    out_ref[KIND] = kind_ref[me_d]
    out_ref[PART] = me_m
    out_ref[GROUP] = me_d
    for s in range(slots):
        out_ref[POS + s] = slot_ref[me_d, s]

    def one(i, found):
        owner = i // image_local
        inside = i - owner * image_local
        here = jnp.logical_and(inside < count_ref[owner], seq_ref[i] == me_d)
        rank = jnp.minimum(found, slots - 1)

        @pl.when(here)
        def _():
            out_ref[REAL + rank] = 1
            out_ref[SOURCE + rank] = (owner ^ me_d) * image_local + inside
            out_ref[BLOCK + slot_ref[me_d, rank]] = rank
            out_ref[RANK + i] = rank

        return found + here.astype(jnp.int32)

    lax.fori_loop(0, images, one, jnp.int32(0))


def make_meta(owner_count, image_seq, slot_block, seq_kind, image_local):
    me = jnp.stack([lax.axis_index("mp"), lax.axis_index("dp")]).astype(jnp.int32)
    images = image_seq.shape[0]
    smem = pl.BlockSpec(memory_space=pltpu.SMEM)
    return pl.pallas_call(
        functools.partial(
            meta_body, image_local=image_local, slots=slot_block.shape[1], images=images
        ),
        out_shape=jax.ShapeDtypeStruct((RANK + images,), jnp.int32),
        in_specs=[smem] * 5,
        out_specs=smem,
    )(owner_count, image_seq, slot_block, seq_kind, me)


def other_of(me, j):
    return [me, me + 1 - 2 * (me % 2), (me + 2) % 4, 3 - me][j]


def pair_sums(terms, out_refs, scratch):
    sent, came, kept, send_sem, recv_sem = scratch
    step, steps = pl.program_id(0), pl.num_programs(0)
    partner = {"mp": other_of(lax.axis_index("mp"), 1)}

    @pl.when(step == 0)
    def _():
        barrier = pltpu.get_barrier_semaphore()
        pl.semaphore_signal(barrier, inc=1, device_id=partner)
        pl.semaphore_wait(barrier, 1)

    def move(n, place):
        return pltpu.make_async_remote_copy(
            src_ref=sent.at[n, place],
            dst_ref=came.at[n, place],
            send_sem=send_sem.at[n, place],
            recv_sem=recv_sem.at[n, place],
            device_id=partner,
        )

    for n, (mine, theirs) in enumerate(terms):
        sent[n, step] = theirs().astype(BF)
        move(n, step).start()
        kept[n, step] = mine()

    @pl.when(step == steps - 1)
    def _():
        tile = sent.shape[-1]
        for n, out_ref in enumerate(out_refs):
            for place in range(sent.shape[1]):
                move(n, place).wait()
                total = kept[n, place] + came[n, place].astype(F32)
                out_ref[:, place * tile : (place + 1) * tile] = total.astype(BF)


def flipped(me, bit):
    return me + bit * (1 - 2 * ((me // bit) % 2))


def exchange(meta, *items):
    places = sorted({(axis, bit) for _, axis, bit in items})
    count = len(items)

    def body(meta_ref, *refs):
        sources, targets, (send_sem, recv_sem) = refs[:count], refs[count : 2 * count], refs[-2:]

        def partner(axis, bit):
            me = lax.axis_index(axis)
            for one in bits_of(lax.axis_size(axis)):
                if bit & one:
                    me = flipped(me, one)
            return {axis: me}

        barrier = pltpu.get_barrier_semaphore()
        for axis, bit in places:
            pl.semaphore_signal(barrier, inc=1, device_id=partner(axis, bit))
        pl.semaphore_wait(barrier, len(places))
        copies = [
            pltpu.make_async_remote_copy(
                src_ref=sources[n],
                dst_ref=targets[n],
                send_sem=send_sem.at[n],
                recv_sem=recv_sem.at[n],
                device_id=partner(axis, bit),
            )
            for n, (_, axis, bit) in enumerate(items)
        ]
        for copy in copies:
            copy.start()
        for copy in copies:
            copy.wait()

    return call(
        body,
        meta,
        (1,),
        [(array, None) for array, _, _ in items],
        [(array.shape, array.dtype, None, "any") for array, _, _ in items],
        scratch=[pltpu.SemaphoreType.DMA((count,)), pltpu.SemaphoreType.DMA((count,))],
        remote=True,
        room=2 * 1024 * 1024,
    )


def spread_stats(meta, values):
    others = range(1, lax.axis_size("mp"))
    return [values] + list(exchange(meta, *[(values, "mp", b) for b in others]))


def gather_now(meta, values):
    far, near = exchange(meta, (values, "mp", 2), (values, "mp", 1))
    return [values, near, far, exchange(meta, (far, "mp", 1))[0]]


def scatter_now(meta, even, odd):
    near = add_low(even, exchange(meta, (odd, "mp", 1))[0])
    return near[0], exchange(meta, (near[1], "mp", 2))[0]


def pair_scratch(count, steps, rows, tile):
    shape = (count, steps, rows, tile)
    return [
        pltpu.VMEM(shape, BF),
        pltpu.VMEM(shape, BF),
        pltpu.VMEM(shape, F32),
        pltpu.SemaphoreType.DMA((count, steps)),
        pltpu.SemaphoreType.DMA((count, steps)),
    ]


def kind_of(meta, table_ref):
    return table_ref[pl.ds(meta[KIND], 1), :]


def text_body(meta, text_ref, table_ref, gain_ref, out_ref):
    mixed = text_ref[...].astype(F32) + kind_of(meta, table_ref)
    out_ref[...] = (norm_parts(mixed)[0] * gain_ref[...]).astype(BF)


def rotated(values, cosine, sine):
    width = values.shape[1]
    lane = lax.broadcasted_iota(jnp.int32, values.shape, 1)
    other = jnp.where(
        lane % HEAD < HEAD // 2,
        pltpu.roll(values, width - HEAD // 2, 1),
        pltpu.roll(values, HEAD // 2, 1),
    )
    repeat = width // LANES
    cosine = jnp.concatenate([cosine] * repeat, axis=1)
    sine = jnp.concatenate([sine] * repeat, axis=1)
    return values * cosine + other * sine


def qkv_body(meta, near_ref, far_ref, weight_ref, turn_ref, *refs, which):
    out_ref, in_ref = refs[-2:]
    rows = near_ref.shape[0]
    for n, ref in enumerate((near_ref, far_ref)):
        at = pl.ds(pl.multiple_of(((meta[PART] ^ (which + n)) % 2) * rows, rows), rows)
        product = dot(ref[...], weight_ref[0])
        out_ref[at, :] = rotated(product, turn_ref[0, 0, at, :], turn_ref[0, 1, at, :]).astype(BF)
        in_ref[at, :] = ref[...]


def project(meta, pieces, weight, turn, before, which, after=()):
    rows, depth = pieces[0].shape
    width = weight.shape[2]
    length = rows * lax.axis_size("mp")
    pair = lambda m: (m[PART] ^ which) // 2
    ins = [(pieces[0],), (pieces[1],), (weight, (1, depth, width), lambda i, m: (i, 0, 0))]
    ins.append((turn, (1, 2, 2 * rows, LANES), lambda i, m: (i, 0, pair(m), 0)))
    aliases = {}
    if before is not None:
        for n, array in enumerate(before):
            ins.append((array, None))
            aliases[5 + n] = n
    return call(
        functools.partial(qkv_body, which=which),
        meta,
        (3,),
        ins,
        [
            ((length, 3 * width), BF, (2 * rows, width), lambda i, m: (pair(m), i)),
            ((length, depth), BF, (2 * rows, depth), lambda i, m: (pair(m), 0)),
        ],
        aliases=aliases,
        after=after,
    )


def slot_body(meta, *refs, mp, slots, latent):
    pieces = refs[:mp]
    table_ref, gain_ref, weight_ref, turn_ref, qkv_in, x_in = refs[mp : mp + 6]
    qkv_ref, x_ref, slots_ref, rows_ref, new_ref, norm_ref = refs[mp + 6 :]
    step = pl.program_id(0)
    part = latent // mp

    @pl.when(step == 0)
    def _():
        for j in range(mp):
            place = pl.multiple_of((meta[PART] ^ j) * part, part)
            for s in range(slots):
                rows_ref[s, pl.ds(place, part), :] = pieces[j][s].astype(F32)
        mixed = rows_ref[...].reshape(slots * latent, -1)
        slots_ref[...] = mixed.astype(BF).reshape(slots_ref.shape)
        mixed = mixed + kind_of(meta, table_ref)
        normed = (norm_parts(mixed)[0] * gain_ref[...]).astype(BF)
        norm_ref[...] = normed.reshape(norm_ref.shape)

    @pl.when(step < 3)
    def _():
        product = dot(norm_ref[...].reshape(slots * latent, -1), weight_ref[0])
        new_ref[step] = product.reshape(new_ref.shape[1:])

    @pl.when(step >= 3)
    def _():
        slot = step - 3
        real = meta[REAL + slot] > 0
        width = new_ref.shape[-1]
        for c in range(3):
            at = slice(c * width, (c + 1) * width)
            value = rotated(new_ref[c, slot], turn_ref[c, 0], turn_ref[c, 1]).astype(BF)
            qkv_ref[:, at] = jnp.where(real, value, qkv_in[:, at])
        x_ref[...] = jnp.where(real, norm_ref[slot], x_in[...])


def turn_tables(length):
    positions = jnp.arange(length, dtype=F32)[:, None]
    lane = jnp.arange(LANES)
    ladder = (lane % (HEAD // 2)).astype(F32)
    angle = positions * jnp.power(10000.0, -2.0 * ladder / HEAD)[None, :]
    decay = (2.0 * ladder + 0.4 * HEAD) / (1.4 * HEAD)
    power = (positions - length // 2) / XPOS_BASE
    sign = jnp.where(lane % HEAD < HEAD // 2, -1.0, 1.0)[None, :]
    cosine, sine = jnp.cos(angle), jnp.sin(angle) * sign
    up = jnp.power(decay[None, :], power)
    down = jnp.power(decay[None, :], -power)
    one, zero = jnp.ones_like(cosine), jnp.zeros_like(cosine)
    return jnp.stack(
        [
            jnp.stack([cosine * up, sine * up]),
            jnp.stack([cosine * down, sine * down]),
            jnp.stack([one, zero]),
        ]
    )


def pool_shares_of(query, keys, head):
    lane = lax.broadcasted_iota(jnp.int32, query.shape, 1)
    masked = jnp.where(lane // HEAD == head, query, jnp.zeros_like(query))
    scores = dot(masked, keys, ROWS_BY_ROWS) * 0.125
    top = jnp.max(scores, axis=-1, keepdims=True)
    weights = jnp.exp(scores - top)
    return weights / jnp.sum(weights, axis=-1, keepdims=True)


def pool_body(
    meta, clip_ref, key_w, value_w, query_ref, key_ref, value_ref, pool_ref, *, images
):
    clip = clip_ref[...]
    key_ref[...] = dot(clip, key_w[...]).astype(BF)
    value_ref[...] = dot(clip, value_w[...]).astype(BF)
    patches = clip.shape[0] // images
    latent = query_ref.shape[0]
    for i in range(images):
        for pair in range(query_ref.shape[1] // LANES):
            lanes = slice(pair * LANES, (pair + 1) * LANES)
            rows = slice(i * patches, (i + 1) * patches)
            query, keys, values = query_ref[:, lanes], key_ref[rows, lanes], value_ref[rows, lanes]
            lane = lax.broadcasted_iota(jnp.int32, query.shape, 1)
            heads = [
                dot(pool_shares_of(query, keys, h).astype(BF), values) for h in range(2)
            ]
            pool_ref[i * latent : (i + 1) * latent, lanes] = jnp.where(
                lane < HEAD, heads[0], heads[1]
            ).astype(BF)


def pooled_body(meta, *refs, slots, mp):
    pieces, out_w, even_ref, odd_ref, scratch = refs[:slots], refs[slots], *refs[slots + 1 :]
    rows = jnp.concatenate([p[...] for p in pieces], axis=0)
    scratch[...] = dot(rows, out_w[...])
    latent = pieces[0].shape[0]
    part = latent // mp
    for j in range(mp):
        for s in range(slots):
            start = pl.multiple_of(s * latent + (meta[PART] ^ j) * part, part)
            (odd_ref if j % 2 else even_ref)[j // 2, s] = scratch[pl.ds(start, part), :].astype(BF)


def copy_body(meta, in_ref, out_ref):
    out_ref[...] = in_ref[...]


def head_lanes(pair, width):
    return [
        pl.ds(pl.multiple_of(c * width + pair * LANES, LANES), LANES) for c in range(3)
    ]


def attend_body(meta, qkv_ref, out_ref, lse_ref, stat_ref, first, second, lse, *, block):
    length, width = out_ref.shape
    first[...] = jnp.zeros_like(first)
    second[...] = jnp.zeros_like(second)

    def pair(hp, _):
        lanes, k_lanes, v_lanes = head_lanes(hp, width)
        keys, values = qkv_ref[:, k_lanes], qkv_ref[:, v_lanes]
        lane = lax.broadcasted_iota(jnp.int32, (block, LANES), 1)
        row = lax.broadcasted_iota(jnp.int32, (block, block), 0)
        col = lax.broadcasted_iota(jnp.int32, (block, block), 1)
        for b in range(length // block):
            rows = slice(b * block, (b + 1) * block)
            end = (b + 1) * block
            query = qkv_ref[rows, lanes]
            outs = []
            for h in range(2):
                masked = jnp.where(lane // HEAD == h, query, jnp.zeros_like(query))
                scores = dot(masked, keys[:end], ROWS_BY_ROWS) * 0.125
                edge = jnp.where(row >= col, scores[:, b * block :], NEG)
                scores = edge if b == 0 else jnp.concatenate([scores[:, : b * block], edge], axis=1)
                top = jnp.max(scores, axis=-1, keepdims=True)
                weights = jnp.exp(scores - top)
                total = jnp.sum(weights, axis=-1, keepdims=True)
                outs.append(dot(weights.astype(BF), values[:end]) / total)
                lse[rows, :] = jnp.where(lane == 2 * hp + h, top + jnp.log(total), lse[rows, :])
            out = jnp.where(lane < HEAD, outs[0], outs[1])
            first[rows, :] += out
            second[rows, :] += out * out
            out_ref[rows, lanes] = out.astype(BF)
        return 0

    lax.fori_loop(0, width // LANES, pair, 0)
    lse_ref[...] = lse[...].T[: lse_ref.shape[0]]
    stat_ref[...] = two_rows(rows_from(first[...]), rows_from(second[...]))


def total_columns(stats):
    total = stats[0][...]
    for other in stats[1:]:
        total = total + other[...]
    return columns_of(total)


def stat_norm(values, columns, at, width):
    mean = columns[:, at : at + 1] / width
    square = columns[:, at + 1 : at + 2] / width
    inv_std = lax.rsqrt(square - mean * mean + EPS)
    return (values - mean) * inv_std, inv_std


def mid_body(meta, att_ref, gain_ref, *refs, mp, width):
    normed, _ = stat_norm(att_ref[...].astype(F32), total_columns(refs[:mp]), 0, width)
    refs[mp][...] = (normed * gain_ref[...]).astype(BF)


def out_body(meta, rows_ref, weight_ref, out_ref, *scratch):
    rows = out_ref.shape[0]
    pair_sums(
        [
            (
                lambda: dot(rows_ref[:rows, :], weight_ref[...]),
                lambda: dot(rows_ref[rows:, :], weight_ref[...]),
            )
        ],
        [out_ref],
        scratch,
    )


def back_body(meta, rows_ref, weight_ref, out_ref, *scratch):
    rows = out_ref.shape[0]
    pair_sums(
        [
            (
                lambda: dot(rows_ref[:rows, :], weight_ref[...], ROWS_BY_ROWS),
                lambda: dot(rows_ref[rows:, :], weight_ref[...], ROWS_BY_ROWS),
            )
        ],
        [out_ref],
        scratch,
    )


def after_body(meta, own_ref, far_ref, text_ref, slots_ref, table_ref, gain_ref, after_ref, low_ref):
    mixed = mixed_rows(meta, text_ref, slots_ref, table_ref)
    after = mixed + (own_ref[...].astype(F32) + far_ref[...].astype(F32))
    after_ref[...] = after
    low_ref[...] = (norm_parts(after)[0] * gain_ref[...]).astype(BF)


def mixed_rows(meta, text_ref, slots_ref, table_ref):
    block = meta[PART] * pl.num_programs(0) + pl.program_id(0)
    filled = meta[BLOCK + block] >= 0
    return (
        jnp.where(filled, slots_ref[0].astype(F32), text_ref[...].astype(F32))
        + kind_of(meta, table_ref)
    )


def slot_index(blocks):
    return lambda i, m: (jnp.maximum(m[BLOCK + m[PART] * blocks + i], 0), 0, 0)


def times_rows_body(meta, *refs, count):
    pieces, weight_ref, outs = refs[:count], refs[count], refs[-count:]
    for piece, out_ref in zip(pieces, outs):
        out_ref[...] = dot(piece[...], weight_ref[...], ROWS_BY_ROWS).astype(out_ref.dtype)


def up_body(meta, a_ref, b_ref, weight_ref, dup_a, dup_b, gain_ref, *refs):
    act_ref, slope_ref, stat_ref = refs[-7:-4]
    sums = refs[-4:]
    step = pl.program_id(0)
    rows = a_ref.shape[0]

    @pl.when(step == 0)
    def _():
        for ref in sums:
            ref[...] = jnp.zeros_like(ref)

    for n, (ref, dup_ref) in enumerate(((a_ref, dup_a), (b_ref, dup_b))):
        here = slice(n * rows, (n + 1) * rows)
        pre = dot(ref[...], weight_ref[...])
        share = 0.5 + 0.5 * lax.erf(pre * (0.5**0.5))
        density = jnp.exp(pre * pre * -0.5) * ((2.0 * jnp.pi) ** -0.5)
        act = pre * share
        act_ref[here, :] = act.astype(BF)
        slope_ref[here, :] = (share + pre * density).astype(BF)
        scaled = dup_ref[...].astype(F32) * gain_ref[...]
        for ref_sum, term in zip(sums, (act, act * act, scaled, scaled * act)):
            ref_sum[here, :] += lane_sums(term)

    @pl.when(step == pl.num_programs(0) - 1)
    def _():
        rows_of = [rows_from(ref_sum[...]) for ref_sum in sums]
        row = lax.broadcasted_iota(jnp.int32, rows_of[0].shape, 0)
        total = jnp.zeros_like(rows_of[0])
        for n, value in enumerate(rows_of):
            total = jnp.where(row == n, value, total)
        stat_ref[...] = total


def spread_body(meta, act_ref, slope_ref, dup_0, dup_1, dup_2, dup_3, gain_ref, *refs, mp, width):
    stats = refs[:mp]
    pre_ref, low_ref, grad_ref = refs[mp:]
    columns = total_columns(stats)
    act = act_ref[...].astype(F32)
    normed, inv_std = stat_norm(act, columns, 0, width)
    gain = gain_ref[...]
    low_ref[...] = (normed * gain).astype(BF)
    step = pl.program_id(0) // (pl.num_programs(0) // 4)
    upstream = jnp.where(
        step < 2,
        jnp.where(step == 0, dup_0[...], dup_1[...]),
        jnp.where(step == 2, dup_2[...], dup_3[...]),
    ).astype(F32)
    first = columns[:, 2:3] / width
    mean = columns[:, 0:1] / width
    second = (columns[:, 3:4] - mean * columns[:, 2:3]) * inv_std / width
    d_act = inv_std * (upstream * gain - first - normed * second)
    pre_ref[...] = (d_act * slope_ref[...].astype(F32)).astype(BF)
    add_rows(grad_ref, upstream * normed)


def down_body(meta, low_ref, weight_ref, near_ref, far_ref, *scratch):
    rows = near_ref.shape[0]

    def term(j):
        return lambda: dot(low_ref[j * rows : (j + 1) * rows, :], weight_ref[...])

    pair_sums([(term(2), term(3)), (term(0), term(1))], [far_ref, near_ref], scratch)


def sum_body(meta, first_ref, second_ref, third_ref, out_ref):
    out_ref[...] = first_ref[...] + (second_ref[...].astype(F32) + third_ref[...].astype(F32))


def ffn_back_body(meta, own_ref, far_ref, after_ref, cot_ref, gain_ref, out_ref, low_ref, grad_ref):
    upstream = own_ref[...].astype(F32) + far_ref[...].astype(F32)
    normed, inv_std = norm_parts(after_ref[...])
    d_after = cot_ref[...].astype(F32) + norm_back(upstream, normed, inv_std, gain_ref[...])
    out_ref[...] = d_after
    low_ref[...] = d_after.astype(BF)
    add_rows(grad_ref, upstream * normed)


def add_rows(ref, values):
    total = jnp.sum(values, axis=0, keepdims=True)

    @pl.when(pl.program_id(0) == 0)
    def _():
        ref[...] = total

    @pl.when(pl.program_id(0) != 0)
    def _():
        ref[...] += total


def d_mid_body(meta, *refs, mp, width):
    pieces, weight_ref, gain_ref, att_ref = refs[:2], refs[2], refs[3], refs[4]
    stats = refs[5 : 5 + mp]
    out_ref, stat_ref, grad_ref = refs[-3:]
    rows = jnp.where(pl.program_id(0) == 0, pieces[0][...], pieces[1][...])
    d_mid = dot(rows, weight_ref[...], ROWS_BY_ROWS)
    out_ref[...] = d_mid.astype(BF)
    normed, _ = stat_norm(att_ref[...].astype(F32), total_columns(stats), 0, width)
    scaled = d_mid * gain_ref[...]
    add_rows(grad_ref, d_mid * normed)
    stat_ref[...] = two_rows(
        rows_from(lane_sums(scaled)), rows_from(lane_sums(scaled * normed))
    )


def attend_back_body(
    meta, qkv_ref, att_ref, dmid_ref, lse_ref, gain_ref, turn_ref, *refs, mp, width, block
):
    stats, more = refs[:mp], refs[mp : 2 * mp]
    out_ref, d_att, dq, dk, dv = refs[2 * mp :]
    length, wide = att_ref.shape
    columns = total_columns(stats)
    normed, inv_std = stat_norm(att_ref[...].astype(F32), columns, 0, width)
    sums = total_columns(more)
    scaled = dmid_ref[...].astype(F32) * gain_ref[...]
    d_att[...] = (
        inv_std * (scaled - sums[:, 0:1] / width - normed * (sums[:, 1:2] / width))
    ).astype(BF)

    def pair(hp, _):
        lanes, k_lanes, v_lanes = head_lanes(hp, wide)
        keys, values = qkv_ref[:, k_lanes], qkv_ref[:, v_lanes]
        lane = lax.broadcasted_iota(jnp.int32, (block, LANES), 1)
        row = lax.broadcasted_iota(jnp.int32, (block, block), 0)
        col = lax.broadcasted_iota(jnp.int32, (block, block), 1)
        dk[...] = jnp.zeros_like(dk)
        dv[...] = jnp.zeros_like(dv)
        both = d_att[:, lanes].astype(F32) * att_ref[:, lanes].astype(F32)
        side = lax.broadcasted_iota(jnp.int32, (8, LANES), 1) // HEAD
        pick_head = lax.broadcasted_iota(jnp.int32, (8, LANES), 0) == side
        inner = dot_exact(pick_head.astype(F32), both)
        for b in range(length // block):
            rows = slice(b * block, (b + 1) * block)
            end = (b + 1) * block
            query, grad = qkv_ref[rows, lanes], d_att[rows, lanes]
            d_query = jnp.zeros((block, LANES), F32)
            for h in range(2):
                keep = lane // HEAD == h
                q_one = jnp.where(keep, query, jnp.zeros_like(query))
                g_one = jnp.where(keep, grad, jnp.zeros_like(grad))
                scores = dot(keys[:end], q_one, ROWS_BY_ROWS) * 0.125
                shares = jnp.exp(scores - lse_ref[pl.ds(2 * hp + h, 1), rows])
                edge = jnp.where(col >= row, shares[b * block :], 0.0)
                shares = edge if b == 0 else jnp.concatenate([shares[: b * block], edge], axis=0)
                d_shares = dot(values[:end], g_one, ROWS_BY_ROWS)
                d_scores = (shares * (d_shares - inner[h : h + 1, rows])).astype(BF)
                dv[:end, :] += dot(shares.astype(BF), g_one)
                dk[:end, :] += dot(d_scores, q_one)
                turned = dot(d_scores, keys[:end], OVER_ROWS)
                d_query = jnp.where(keep, turned, d_query)
            dq[rows, :] = d_query
        out_ref[:, lanes] = rotated(
            dq[...] * 0.125, turn_ref[0, 0], -turn_ref[0, 1]
        ).astype(BF)
        out_ref[:, k_lanes] = rotated(
            dk[...] * 0.125, turn_ref[1, 0], -turn_ref[1, 1]
        ).astype(BF)
        out_ref[:, v_lanes] = dv[...].astype(BF)
        return 0

    lax.fori_loop(0, wide // LANES, pair, 0)


def three_dots(rows, weight_ref):
    width = weight_ref.shape[2]
    total = None
    for c in range(3):
        term = dot(rows[:, c * width : (c + 1) * width], weight_ref[c], ROWS_BY_ROWS)
        total = term if total is None else total + term
    return total


def slot_back_body(meta, *refs, slots, mp):
    pieces, weight_ref, even_ref, odd_ref, scratch = refs[:slots], refs[slots], *refs[-3:]
    rows = jnp.concatenate([p[...] for p in pieces], axis=0)
    scratch[...] = three_dots(rows, weight_ref)
    latent = pieces[0].shape[0]
    part = latent // mp
    for j in range(mp):
        for s in range(slots):
            start = pl.multiple_of(s * latent + (meta[PART] ^ j) * part, part)
            (odd_ref if j % 2 else even_ref)[j // 2, s] = scratch[pl.ds(start, part), :].astype(BF)


def row_back_body(meta, rows_ref, weight_ref, out_ref, *scratch, which):
    rows = out_ref.shape[0]
    me = lax.axis_index("mp")

    def term(j):
        at = pl.ds(pl.multiple_of(other_of(me, j) * rows, rows), rows)
        return lambda: three_dots(rows_ref[at, :], weight_ref)

    pair_sums([(term(which), term(which + 1))], [out_ref], scratch)


def slot_grad_body(meta, *refs, mp, slots, latent, images, groups):
    own_ref, far_ref, slots_ref, table_ref, gain_ref = refs[:5]
    after, (keep_ref, send_ref, grad_ref) = refs[5:-3], refs[-3:]
    part = latent // mp
    start = pl.multiple_of(meta[PART] * part, part)
    for s in range(slots):
        upstream = own_ref[s].astype(F32) + far_ref[s].astype(F32)
        mixed = slots_ref[s, pl.ds(start, part), :].astype(F32) + kind_of(meta, table_ref)
        normed, inv_std = norm_parts(mixed)
        block = meta[POS + s]
        blocks = after[0].shape[0] // latent
        rel = (block // blocks) ^ meta[PART]
        row = pl.multiple_of((block % blocks) * latent + start, part)
        d_after = after[0][pl.ds(row, part), :]
        for j in range(1, mp):
            d_after = jnp.where(rel == j, after[j][pl.ds(row, part), :], d_after)
        grad_ref[s] = (
            d_after.astype(F32) + norm_back(upstream, normed, inv_std, gain_ref[...])
        ).astype(BF)
    for k in range(groups):
        for i in range(images):
            rank = meta[RANK + (k ^ meta[GROUP]) * images + i]
            value = grad_ref[jnp.maximum(rank, 0)]
            value = jnp.where(rank >= 0, value, jnp.zeros_like(value))
            (send_ref if k % 2 else keep_ref)[k // 2, i * part : (i + 1) * part, :] = value


def in_back_body(
    meta, own_ref, far_ref, after_ref, text_ref, slots_ref, table_ref, gain_ref, out_ref, gain_grad, type_grad
):
    upstream = own_ref[...].astype(F32) + far_ref[...].astype(F32)
    normed, inv_std = norm_parts(mixed_rows(meta, text_ref, slots_ref, table_ref))
    d_mixed = after_ref[...] + norm_back(upstream, normed, inv_std, gain_ref[...])
    block = meta[PART] * pl.num_programs(0) + pl.program_id(0)
    out_ref[...] = jnp.where(meta[BLOCK + block] >= 0, 0.0, d_mixed)
    add_rows(gain_grad, upstream * normed)
    add_rows(type_grad, d_mixed)


def pool_back_body(
    meta, *refs, images, mp
):
    pieces, out_w, key_ref, value_ref, query_ref, key_w, value_w = refs[:mp], *refs[mp : mp + 6]
    kv_ref, query_grad, clip_even, clip_odd, grad_ref, scratch = refs[mp + 6 :]
    part = pieces[0].shape[1]
    for j in range(mp):
        for i in range(images):
            start = pl.multiple_of(i * part * mp + (meta[PART] ^ j) * part, part)
            grad_ref[pl.ds(start, part), :] = pieces[j][i]
    d_heads = dot(grad_ref[...], out_w[...], ROWS_BY_ROWS).astype(BF)
    patches = key_ref.shape[0] // images
    latent, wide = query_ref.shape
    for pair in range(wide // LANES):
        lanes = slice(pair * LANES, (pair + 1) * LANES)
        query = query_ref[:, lanes]
        lane = lax.broadcasted_iota(jnp.int32, query.shape, 1)
        d_query = jnp.zeros((latent, LANES), F32)
        for i in range(images):
            rows = slice(i * patches, (i + 1) * patches)
            keys, values = key_ref[rows, lanes], value_ref[rows, lanes]
            grad = d_heads[i * latent : (i + 1) * latent, lanes]
            d_keys = jnp.zeros((patches, LANES), F32)
            d_values = jnp.zeros((patches, LANES), F32)
            for h in range(2):
                keep = lane // HEAD == h
                shares = pool_shares_of(query, keys, h)
                g_one = jnp.where(keep, grad, jnp.zeros_like(grad))
                q_one = jnp.where(keep, query, jnp.zeros_like(query))
                d_shares = dot(g_one, values, ROWS_BY_ROWS)
                inner = jnp.sum(shares * d_shares, axis=-1, keepdims=True)
                d_scores = (shares * (d_shares - inner)).astype(BF)
                d_query += jnp.where(keep, dot(d_scores, keys), 0.0)
                d_keys += dot(d_scores, q_one, OVER_ROWS)
                d_values += dot(shares.astype(BF), g_one, OVER_ROWS)
            kv_ref[rows, lanes] = (d_keys * 0.125).astype(BF)
            kv_ref[rows, slice(wide + pair * LANES, wide + (pair + 1) * LANES)] = d_values.astype(BF)
        query_grad[:, lanes] = d_query * 0.125
    scratch[...] = dot(kv_ref[:, :wide], key_w[...], ROWS_BY_ROWS) + dot(
        kv_ref[:, wide:], value_w[...], ROWS_BY_ROWS
    )
    piece = patches // mp
    for j in range(mp):
        for i in range(images):
            start = pl.multiple_of(i * patches + (meta[PART] ^ j) * piece, piece)
            (clip_odd if j % 2 else clip_even)[j // 2, i] = scratch[
                pl.ds(start, piece), :
            ].astype(BF)


def weight_body(meta, *refs, lefts, rights, before, has_got, split):
    left, right = refs[:lefts], refs[lefts : lefts + rights]
    rest = refs[lefts + rights :]
    depth = sum(r.shape[0] for r in left)
    total = None
    step = depth // max(lefts, rights)
    for start in range(0, depth, step):
        l_ref, l_at = find(left, start)
        r_ref, r_at = find(right, start)
        term = dot(l_ref[l_at : l_at + step, :], r_ref[r_at : r_at + step, :], OVER_ROWS)
        total = term if total is None else total + term
    if split:
        wide = total.shape[1] // 2
        total = jnp.concatenate([total[:, :wide], total[:, wide:]], axis=0)
    if not has_got:
        rest[-1][0] = total.astype(BF)
        return
    even, odd = rest[-2:]
    total = (total + rest[0][0].astype(F32)).astype(BF)
    step = pl.program_id(0)

    @pl.when(step % 2 == 0)
    def _():
        even[0] = total

    @pl.when(step % 2 == 1)
    def _():
        odd[0] = total


def find(refs, start):
    for ref in refs:
        if start < ref.shape[0]:
            return ref, start
        start -= ref.shape[0]
    return None


def add_body(meta, keep_ref, got_ref, keep_out, send_out):
    keep_out[0] = (keep_ref[0].astype(F32) + got_ref[0].astype(F32)).astype(BF)
    send_out[0] = (keep_ref[1].astype(F32) + got_ref[1].astype(F32)).astype(BF)


def flat_body(meta, kinds, gain_in, gain_ffn, mid_near, mid_far, gain_ff, query_ref, flat_ref, rows_ref):
    rows_ref[...] = jnp.zeros_like(rows_ref)
    line = 0
    lines = [jnp.where(meta[KIND] == c, kinds[...], 0.0) for c in range(3)]
    lines += [gain_in[...], gain_ffn[...], mid_near[...] + mid_far[...], gain_ff[...]]
    for value in lines:
        for start in range(0, value.shape[1], LANES):
            rows_ref[line : line + 1, :] = value[:, start : start + LANES]
            line += 1
    latent, wide = query_ref.shape
    line = rows_ref.shape[0] - latent * wide // LANES
    for start in range(0, wide, LANES):
        rows_ref[line : line + latent, :] = query_ref[:, start : start + LANES]
        line += latent
    flat_ref[...] = rows_ref[...].astype(BF)


def last_body(meta, keep_ref, got_ref, out_ref):
    out_ref[...] = (keep_ref[...].astype(F32) + got_ref[...].astype(F32)).astype(out_ref.dtype)


def plus(meta, first, second, dtype):
    shape = first.shape
    steps = 2 if shape[-2] % 32 == 0 and len(shape) == 2 else 1
    block = (shape[-2] // steps,) + shape[-1:]
    if len(shape) == 3:
        block = shape
    index = lambda i, m: (i,) + (0,) * (len(shape) - 1)
    return call(
        last_body,
        meta,
        (steps,),
        [(first, block, index), (second, block, index)],
        [(shape, dtype, block, index)],
    )[0]


def split_sum(meta, keep, got):
    count, *dims = keep.shape
    pair, one = (2,) + tuple(dims), (1,) + tuple(dims)
    at = lambda i, m: (i, 0, 0)
    return call(
        add_body,
        meta,
        (count // 2,),
        [(keep, pair, at), (got, pair, at)],
        [((count // 2,) + tuple(dims), BF, one, at)] * 2,
    )


def stack_body(meta, first_ref, second_ref, out_ref):
    out_ref[:, 0] = first_ref[...]
    out_ref[:, 1] = second_ref[...]


class GatherDp:
    def __init__(self, meta, values):
        self.meta, self.values = meta, values[None]
        self.pending = list(reversed(bits_of(lax.axis_size("dp"))))
        self.got = swap(self.values, "dp", self.pending.pop(0))

    def step(self):
        count, *dims = self.values.shape
        stacked = call(
            stack_body,
            self.meta,
            (1,),
            [(self.values,), (self.got,)],
            [((count, 2) + tuple(dims), self.values.dtype, None, None)],
        )[0]
        self.values = stacked.reshape((2 * count,) + tuple(dims))
        if self.pending:
            self.got = swap(self.values, "dp", self.pending.pop(0))

    def end(self):
        while self.pending:
            self.step()
        self.step()
        return self.values


class WeightGrads:
    def __init__(self, meta, members, shape, first=1, cost=1):
        self.meta, self.members, self.shape = meta, members, shape
        self.size = lax.axis_size("dp")
        bits = bits_of(self.size)
        widths = [left[0].shape[1] // self.size for left, *_ in members]
        self.plain = any(w % LANES for w in widths) or self.size < 8
        self.first, self.cost = first, cost
        self.order = [first] + [b for b in bits if b != first]
        self.pending = list(self.order)

    def run(self, side, got):
        half, first = self.size // 2, self.first
        before = None
        for left, right, split, at in self.members:
            part = left[0].shape[1] // self.size
            inner = right[0].shape[1]
            block = (1, 2 * part, inner // 2) if split else (1, part, inner)
            place = lambda i, m, at=at: (i,) + at
            pair_place = lambda i, m, at=at: (i // 2,) + at
            column = lambda i, m: (
                0,
                m[GROUP] ^ ((i // first) * 2 * first + side * first + i % first),
            )
            ins = [(a, (a.shape[0], part), column) for a in left] + [(a,) for a in right]
            if got is not None:
                ins.append((got, block, place))
                outs = [((half // 2,) + self.shape, BF, block, pair_place)] * 2
            else:
                outs = [((half,) + self.shape, BF, block, place)]
            aliases = {}
            if before is not None:
                aliases = {len(ins) + 1 + n: n for n in range(len(outs))}
                ins += [(a, None) for a in before]
            before = call(
                functools.partial(
                    weight_body,
                    lefts=len(left),
                    rights=len(right),
                    before=before is not None,
                    has_got=got is not None,
                    split=split,
                ),
                self.meta,
                (half,),
                ins,
                outs,
                aliases=aliases,
                cost=self.cost,
            )
        return before

    def start(self):
        if not self.plain:
            self.got = swap(self.run(1, None)[0], "dp", self.pending.pop(0))

    def step(self):
        if self.plain:
            return
        if len(self.pending) == len(self.order) - 1:
            self.keep, send = self.run(0, self.got)
        else:
            self.keep, send = split_sum(self.meta, self.keep, self.got)
        self.got = swap(send, "dp", self.pending.pop(0))

    def finish(self):
        if not self.plain:
            while self.pending:
                self.step()
            self.total = plus(self.meta, self.keep[0], self.got[0], F32)

    def end(self):
        me = lax.axis_index("dp")
        results = []
        if self.plain:
            for left, right, split, at in self.members:
                whole = dot(jnp.concatenate(left), jnp.concatenate(right), OVER_ROWS).astype(BF)
                whole = whole.reshape(self.size, -1, whole.shape[1])
                whole = pick(whole, [me ^ k for k in range(self.size)])
                results.append(scatter_dp(whole, bits_of(self.size), F32))
            return results
        for left, right, split, at in self.members:
            part = left[0].shape[1] // self.size
            inner = right[0].shape[1]
            high, wide = (2 * part, inner // 2) if split else (part, inner)
            cut = (slice(at[0] * high, (at[0] + 1) * high), slice(at[1] * wide, (at[1] + 1) * wide))
            value = self.total[cut]
            if split:
                value = jnp.concatenate([value[:part], value[part:]], axis=1)
            results.append(value)
        return results


def shards(
    text_embed,
    clip_feats,
    type_table,
    gain_attn_in,
    qkv_weight,
    gain_attn_out,
    out_weight,
    gain_ffn_in,
    up_weight,
    gain_ffn_out,
    down_weight,
    res_query,
    res_key,
    res_value,
    res_out,
    cotangent,
    owner_count,
    image_seq,
    slot_block,
    seq_kind,
):
    mp = lax.axis_size("mp")
    dp = lax.axis_size("dp")
    rows, width = text_embed.shape
    length = rows * mp
    latent = res_query.shape[0]
    slots = slot_block.shape[1]
    images, patches, clip_width = clip_feats.shape
    wide = qkv_weight.shape[2]
    heads = wide // HEAD
    ff = up_weight.shape[1]
    ff_all = ff * mp
    here = rows // latent
    part = latent // mp
    tile = 512

    Order.mark, Order.channel = None, 0
    meta = make_meta(owner_count, image_seq, slot_block, seq_kind, images)
    table = type_table.astype(F32)
    gain_in, gain_out = gain_attn_in[None], gain_attn_out[None]
    gain_ffn, gain_ff = gain_ffn_in[None], gain_ffn_out[None]
    row_block = lambda i, m: (i, 0)
    few = (latent, width)
    weight = jnp.moveaxis(qkv_weight, 1, 0)
    turn = turn_tables(length)

    clip = clip_feats.reshape(images * patches, clip_width)
    key_proj, value_proj, pool_out = call(
        functools.partial(pool_body, images=images),
        meta,
        (1,),
        [(clip,), (res_key,), (res_value,), (res_query,)],
        [
            ((images * patches, wide), BF, None, None),
            ((images * patches, wide), BF, None, None),
            ((images * latent, wide), BF, None, None),
        ],
    )
    gathering = GatherDp(meta, pool_out)

    text_in = call(
        text_body,
        meta,
        (4,),
        [(text_embed, (rows // 4, width), row_block), (table,), (gain_in,)],
        [((rows, width), BF, (rows // 4, width), row_block)],
    )[0]
    text_pieces = gather_start(text_in)
    gathering.step()
    state = project(meta, text_pieces[:2], weight, turn, None, 0)
    gathering.step()
    gather_end(meta, text_pieces)
    state = project(meta, text_pieces[2:], weight, turn, state, 2)

    def d_up_half(which):
        return call(
            functools.partial(times_rows_body, count=2),
            meta,
            (ff // tile,),
            [(cot_pieces[which + n],) for n in range(2)]
            + [(down_weight, (tile, width), row_block)],
            [((rows, ff), BF, (rows, tile), lambda i, m: (0, i))] * 2,
        )

    pool_rows = gathering.end().reshape(dp * images * latent, wide)
    slot_terms = call(
        functools.partial(pooled_body, slots=slots, mp=mp),
        meta,
        (1,),
        [
            (pool_rows, (latent, wide), lambda i, m, s=s: (m[SOURCE + s], 0))
            for s in range(slots)
        ]
        + [(res_out,)],
        [((mp // 2, slots, part, width), BF, None, None)] * 2,
        scratch=[pltpu.VMEM((slots * latent, width), F32)],
    )
    slot_own, slot_far = scatter_now(meta, *slot_terms)
    slot_pieces = gather_now(meta, add_low(slot_own, slot_far))

    cot = call(
        copy_body,
        meta,
        (2,),
        [(cotangent, (rows // 2, width), row_block)],
        [((rows, width), BF, (rows // 2, width), row_block)],
    )[0]
    cot_pieces = gather_start(cot)

    at_slot = lambda i, m: (m[POS + jnp.maximum(i - 3, 0)], 0)
    state = call(
        functools.partial(slot_body, mp=mp, slots=slots, latent=latent),
        meta,
        (3 + slots,),
        [(p,) for p in slot_pieces]
        + [(table,), (gain_in,)]
        + [(weight, (1, width, wide), lambda i, m: (jnp.minimum(i, 2), 0, 0))]
        + [(turn, (3, 2, latent, LANES), lambda i, m: (0, 0) + at_slot(i, m))]
        + [(a, (latent, a.shape[1]), at_slot) for a in state],
        [(a.shape, BF, (latent, a.shape[1]), at_slot) for a in state]
        + [((slots, latent, width), BF, None, None)],
        scratch=[
            pltpu.VMEM((slots, latent, width), F32),
            pltpu.VMEM((3, slots, latent, wide), F32),
            pltpu.VMEM((slots, latent, width), BF),
        ],
        aliases={mp + 5 + n: n for n in range(2)},
    )
    qkv, in_full, slot_rows = state

    att, lse, att_stats = call(
        functools.partial(attend_body, block=rows),
        meta,
        (1,),
        [(qkv,)],
        [
            ((length, wide), BF, None, None),
            ((heads, length), F32, None, None),
            ((8, length), F32, None, None),
        ],
        scratch=[pltpu.VMEM((length, LANES), F32)] * 3,
    )
    att_stats = spread_stats(meta, att_stats)

    mids = call(
        functools.partial(mid_body, mp=mp, width=width),
        meta,
        (mp,),
        [(att, (rows, wide), lambda j, m: (m[PART] ^ j, 0)), (gain_out,)]
        + [(s, (8, rows), lambda j, m: (0, m[PART] ^ j)) for s in att_stats],
        [((length, wide), BF, (rows, wide), lambda j, m: (j, 0))],
    )[0]
    steps = width // tile

    def summed(body, array, weights, which):
        return call(
            body,
            meta,
            (steps,),
            [(array, (2 * rows, array.shape[1]), lambda i, m: (which // 2, 0)), weights],
            [((rows, width), BF, None, None)],
            scratch=pair_scratch(1, steps, rows, tile),
            remote=True,
        )[0]

    out_w = (out_weight, (wide, tile), lambda i, m: (0, i))
    out_far = swap(summed(out_body, mids, out_w, 2), "mp", 2)
    out_terms = [summed(out_body, mids, out_w, 0), out_far]
    d_up_near = d_up_half(0)
    gather_end(meta, cot_pieces)
    d_up = d_up_near + d_up_half(2)
    after_attn, ffn_in = call(
        after_body,
        meta,
        (here,),
        [(t, few, row_block) for t in out_terms]
        + [(text_embed, few, row_block), (slot_rows, (1,) + few, slot_index(here))]
        + [(table,), (gain_ffn,)],
        [((rows, width), F32, few, row_block), ((rows, width), BF, few, row_block)],
    )
    ffn_pieces = gather_start(ffn_in)

    def up_half(which, before):
        lanes_of = lambda i, m: (0, i)
        half = lambda i, m: (which // 2, i)
        ins = [(ffn_pieces[which],), (ffn_pieces[which + 1],)]
        ins += [(up_weight, (width, tile), lanes_of)]
        ins += [(d_up[which + n], (rows, tile), lanes_of) for n in range(2)]
        ins += [(gain_ff, (1, tile), lanes_of)]
        aliases = {}
        if before is not None:
            aliases = {len(ins) + 1 + n: n for n in range(3)}
            ins += [(a, None) for a in before]
        return call(
            up_body,
            meta,
            (ff // tile,),
            ins,
            [
                ((length, ff), BF, (2 * rows, tile), half),
                ((length, ff), BF, (2 * rows, tile), half),
                ((8, length), F32, (8, 2 * rows), lambda i, m: (0, which // 2)),
            ],
            scratch=[pltpu.VMEM((2 * rows, LANES), F32)] * 4,
            aliases=aliases,
        )

    state = up_half(0, None)
    gather_end(meta, ffn_pieces)
    act, slope, ff_stats = up_half(2, state)
    ff_stats = spread_stats(meta, ff_stats)
    cut = rows // 2
    fine = lambda i, m: (i, 0)
    pre, low, gain_ff_local = call(
        functools.partial(spread_body, mp=mp, width=ff_all),
        meta,
        (length // cut,),
        [(act, (cut, ff), fine), (slope, (cut, ff), fine)]
        + [
            (d_up[j], (cut, ff), lambda i, m, j=j: (jnp.clip(i - 2 * j, 0, 1), 0))
            for j in range(mp)
        ]
        + [(gain_ff,)]
        + [
            (s, (8, cut), lambda i, m, b=b: (0, (((i // 2) ^ b) * 2) + i % 2))
            for b, s in enumerate(ff_stats)
        ],
        [((length, ff), BF, (cut, ff), fine)] * 2 + [((1, ff), F32, None, None)],
    )

    up_w = (up_weight, (tile, ff), row_block)
    down_grad = WeightGrads(meta, [(cot_pieces, [low], False, (0, 0))], (width // dp, ff))
    up_grad = WeightGrads(meta, [(ffn_pieces, [pre], False, (0, 0))], (width // dp, ff), 2)
    down_grad.start()
    up_grad.start()
    back_far = swap(summed(back_body, pre, up_w, 2), "mp", 2)
    ffn_terms = [summed(back_body, pre, up_w, 0), back_far]
    d_after, d_after_low, gain_ffn_local = call(
        ffn_back_body,
        meta,
        (here,),
        [(t, few, row_block) for t in ffn_terms]
        + [(after_attn, few, row_block), (cotangent, few, row_block), (gain_ffn,)],
        [
            ((rows, width), F32, few, row_block),
            ((rows, width), BF, few, row_block),
            ((1, width), F32, None, None),
        ],
    )
    after_pieces = gather_start(d_after_low)

    def d_mid_half(which, before):
        block = lambda i, m: (m[PART] ^ (which + i), 0)
        lane_block = lambda i, m: (0, m[PART] ^ (which + i))
        aliases = {}
        ins = [(after_pieces[which],), (after_pieces[which + 1],), (out_weight,), (gain_out,)]
        ins += [(att, (rows, wide), block)] + [(s, (8, rows), lane_block) for s in att_stats]
        if before is not None:
            aliases = {len(ins) + 1 + n: n for n in range(2)}
            ins += [(a, None) for a in before]
        return call(
            functools.partial(d_mid_body, mp=mp, width=width),
            meta,
            (2,),
            ins,
            [
                ((length, wide), BF, (rows, wide), block),
                ((8, length), F32, (8, rows), lane_block),
                ((1, wide), F32, None, None),
            ],
            aliases=aliases,
        )

    d_mid, mid_stats, gain_mid_near = d_mid_half(0, None)
    down_near, down_far = call(
        down_body,
        meta,
        (steps,),
        [(low,), (down_weight, (ff, tile), lambda i, m: (0, i))],
        [((rows, width), BF, None, None)] * 2,
        scratch=pair_scratch(2, steps, rows, tile),
        remote=True,
    )
    gather_end(meta, after_pieces)
    d_mid, mid_stats, gain_mid_far = d_mid_half(2, (d_mid, mid_stats))
    mid_stats = spread_stats(meta, mid_stats)
    down_far = swap(
        call(
            copy_body,
            meta,
            (2,),
            [(down_far, (rows // 2, width), row_block)],
            [((rows, width), BF, (rows // 2, width), row_block)],
        )[0],
        "mp",
        2,
    )
    out_grad = WeightGrads(meta, [(after_pieces, [mids], False, (0, 0))], (width // dp, wide))
    out_grad.start()
    down_grad.step()
    d_qkv = call(
        functools.partial(attend_back_body, mp=mp, width=width, block=rows),
        meta,
        (1,),
        [(a,) for a in (qkv, att, d_mid, lse, gain_out, turn)]
        + [(s,) for s in att_stats]
        + [(s,) for s in mid_stats],
        [((length, 3 * wide), BF, None, None)],
        scratch=[pltpu.VMEM((length, wide), BF)] + [pltpu.VMEM((length, LANES), F32)] * 3,
    )[0]

    slot_terms = call(
        functools.partial(slot_back_body, slots=slots, mp=mp),
        meta,
        (1,),
        [
            (d_qkv, (latent, 3 * wide), lambda i, m, s=s: (m[POS + s], 0))
            for s in range(slots)
        ]
        + [(weight,)],
        [((mp // 2, slots, part, width), BF, None, None)] * 2,
        scratch=[pltpu.VMEM((slots * latent, width), F32)],
    )
    slot_terms = scatter_now(meta, *slot_terms)
    image_keep, image_send, _ = call(
        functools.partial(
            slot_grad_body, mp=mp, slots=slots, latent=latent, images=images, groups=dp
        ),
        meta,
        (1,),
        [(t,) for t in slot_terms]
        + [(slot_rows,), (table,), (gain_in,)]
        + [(a,) for a in after_pieces],
        [((dp // 2, images * part, width), BF, None, None)] * 2
        + [((slots, part, width), BF, None, None)],
    )
    image_got = exchange(meta, (image_send, "dp", 1))[0]
    in_grad = WeightGrads(meta, [([in_full], [d_qkv], False, (0, 0))], (width // dp, 3 * wide))
    def row_terms(which):
        return call(
            functools.partial(row_back_body, which=which),
            meta,
            (steps,),
            [(d_qkv,), (weight, (3, tile, wide), lambda i, m: (0, i, 0))],
            [((rows, width), BF, None, None)],
            scratch=pair_scratch(1, steps, rows, tile),
            remote=True,
        )[0]

    for bit in bits_of(dp)[1:]:
        image_keep, image_send = split_sum(meta, image_keep, image_got)
        image_got = exchange(meta, (image_send, "dp", bit))[0]
        if bit == 2:
            layer_out = call(
                sum_body,
                meta,
                (here,),
                [(after_attn, few, row_block), (down_near, few, row_block), (down_far, few, row_block)],
                [((rows, width), F32, few, row_block)],
            )[0]
            out_grad.step()
            up_grad.step()
            in_grad.start()
            in_far = swap(row_terms(2), "mp", 2)
    down_grad.step()
    out_grad.step()
    owned = plus(meta, image_keep, image_got, BF).reshape(images, part, width)
    owned_pieces = gather_now(meta, owned)
    d_kv, query_local, clip_even, clip_odd, pool_grad = call(
        functools.partial(pool_back_body, images=images, mp=mp),
        meta,
        (1,),
        [(a,) for a in owned_pieces]
        + [(a,) for a in (res_out, key_proj, value_proj, res_query, res_key, res_value)],
        [
            ((images * patches, 2 * wide), BF, None, None),
            ((latent, wide), F32, None, None),
            ((mp // 2, images, patches // mp, clip_width), BF, None, None),
            ((mp // 2, images, patches // mp, clip_width), BF, None, None),
            ((images * latent, width), BF, None, None),
        ],
        scratch=[pltpu.VMEM((images * patches, clip_width), F32)],
    )
    pool_grads = WeightGrads(
        meta,
        [
            ([pool_grad], [pool_out], False, (0, 0)),
            ([clip], [d_kv], True, (1, 0)),
        ],
        (width // dp + 2 * (clip_width // dp), wide),
    )
    down_grad.finish()
    in_grad.step()
    pool_grads.start()
    in_terms = [row_terms(0), in_far]
    text_grad, gain_in_local, type_local = call(
        in_back_body,
        meta,
        (here,),
        [(t, few, row_block) for t in in_terms]
        + [(d_after, few, row_block), (text_embed, few, row_block)]
        + [(slot_rows, (1,) + few, slot_index(here)), (table,), (gain_in,)],
        [
            ((rows, width), F32, few, row_block),
            ((1, width), F32, None, None),
            ((1, width), F32, None, None),
        ],
    )
    down_grad.finish()
    hops = bits_of(dp)[1:] + [1]
    small = (type_local, gain_in_local, gain_ffn_local, gain_mid_near, gain_mid_far, gain_ff_local)
    sizes = 5 * width + wide + ff
    lines = -(-sizes // (16 * LANES)) * 16 + latent * wide // LANES
    flat = call(
        flat_body,
        meta,
        (1,),
        [(x,) for x in small] + [(query_local,)],
        [((lines, LANES), BF, None, None)],
        scratch=[pltpu.VMEM((lines, LANES), F32)],
    )[0]
    for n, bit in enumerate(hops):
        got = swap(flat, "dp", bit)
        if n == 0:
            up_grad.step()
            clip_even = add_low(clip_even, exchange(meta, (clip_odd, "mp", 1))[0])
            clip_far = exchange(meta, (clip_even[1], "mp", 2))[0]
        elif n == len(hops) - 2:
            pool_grads.step()
            in_grad.step()
        elif n == len(hops) - 1:
            up_grad.finish()
            pool_grads.step()
        flat = plus(meta, flat, got, BF)
    flat_far, flat_near = exchange(meta, (flat, "mp", 2), (flat, "mp", 1))
    flat_last = exchange(meta, (flat_far, "mp", 1))[0]
    out_grad.finish()
    pool_grads.finish()
    in_grad.finish()
    clip_grad = clip_even[0].astype(F32) + clip_far.astype(F32)
    flat = by_mp(jnp.stack([flat, flat_near, flat_far, flat_last])).astype(F32)
    edge = flat.shape[1] - latent * wide // LANES
    parts = flat[:, :edge].reshape(mp, -1)
    sums = jnp.sum(parts[:, : 5 * width].reshape(mp, 5, width), axis=0)
    parts = parts[:, 5 * width :]
    query_grad = flat[:, edge:].reshape(mp, wide // LANES, latent, LANES).swapaxes(1, 2)
    query_grad = jnp.swapaxes(query_grad.reshape(mp, latent, wide), 0, 1)
    res_out_grad, kv_grad = pool_grads.end()
    qkv_grad, out_grad = in_grad.end()[0], out_grad.end()[0]
    return (
        layer_out,
        text_grad,
        clip_grad,
        sums[:3],
        sums[3],
        qkv_grad.reshape(-1, 3, wide),
        parts[:, :wide].reshape(-1),
        out_grad.T,
        sums[4],
        up_grad.end()[0],
        parts[:, wide : wide + ff].reshape(-1),
        down_grad.end()[0].T,
        query_grad.reshape(latent, width),
        kv_grad[:, :wide],
        kv_grad[:, wide:],
        res_out_grad.T,
    )


def solution(mesh):
    return jax.shard_map(
        shards,
        mesh=mesh,
        in_specs=(
            P(("dp", "mp"), None),
            P("dp", None, None),
            P(),
            P(),
            P(None, None, "mp"),
            P("mp"),
            P("mp", None),
            P(),
            P(None, "mp"),
            P("mp"),
            P("mp", None),
            P(None, "mp"),
            P(None, "mp"),
            P(None, "mp"),
            P("mp", None),
            P(("dp", "mp"), None),
            P(),
            P(),
            P(),
            P(),
        ),
        out_specs=(
            P(("dp", "mp"), None),
            P(("dp", "mp"), None),
            P("dp", "mp", None),
            P(),
            P(),
            P("dp", None, "mp"),
            P(),
            P("mp", "dp"),
            P(),
            P("dp", "mp"),
            P(),
            P("mp", "dp"),
            P(),
            P("dp", "mp"),
            P("dp", "mp"),
            P("mp", "dp"),
        ),
        check_vma=False,
    )
```

```python
import functools

import jax
import jax.numpy as jnp
from jax import lax
from jax.experimental import pallas as pl
from jax.experimental.pallas import tpu as pltpu
from jax.sharding import PartitionSpec as P

HEAD = 64
LANES = 128
EPS = 1e-05
NEG = -1e30
XPOS_BASE = 512.0
BF = jnp.bfloat16
F32 = jnp.float32
ROWS_BY_ROWS = (((1,), (1,)), ((), ()))
PLAIN = (((1,), (0,)), ((), ()))
OVER_ROWS = (((0,), (0,)), ((), ()))
KIND, PART, GROUP, REAL, POS, SOURCE, BLOCK, RANK = 0, 1, 2, 4, 8, 12, 16, 32
VMEM_BYTES = 14 * 1024 * 1024


def dot(left, right, form=PLAIN):
    return lax.dot_general(left, right, form, preferred_element_type=F32)


def dot_exact(left, right, form=ROWS_BY_ROWS):
    return lax.dot_general(
        left, right, form, precision=lax.Precision.HIGHEST, preferred_element_type=F32
    )


def swap(values, axis, bit):
    size = lax.axis_size(axis)
    return lax.ppermute(values, axis, [(i, i ^ bit) for i in range(size)])


def bits_of(size):
    return [1 << i for i in range(size.bit_length() - 1)]


def gather_start(values):
    far, near = swap(values, "mp", 2), swap(values, "mp", 1)
    return [values, near, far]


def gather_end(meta, pieces):
    pieces.append(exchange(meta, (pieces[2], "mp", 1))[0])


def add_low(first, second):
    return (first.astype(F32) + second.astype(F32)).astype(BF)


def scatter_pairs(even, odd):
    near = add_low(even, swap(odd, "mp", 1))
    return near[0], swap(near[1], "mp", 2), near


def sum_pairs(even, odd):
    own, far, _ = scatter_pairs(even, odd)
    return own.astype(F32) + far.astype(F32)


def pick(values, indices):
    return jnp.stack([lax.dynamic_index_in_dim(values, i, 0, keepdims=False) for i in indices])


def by_mp(values):
    me = lax.axis_index("mp")
    return pick(values, [me ^ j for j in range(lax.axis_size("mp"))])


def halve(values, axis):
    return (
        lax.index_in_dim(values, 0, axis, keepdims=False),
        lax.index_in_dim(values, 1, axis, keepdims=False),
    )


def scatter_dp(values, bits, last):
    for bit in bits:
        values = values.reshape((-1, 2) + values.shape[1:])
        keep, send = halve(values, 1)
        got = swap(send, "dp", bit)
        total = keep.astype(F32) + got.astype(F32)
        values = total.astype(last if bit == bits[-1] else BF)
    return values[0]


class Order:
    mark = None
    channel = 0


def call(body, meta, grid, ins, outs, scratch=(), aliases=None, remote=False, after=(), cost=1, room=VMEM_BYTES):
    arrays, specs = [], []
    for item in ins:
        arrays.append(item[0])
        if len(item) == 1:
            dims = item[0].ndim
            specs.append(
                pl.BlockSpec(
                    item[0].shape,
                    lambda *_, dims=dims: (0,) * dims,
                    pipeline_mode=pl.Buffered(1),
                )
            )
        elif item[1] is None:
            specs.append(pl.BlockSpec(memory_space=pl.ANY))
        else:
            specs.append(pl.BlockSpec(item[1], item[2]))
    shapes, out_specs = [], []
    for shape, dtype, block, index in list(outs) + [((8, LANES), F32, None, None)]:
        shapes.append(jax.ShapeDtypeStruct(shape, dtype))
        if index == "any":
            out_specs.append(pl.BlockSpec(memory_space=pl.ANY))
        elif block is None:
            dims = len(shape)
            out_specs.append(pl.BlockSpec(shape, lambda *_, dims=dims: (0,) * dims))
        else:
            out_specs.append(pl.BlockSpec(block, index))
    count, after = len(ins), list(after)
    if Order.mark is not None:
        after.append(Order.mark)
    specs += [pl.BlockSpec(memory_space=pl.ANY)] * len(after)

    params = pltpu.CompilerParams(vmem_limit_bytes=room)
    if remote:
        Order.channel += 1
        params = pltpu.CompilerParams(
            vmem_limit_bytes=room, collective_id=Order.channel, has_side_effects=True
        )

    def marked(meta_ref, *refs):
        refs = refs[:count] + refs[count + len(after) :]
        place = count + len(outs)
        refs[place][...] = jnp.zeros((8, LANES), F32)
        body(meta_ref, *refs[:place], *refs[place + 1 :])

    result = pl.pallas_call(
        marked,
        out_shape=shapes,
        grid_spec=pltpu.PrefetchScalarGridSpec(
            num_scalar_prefetch=1,
            grid=grid,
            in_specs=specs,
            out_specs=out_specs,
            scratch_shapes=list(scratch),
        ),
        input_output_aliases=aliases or {},
        compiler_params=params,
        cost_estimate=pl.CostEstimate(
            flops=cost * 1000000, bytes_accessed=1024, transcendentals=0
        ),
        name=getattr(body, "func", body).__name__,
    )(meta, *arrays, *after)
    Order.mark = result[-1]
    return result[:-1]


def norm_parts(values):
    width = values.shape[-1]
    mean = jnp.sum(values, axis=-1, keepdims=True) / width
    square = jnp.sum(values * values, axis=-1, keepdims=True) / width
    inv_std = lax.rsqrt(square - mean * mean + EPS)
    return (values - mean) * inv_std, inv_std


def norm_back(upstream, normed, inv_std, gain):
    width = upstream.shape[-1]
    scaled = upstream * gain
    first = jnp.sum(scaled, axis=-1, keepdims=True) / width
    second = jnp.sum(scaled * normed, axis=-1, keepdims=True) / width
    return inv_std * (scaled - first - normed * second)


def columns_of(rows):
    count, length = rows.shape
    full = jnp.concatenate([rows, jnp.zeros((LANES - count, length), F32)], axis=0)
    return full.T


def lane_sums(values):
    total = values[:, :LANES]
    for start in range(LANES, values.shape[1], LANES):
        total = total + values[:, start : start + LANES]
    return total


def rows_from(partials):
    return dot_exact(jnp.ones((8, LANES), F32), partials)


def two_rows(first, second):
    row = lax.broadcasted_iota(jnp.int32, first.shape, 0)
    return jnp.where(row == 0, first, jnp.where(row == 1, second, 0.0))


def meta_body(count_ref, seq_ref, slot_ref, kind_ref, me_ref, out_ref, *, image_local, slots, images):
    me_m, me_d = me_ref[0], me_ref[1]

    def clear(i, _):
        out_ref[i] = 0
        return 0

    lax.fori_loop(0, BLOCK, clear, 0)

    def absent(i, _):
        out_ref[BLOCK + i] = -1
        return 0

    lax.fori_loop(0, RANK - BLOCK + images, absent, 0)
    out_ref[KIND] = kind_ref[me_d]
    out_ref[PART] = me_m
    out_ref[GROUP] = me_d
    for s in range(slots):
        out_ref[POS + s] = slot_ref[me_d, s]

    def one(i, found):
        owner = i // image_local
        inside = i - owner * image_local
        here = jnp.logical_and(inside < count_ref[owner], seq_ref[i] == me_d)
        rank = jnp.minimum(found, slots - 1)

        @pl.when(here)
        def _():
            out_ref[REAL + rank] = 1
            out_ref[SOURCE + rank] = (owner ^ me_d) * image_local + inside
            out_ref[BLOCK + slot_ref[me_d, rank]] = rank
            out_ref[RANK + i] = rank

        return found + here.astype(jnp.int32)

    lax.fori_loop(0, images, one, jnp.int32(0))


def make_meta(owner_count, image_seq, slot_block, seq_kind, image_local):
    me = jnp.stack([lax.axis_index("mp"), lax.axis_index("dp")]).astype(jnp.int32)
    images = image_seq.shape[0]
    smem = pl.BlockSpec(memory_space=pltpu.SMEM)
    return pl.pallas_call(
        functools.partial(
            meta_body, image_local=image_local, slots=slot_block.shape[1], images=images
        ),
        out_shape=jax.ShapeDtypeStruct((RANK + images,), jnp.int32),
        in_specs=[smem] * 5,
        out_specs=smem,
    )(owner_count, image_seq, slot_block, seq_kind, me)


def other_of(me, j):
    return [me, me + 1 - 2 * (me % 2), (me + 2) % 4, 3 - me][j]


def pair_sums(terms, out_refs, scratch):
    sent, came, kept, send_sem, recv_sem = scratch
    step, steps = pl.program_id(0), pl.num_programs(0)
    partner = {"mp": other_of(lax.axis_index("mp"), 1)}

    @pl.when(step == 0)
    def _():
        barrier = pltpu.get_barrier_semaphore()
        pl.semaphore_signal(barrier, inc=1, device_id=partner)
        pl.semaphore_wait(barrier, 1)

    def move(n, place):
        return pltpu.make_async_remote_copy(
            src_ref=sent.at[n, place],
            dst_ref=came.at[n, place],
            send_sem=send_sem.at[n, place],
            recv_sem=recv_sem.at[n, place],
            device_id=partner,
        )

    for n, (mine, theirs) in enumerate(terms):
        sent[n, step] = theirs().astype(BF)
        move(n, step).start()
        kept[n, step] = mine()

    @pl.when(step == steps - 1)
    def _():
        tile = sent.shape[-1]
        for n, out_ref in enumerate(out_refs):
            for place in range(sent.shape[1]):
                move(n, place).wait()
                total = kept[n, place] + came[n, place].astype(F32)
                out_ref[:, place * tile : (place + 1) * tile] = total.astype(BF)


def flipped(me, bit):
    return me + bit * (1 - 2 * ((me // bit) % 2))


def exchange(meta, *items):
    places = sorted({(axis, bit) for _, axis, bit in items})
    count = len(items)

    def body(meta_ref, *refs):
        sources, targets, (send_sem, recv_sem) = refs[:count], refs[count : 2 * count], refs[-2:]

        def partner(axis, bit):
            me = lax.axis_index(axis)
            for one in bits_of(lax.axis_size(axis)):
                if bit & one:
                    me = flipped(me, one)
            return {axis: me}

        barrier = pltpu.get_barrier_semaphore()
        for axis, bit in places:
            pl.semaphore_signal(barrier, inc=1, device_id=partner(axis, bit))
        pl.semaphore_wait(barrier, len(places))
        copies = [
            pltpu.make_async_remote_copy(
                src_ref=sources[n],
                dst_ref=targets[n],
                send_sem=send_sem.at[n],
                recv_sem=recv_sem.at[n],
                device_id=partner(axis, bit),
            )
            for n, (_, axis, bit) in enumerate(items)
        ]
        for copy in copies:
            copy.start()
        for copy in copies:
            copy.wait()

    return call(
        body,
        meta,
        (1,),
        [(array, None) for array, _, _ in items],
        [(array.shape, array.dtype, None, "any") for array, _, _ in items],
        scratch=[pltpu.SemaphoreType.DMA((count,)), pltpu.SemaphoreType.DMA((count,))],
        remote=True,
        room=2 * 1024 * 1024,
    )


def spread_stats(meta, values):
    others = range(1, lax.axis_size("mp"))
    return [values] + list(exchange(meta, *[(values, "mp", b) for b in others]))


def gather_now(meta, values):
    far, near = exchange(meta, (values, "mp", 2), (values, "mp", 1))
    return [values, near, far, exchange(meta, (far, "mp", 1))[0]]


def scatter_now(meta, even, odd):
    near = add_low(even, exchange(meta, (odd, "mp", 1))[0])
    return near[0], exchange(meta, (near[1], "mp", 2))[0]


def pair_scratch(count, steps, rows, tile):
    shape = (count, steps, rows, tile)
    return [
        pltpu.VMEM(shape, BF),
        pltpu.VMEM(shape, BF),
        pltpu.VMEM(shape, F32),
        pltpu.SemaphoreType.DMA((count, steps)),
        pltpu.SemaphoreType.DMA((count, steps)),
    ]


def kind_of(meta, table_ref):
    return table_ref[pl.ds(meta[KIND], 1), :]


def text_body(meta, text_ref, table_ref, gain_ref, out_ref):
    mixed = text_ref[...].astype(F32) + kind_of(meta, table_ref)
    out_ref[...] = (norm_parts(mixed)[0] * gain_ref[...]).astype(BF)


def rotated(values, cosine, sine):
    width = values.shape[1]
    lane = lax.broadcasted_iota(jnp.int32, values.shape, 1)
    other = jnp.where(
        lane % HEAD < HEAD // 2,
        pltpu.roll(values, width - HEAD // 2, 1),
        pltpu.roll(values, HEAD // 2, 1),
    )
    repeat = width // LANES
    cosine = jnp.concatenate([cosine] * repeat, axis=1)
    sine = jnp.concatenate([sine] * repeat, axis=1)
    return values * cosine + other * sine


def qkv_body(meta, near_ref, far_ref, weight_ref, turn_ref, *refs, which):
    out_ref, in_ref = refs[-2:]
    rows = near_ref.shape[0]
    for n, ref in enumerate((near_ref, far_ref)):
        at = pl.ds(pl.multiple_of(((meta[PART] ^ (which + n)) % 2) * rows, rows), rows)
        product = dot(ref[...], weight_ref[0])
        out_ref[at, :] = rotated(product, turn_ref[0, 0, at, :], turn_ref[0, 1, at, :]).astype(BF)
        in_ref[at, :] = ref[...]


def project(meta, pieces, weight, turn, before, which, after=()):
    rows, depth = pieces[0].shape
    width = weight.shape[2]
    length = rows * lax.axis_size("mp")
    pair = lambda m: (m[PART] ^ which) // 2
    ins = [(pieces[0],), (pieces[1],), (weight, (1, depth, width), lambda i, m: (i, 0, 0))]
    ins.append((turn, (1, 2, 2 * rows, LANES), lambda i, m: (i, 0, pair(m), 0)))
    aliases = {}
    if before is not None:
        for n, array in enumerate(before):
            ins.append((array, None))
            aliases[5 + n] = n
    return call(
        functools.partial(qkv_body, which=which),
        meta,
        (3,),
        ins,
        [
            ((length, 3 * width), BF, (2 * rows, width), lambda i, m: (pair(m), i)),
            ((length, depth), BF, (2 * rows, depth), lambda i, m: (pair(m), 0)),
        ],
        aliases=aliases,
        after=after,
    )


def slot_body(meta, *refs, mp, slots, latent):
    pieces = refs[:mp]
    table_ref, gain_ref, weight_ref, turn_ref, qkv_in, x_in = refs[mp : mp + 6]
    qkv_ref, x_ref, slots_ref, rows_ref, new_ref, norm_ref = refs[mp + 6 :]
    step = pl.program_id(0)
    part = latent // mp

    @pl.when(step == 0)
    def _():
        for j in range(mp):
            place = pl.multiple_of((meta[PART] ^ j) * part, part)
            for s in range(slots):
                rows_ref[s, pl.ds(place, part), :] = pieces[j][s].astype(F32)
        mixed = rows_ref[...].reshape(slots * latent, -1)
        slots_ref[...] = mixed.astype(BF).reshape(slots_ref.shape)
        mixed = mixed + kind_of(meta, table_ref)
        normed = (norm_parts(mixed)[0] * gain_ref[...]).astype(BF)
        norm_ref[...] = normed.reshape(norm_ref.shape)

    @pl.when(step < 3)
    def _():
        product = dot(norm_ref[...].reshape(slots * latent, -1), weight_ref[0])
        new_ref[step] = product.reshape(new_ref.shape[1:])

    @pl.when(step >= 3)
    def _():
        slot = step - 3
        real = meta[REAL + slot] > 0
        width = new_ref.shape[-1]
        for c in range(3):
            at = slice(c * width, (c + 1) * width)
            value = rotated(new_ref[c, slot], turn_ref[c, 0], turn_ref[c, 1]).astype(BF)
            qkv_ref[:, at] = jnp.where(real, value, qkv_in[:, at])
        x_ref[...] = jnp.where(real, norm_ref[slot], x_in[...])


def turn_tables(length):
    positions = jnp.arange(length, dtype=F32)[:, None]
    lane = jnp.arange(LANES)
    ladder = (lane % (HEAD // 2)).astype(F32)
    angle = positions * jnp.power(10000.0, -2.0 * ladder / HEAD)[None, :]
    decay = (2.0 * ladder + 0.4 * HEAD) / (1.4 * HEAD)
    power = (positions - length // 2) / XPOS_BASE
    sign = jnp.where(lane % HEAD < HEAD // 2, -1.0, 1.0)[None, :]
    cosine, sine = jnp.cos(angle), jnp.sin(angle) * sign
    up = jnp.power(decay[None, :], power)
    down = jnp.power(decay[None, :], -power)
    one, zero = jnp.ones_like(cosine), jnp.zeros_like(cosine)
    return jnp.stack(
        [
            jnp.stack([cosine * up, sine * up]),
            jnp.stack([cosine * down, sine * down]),
            jnp.stack([one, zero]),
        ]
    )


def pool_shares_of(query, keys, head):
    lane = lax.broadcasted_iota(jnp.int32, query.shape, 1)
    masked = jnp.where(lane // HEAD == head, query, jnp.zeros_like(query))
    scores = dot(masked, keys, ROWS_BY_ROWS) * 0.125
    top = jnp.max(scores, axis=-1, keepdims=True)
    weights = jnp.exp(scores - top)
    return weights / jnp.sum(weights, axis=-1, keepdims=True)


def pool_body(
    meta, clip_ref, key_w, value_w, query_ref, key_ref, value_ref, pool_ref, *, images
):
    clip = clip_ref[...]
    key_ref[...] = dot(clip, key_w[...]).astype(BF)
    value_ref[...] = dot(clip, value_w[...]).astype(BF)
    patches = clip.shape[0] // images
    latent = query_ref.shape[0]
    for i in range(images):
        for pair in range(query_ref.shape[1] // LANES):
            lanes = slice(pair * LANES, (pair + 1) * LANES)
            rows = slice(i * patches, (i + 1) * patches)
            query, keys, values = query_ref[:, lanes], key_ref[rows, lanes], value_ref[rows, lanes]
            lane = lax.broadcasted_iota(jnp.int32, query.shape, 1)
            heads = [
                dot(pool_shares_of(query, keys, h).astype(BF), values) for h in range(2)
            ]
            pool_ref[i * latent : (i + 1) * latent, lanes] = jnp.where(
                lane < HEAD, heads[0], heads[1]
            ).astype(BF)


def pooled_body(meta, *refs, slots, mp):
    pieces, out_w, even_ref, odd_ref, scratch = refs[:slots], refs[slots], *refs[slots + 1 :]
    rows = jnp.concatenate([p[...] for p in pieces], axis=0)
    scratch[...] = dot(rows, out_w[...])
    latent = pieces[0].shape[0]
    part = latent // mp
    for j in range(mp):
        for s in range(slots):
            start = pl.multiple_of(s * latent + (meta[PART] ^ j) * part, part)
            (odd_ref if j % 2 else even_ref)[j // 2, s] = scratch[pl.ds(start, part), :].astype(BF)


def copy_body(meta, in_ref, out_ref):
    out_ref[...] = in_ref[...]


def head_lanes(pair, width):
    return [
        pl.ds(pl.multiple_of(c * width + pair * LANES, LANES), LANES) for c in range(3)
    ]


def attend_body(meta, qkv_ref, out_ref, lse_ref, stat_ref, first, second, lse, *, block):
    length, width = out_ref.shape
    first[...] = jnp.zeros_like(first)
    second[...] = jnp.zeros_like(second)

    def pair(hp, _):
        lanes, k_lanes, v_lanes = head_lanes(hp, width)
        keys, values = qkv_ref[:, k_lanes], qkv_ref[:, v_lanes]
        lane = lax.broadcasted_iota(jnp.int32, (block, LANES), 1)
        row = lax.broadcasted_iota(jnp.int32, (block, block), 0)
        col = lax.broadcasted_iota(jnp.int32, (block, block), 1)
        for b in range(length // block):
            rows = slice(b * block, (b + 1) * block)
            end = (b + 1) * block
            query = qkv_ref[rows, lanes]
            outs = []
            for h in range(2):
                masked = jnp.where(lane // HEAD == h, query, jnp.zeros_like(query))
                scores = dot(masked, keys[:end], ROWS_BY_ROWS) * 0.125
                edge = jnp.where(row >= col, scores[:, b * block :], NEG)
                scores = edge if b == 0 else jnp.concatenate([scores[:, : b * block], edge], axis=1)
                top = jnp.max(scores, axis=-1, keepdims=True)
                weights = jnp.exp(scores - top)
                total = jnp.sum(weights, axis=-1, keepdims=True)
                outs.append(dot(weights.astype(BF), values[:end]) / total)
                lse[rows, :] = jnp.where(lane == 2 * hp + h, top + jnp.log(total), lse[rows, :])
            out = jnp.where(lane < HEAD, outs[0], outs[1])
            first[rows, :] += out
            second[rows, :] += out * out
            out_ref[rows, lanes] = out.astype(BF)
        return 0

    lax.fori_loop(0, width // LANES, pair, 0)
    lse_ref[...] = lse[...].T[: lse_ref.shape[0]]
    stat_ref[...] = two_rows(rows_from(first[...]), rows_from(second[...]))


def total_columns(stats):
    total = stats[0][...]
    for other in stats[1:]:
        total = total + other[...]
    return columns_of(total)


def stat_norm(values, columns, at, width):
    mean = columns[:, at : at + 1] / width
    square = columns[:, at + 1 : at + 2] / width
    inv_std = lax.rsqrt(square - mean * mean + EPS)
    return (values - mean) * inv_std, inv_std


def mid_body(meta, att_ref, gain_ref, *refs, mp, width):
    normed, _ = stat_norm(att_ref[...].astype(F32), total_columns(refs[:mp]), 0, width)
    refs[mp][...] = (normed * gain_ref[...]).astype(BF)


def out_body(meta, rows_ref, weight_ref, out_ref, *scratch):
    rows = out_ref.shape[0]
    pair_sums(
        [
            (
                lambda: dot(rows_ref[:rows, :], weight_ref[...]),
                lambda: dot(rows_ref[rows:, :], weight_ref[...]),
            )
        ],
        [out_ref],
        scratch,
    )


def back_body(meta, rows_ref, weight_ref, out_ref, *scratch):
    rows = out_ref.shape[0]
    pair_sums(
        [
            (
                lambda: dot(rows_ref[:rows, :], weight_ref[...], ROWS_BY_ROWS),
                lambda: dot(rows_ref[rows:, :], weight_ref[...], ROWS_BY_ROWS),
            )
        ],
        [out_ref],
        scratch,
    )


def after_body(meta, own_ref, far_ref, text_ref, slots_ref, table_ref, gain_ref, after_ref, low_ref):
    mixed = mixed_rows(meta, text_ref, slots_ref, table_ref)
    after = mixed + (own_ref[...].astype(F32) + far_ref[...].astype(F32))
    after_ref[...] = after
    low_ref[...] = (norm_parts(after)[0] * gain_ref[...]).astype(BF)


def mixed_rows(meta, text_ref, slots_ref, table_ref):
    block = meta[PART] * pl.num_programs(0) + pl.program_id(0)
    filled = meta[BLOCK + block] >= 0
    return (
        jnp.where(filled, slots_ref[0].astype(F32), text_ref[...].astype(F32))
        + kind_of(meta, table_ref)
    )


def slot_index(blocks):
    return lambda i, m: (jnp.maximum(m[BLOCK + m[PART] * blocks + i], 0), 0, 0)


def times_rows_body(meta, *refs, count):
    pieces, weight_ref, outs = refs[:count], refs[count], refs[-count:]
    for piece, out_ref in zip(pieces, outs):
        out_ref[...] = dot(piece[...], weight_ref[...], ROWS_BY_ROWS).astype(out_ref.dtype)


def up_body(meta, a_ref, b_ref, weight_ref, dup_a, dup_b, gain_ref, *refs):
    act_ref, slope_ref, stat_ref = refs[-7:-4]
    sums = refs[-4:]
    step = pl.program_id(0)
    rows = a_ref.shape[0]

    @pl.when(step == 0)
    def _():
        for ref in sums:
            ref[...] = jnp.zeros_like(ref)

    for n, (ref, dup_ref) in enumerate(((a_ref, dup_a), (b_ref, dup_b))):
        here = slice(n * rows, (n + 1) * rows)
        pre = dot(ref[...], weight_ref[...])
        share = 0.5 + 0.5 * lax.erf(pre * (0.5**0.5))
        density = jnp.exp(pre * pre * -0.5) * ((2.0 * jnp.pi) ** -0.5)
        act = pre * share
        act_ref[here, :] = act.astype(BF)
        slope_ref[here, :] = (share + pre * density).astype(BF)
        scaled = dup_ref[...].astype(F32) * gain_ref[...]
        for ref_sum, term in zip(sums, (act, act * act, scaled, scaled * act)):
            ref_sum[here, :] += lane_sums(term)

    @pl.when(step == pl.num_programs(0) - 1)
    def _():
        rows_of = [rows_from(ref_sum[...]) for ref_sum in sums]
        row = lax.broadcasted_iota(jnp.int32, rows_of[0].shape, 0)
        total = jnp.zeros_like(rows_of[0])
        for n, value in enumerate(rows_of):
            total = jnp.where(row == n, value, total)
        stat_ref[...] = total


def spread_body(meta, act_ref, slope_ref, dup_0, dup_1, dup_2, dup_3, gain_ref, *refs, mp, width):
    stats = refs[:mp]
    pre_ref, low_ref, grad_ref = refs[mp:]
    columns = total_columns(stats)
    act = act_ref[...].astype(F32)
    normed, inv_std = stat_norm(act, columns, 0, width)
    gain = gain_ref[...]
    low_ref[...] = (normed * gain).astype(BF)
    step = pl.program_id(0) // (pl.num_programs(0) // 4)
    upstream = jnp.where(
        step < 2,
        jnp.where(step == 0, dup_0[...], dup_1[...]),
        jnp.where(step == 2, dup_2[...], dup_3[...]),
    ).astype(F32)
    first = columns[:, 2:3] / width
    mean = columns[:, 0:1] / width
    second = (columns[:, 3:4] - mean * columns[:, 2:3]) * inv_std / width
    d_act = inv_std * (upstream * gain - first - normed * second)
    pre_ref[...] = (d_act * slope_ref[...].astype(F32)).astype(BF)
    add_rows(grad_ref, upstream * normed)


def down_body(meta, low_ref, weight_ref, near_ref, far_ref, *scratch):
    rows = near_ref.shape[0]

    def term(j):
        return lambda: dot(low_ref[j * rows : (j + 1) * rows, :], weight_ref[...])

    pair_sums([(term(2), term(3)), (term(0), term(1))], [far_ref, near_ref], scratch)


def sum_body(meta, first_ref, second_ref, third_ref, out_ref):
    out_ref[...] = first_ref[...] + (second_ref[...].astype(F32) + third_ref[...].astype(F32))


def ffn_back_body(meta, own_ref, far_ref, after_ref, cot_ref, gain_ref, out_ref, low_ref, grad_ref):
    upstream = own_ref[...].astype(F32) + far_ref[...].astype(F32)
    normed, inv_std = norm_parts(after_ref[...])
    d_after = cot_ref[...].astype(F32) + norm_back(upstream, normed, inv_std, gain_ref[...])
    out_ref[...] = d_after
    low_ref[...] = d_after.astype(BF)
    add_rows(grad_ref, upstream * normed)


def add_rows(ref, values):
    total = jnp.sum(values, axis=0, keepdims=True)

    @pl.when(pl.program_id(0) == 0)
    def _():
        ref[...] = total

    @pl.when(pl.program_id(0) != 0)
    def _():
        ref[...] += total


def d_mid_body(meta, *refs, mp, width):
    pieces, weight_ref, gain_ref, att_ref = refs[:2], refs[2], refs[3], refs[4]
    stats = refs[5 : 5 + mp]
    out_ref, stat_ref, grad_ref = refs[-3:]
    rows = jnp.where(pl.program_id(0) == 0, pieces[0][...], pieces[1][...])
    d_mid = dot(rows, weight_ref[...], ROWS_BY_ROWS)
    out_ref[...] = d_mid.astype(BF)
    normed, _ = stat_norm(att_ref[...].astype(F32), total_columns(stats), 0, width)
    scaled = d_mid * gain_ref[...]
    add_rows(grad_ref, d_mid * normed)
    stat_ref[...] = two_rows(
        rows_from(lane_sums(scaled)), rows_from(lane_sums(scaled * normed))
    )


def attend_back_body(
    meta, qkv_ref, att_ref, dmid_ref, lse_ref, gain_ref, turn_ref, *refs, mp, width, block
):
    stats, more = refs[:mp], refs[mp : 2 * mp]
    out_ref, d_att, dq, dk, dv = refs[2 * mp :]
    length, wide = att_ref.shape
    columns = total_columns(stats)
    normed, inv_std = stat_norm(att_ref[...].astype(F32), columns, 0, width)
    sums = total_columns(more)
    scaled = dmid_ref[...].astype(F32) * gain_ref[...]
    d_att[...] = (
        inv_std * (scaled - sums[:, 0:1] / width - normed * (sums[:, 1:2] / width))
    ).astype(BF)

    def pair(hp, _):
        lanes, k_lanes, v_lanes = head_lanes(hp, wide)
        keys, values = qkv_ref[:, k_lanes], qkv_ref[:, v_lanes]
        lane = lax.broadcasted_iota(jnp.int32, (block, LANES), 1)
        row = lax.broadcasted_iota(jnp.int32, (block, block), 0)
        col = lax.broadcasted_iota(jnp.int32, (block, block), 1)
        dk[...] = jnp.zeros_like(dk)
        dv[...] = jnp.zeros_like(dv)
        both = d_att[:, lanes].astype(F32) * att_ref[:, lanes].astype(F32)
        side = lax.broadcasted_iota(jnp.int32, (8, LANES), 1) // HEAD
        pick_head = lax.broadcasted_iota(jnp.int32, (8, LANES), 0) == side
        inner = dot_exact(pick_head.astype(F32), both)
        for b in range(length // block):
            rows = slice(b * block, (b + 1) * block)
            end = (b + 1) * block
            query, grad = qkv_ref[rows, lanes], d_att[rows, lanes]
            d_query = jnp.zeros((block, LANES), F32)
            for h in range(2):
                keep = lane // HEAD == h
                q_one = jnp.where(keep, query, jnp.zeros_like(query))
                g_one = jnp.where(keep, grad, jnp.zeros_like(grad))
                scores = dot(keys[:end], q_one, ROWS_BY_ROWS) * 0.125
                shares = jnp.exp(scores - lse_ref[pl.ds(2 * hp + h, 1), rows])
                edge = jnp.where(col >= row, shares[b * block :], 0.0)
                shares = edge if b == 0 else jnp.concatenate([shares[: b * block], edge], axis=0)
                d_shares = dot(values[:end], g_one, ROWS_BY_ROWS)
                d_scores = (shares * (d_shares - inner[h : h + 1, rows])).astype(BF)
                dv[:end, :] += dot(shares.astype(BF), g_one)
                dk[:end, :] += dot(d_scores, q_one)
                turned = dot(d_scores, keys[:end], OVER_ROWS)
                d_query = jnp.where(keep, turned, d_query)
            dq[rows, :] = d_query
        out_ref[:, lanes] = rotated(
            dq[...] * 0.125, turn_ref[0, 0], -turn_ref[0, 1]
        ).astype(BF)
        out_ref[:, k_lanes] = rotated(
            dk[...] * 0.125, turn_ref[1, 0], -turn_ref[1, 1]
        ).astype(BF)
        out_ref[:, v_lanes] = dv[...].astype(BF)
        return 0

    lax.fori_loop(0, wide // LANES, pair, 0)


def three_dots(rows, weight_ref):
    width = weight_ref.shape[2]
    total = None
    for c in range(3):
        term = dot(rows[:, c * width : (c + 1) * width], weight_ref[c], ROWS_BY_ROWS)
        total = term if total is None else total + term
    return total


def slot_back_body(meta, *refs, slots, mp):
    pieces, weight_ref, even_ref, odd_ref, scratch = refs[:slots], refs[slots], *refs[-3:]
    rows = jnp.concatenate([p[...] for p in pieces], axis=0)
    scratch[...] = three_dots(rows, weight_ref)
    latent = pieces[0].shape[0]
    part = latent // mp
    for j in range(mp):
        for s in range(slots):
            start = pl.multiple_of(s * latent + (meta[PART] ^ j) * part, part)
            (odd_ref if j % 2 else even_ref)[j // 2, s] = scratch[pl.ds(start, part), :].astype(BF)


def row_back_body(meta, rows_ref, weight_ref, out_ref, *scratch, which):
    rows = out_ref.shape[0]
    me = lax.axis_index("mp")

    def term(j):
        at = pl.ds(pl.multiple_of(other_of(me, j) * rows, rows), rows)
        return lambda: three_dots(rows_ref[at, :], weight_ref)

    pair_sums([(term(which), term(which + 1))], [out_ref], scratch)


def slot_grad_body(meta, *refs, mp, slots, latent, images, groups):
    own_ref, far_ref, slots_ref, table_ref, gain_ref = refs[:5]
    after, (keep_ref, send_ref, grad_ref) = refs[5:-3], refs[-3:]
    part = latent // mp
    start = pl.multiple_of(meta[PART] * part, part)
    for s in range(slots):
        upstream = own_ref[s].astype(F32) + far_ref[s].astype(F32)
        mixed = slots_ref[s, pl.ds(start, part), :].astype(F32) + kind_of(meta, table_ref)
        normed, inv_std = norm_parts(mixed)
        block = meta[POS + s]
        blocks = after[0].shape[0] // latent
        rel = (block // blocks) ^ meta[PART]
        row = pl.multiple_of((block % blocks) * latent + start, part)
        d_after = after[0][pl.ds(row, part), :]
        for j in range(1, mp):
            d_after = jnp.where(rel == j, after[j][pl.ds(row, part), :], d_after)
        grad_ref[s] = (
            d_after.astype(F32) + norm_back(upstream, normed, inv_std, gain_ref[...])
        ).astype(BF)
    for k in range(groups):
        for i in range(images):
            rank = meta[RANK + (k ^ meta[GROUP]) * images + i]
            value = grad_ref[jnp.maximum(rank, 0)]
            value = jnp.where(rank >= 0, value, jnp.zeros_like(value))
            (send_ref if k % 2 else keep_ref)[k // 2, i * part : (i + 1) * part, :] = value


def in_back_body(
    meta, own_ref, far_ref, after_ref, text_ref, slots_ref, table_ref, gain_ref, out_ref, gain_grad, type_grad
):
    upstream = own_ref[...].astype(F32) + far_ref[...].astype(F32)
    normed, inv_std = norm_parts(mixed_rows(meta, text_ref, slots_ref, table_ref))
    d_mixed = after_ref[...] + norm_back(upstream, normed, inv_std, gain_ref[...])
    block = meta[PART] * pl.num_programs(0) + pl.program_id(0)
    out_ref[...] = jnp.where(meta[BLOCK + block] >= 0, 0.0, d_mixed)
    add_rows(gain_grad, upstream * normed)
    add_rows(type_grad, d_mixed)


def pool_back_body(
    meta, *refs, images, mp
):
    pieces, out_w, key_ref, value_ref, query_ref, key_w, value_w = refs[:mp], *refs[mp : mp + 6]
    kv_ref, query_grad, clip_even, clip_odd, grad_ref, scratch = refs[mp + 6 :]
    part = pieces[0].shape[1]
    for j in range(mp):
        for i in range(images):
            start = pl.multiple_of(i * part * mp + (meta[PART] ^ j) * part, part)
            grad_ref[pl.ds(start, part), :] = pieces[j][i]
    d_heads = dot(grad_ref[...], out_w[...], ROWS_BY_ROWS).astype(BF)
    patches = key_ref.shape[0] // images
    latent, wide = query_ref.shape
    for pair in range(wide // LANES):
        lanes = slice(pair * LANES, (pair + 1) * LANES)
        query = query_ref[:, lanes]
        lane = lax.broadcasted_iota(jnp.int32, query.shape, 1)
        d_query = jnp.zeros((latent, LANES), F32)
        for i in range(images):
            rows = slice(i * patches, (i + 1) * patches)
            keys, values = key_ref[rows, lanes], value_ref[rows, lanes]
            grad = d_heads[i * latent : (i + 1) * latent, lanes]
            d_keys = jnp.zeros((patches, LANES), F32)
            d_values = jnp.zeros((patches, LANES), F32)
            for h in range(2):
                keep = lane // HEAD == h
                shares = pool_shares_of(query, keys, h)
                g_one = jnp.where(keep, grad, jnp.zeros_like(grad))
                q_one = jnp.where(keep, query, jnp.zeros_like(query))
                d_shares = dot(g_one, values, ROWS_BY_ROWS)
                inner = jnp.sum(shares * d_shares, axis=-1, keepdims=True)
                d_scores = (shares * (d_shares - inner)).astype(BF)
                d_query += jnp.where(keep, dot(d_scores, keys), 0.0)
                d_keys += dot(d_scores, q_one, OVER_ROWS)
                d_values += dot(shares.astype(BF), g_one, OVER_ROWS)
            kv_ref[rows, lanes] = (d_keys * 0.125).astype(BF)
            kv_ref[rows, slice(wide + pair * LANES, wide + (pair + 1) * LANES)] = d_values.astype(BF)
        query_grad[:, lanes] = d_query * 0.125
    scratch[...] = dot(kv_ref[:, :wide], key_w[...], ROWS_BY_ROWS) + dot(
        kv_ref[:, wide:], value_w[...], ROWS_BY_ROWS
    )
    piece = patches // mp
    for j in range(mp):
        for i in range(images):
            start = pl.multiple_of(i * patches + (meta[PART] ^ j) * piece, piece)
            (clip_odd if j % 2 else clip_even)[j // 2, i] = scratch[
                pl.ds(start, piece), :
            ].astype(BF)


def weight_body(meta, *refs, lefts, rights, before, has_got, split):
    left, right = refs[:lefts], refs[lefts : lefts + rights]
    rest = refs[lefts + rights :]
    depth = sum(r.shape[0] for r in left)
    total = None
    step = depth // max(lefts, rights)
    for start in range(0, depth, step):
        l_ref, l_at = find(left, start)
        r_ref, r_at = find(right, start)
        term = dot(l_ref[l_at : l_at + step, :], r_ref[r_at : r_at + step, :], OVER_ROWS)
        total = term if total is None else total + term
    if split:
        wide = total.shape[1] // 2
        total = jnp.concatenate([total[:, :wide], total[:, wide:]], axis=0)
    if not has_got:
        rest[-1][0] = total.astype(BF)
        return
    even, odd = rest[-2:]
    total = (total + rest[0][0].astype(F32)).astype(BF)
    step = pl.program_id(0)

    @pl.when(step % 2 == 0)
    def _():
        even[0] = total

    @pl.when(step % 2 == 1)
    def _():
        odd[0] = total


def find(refs, start):
    for ref in refs:
        if start < ref.shape[0]:
            return ref, start
        start -= ref.shape[0]
    return None


def add_body(meta, keep_ref, got_ref, keep_out, send_out):
    keep_out[0] = (keep_ref[0].astype(F32) + got_ref[0].astype(F32)).astype(BF)
    send_out[0] = (keep_ref[1].astype(F32) + got_ref[1].astype(F32)).astype(BF)


def flat_body(meta, kinds, gain_in, gain_ffn, mid_near, mid_far, gain_ff, query_ref, flat_ref, rows_ref):
    rows_ref[...] = jnp.zeros_like(rows_ref)
    line = 0
    lines = [jnp.where(meta[KIND] == c, kinds[...], 0.0) for c in range(3)]
    lines += [gain_in[...], gain_ffn[...], mid_near[...] + mid_far[...], gain_ff[...]]
    for value in lines:
        for start in range(0, value.shape[1], LANES):
            rows_ref[line : line + 1, :] = value[:, start : start + LANES]
            line += 1
    latent, wide = query_ref.shape
    line = rows_ref.shape[0] - latent * wide // LANES
    for start in range(0, wide, LANES):
        rows_ref[line : line + latent, :] = query_ref[:, start : start + LANES]
        line += latent
    flat_ref[...] = rows_ref[...].astype(BF)


def last_body(meta, keep_ref, got_ref, out_ref):
    out_ref[...] = (keep_ref[...].astype(F32) + got_ref[...].astype(F32)).astype(out_ref.dtype)


def plus(meta, first, second, dtype):
    shape = first.shape
    steps = 2 if shape[-2] % 32 == 0 and len(shape) == 2 else 1
    block = (shape[-2] // steps,) + shape[-1:]
    if len(shape) == 3:
        block = shape
    index = lambda i, m: (i,) + (0,) * (len(shape) - 1)
    return call(
        last_body,
        meta,
        (steps,),
        [(first, block, index), (second, block, index)],
        [(shape, dtype, block, index)],
    )[0]


def split_sum(meta, keep, got):
    count, *dims = keep.shape
    pair, one = (2,) + tuple(dims), (1,) + tuple(dims)
    at = lambda i, m: (i, 0, 0)
    return call(
        add_body,
        meta,
        (count // 2,),
        [(keep, pair, at), (got, pair, at)],
        [((count // 2,) + tuple(dims), BF, one, at)] * 2,
    )


def stack_body(meta, first_ref, second_ref, out_ref):
    out_ref[:, 0] = first_ref[...]
    out_ref[:, 1] = second_ref[...]


class GatherDp:
    def __init__(self, meta, values):
        self.meta, self.values = meta, values[None]
        self.pending = list(reversed(bits_of(lax.axis_size("dp"))))
        self.got = swap(self.values, "dp", self.pending.pop(0))

    def step(self):
        count, *dims = self.values.shape
        stacked = call(
            stack_body,
            self.meta,
            (1,),
            [(self.values,), (self.got,)],
            [((count, 2) + tuple(dims), self.values.dtype, None, None)],
        )[0]
        self.values = stacked.reshape((2 * count,) + tuple(dims))
        if self.pending:
            self.got = swap(self.values, "dp", self.pending.pop(0))

    def end(self):
        while self.pending:
            self.step()
        self.step()
        return self.values


class WeightGrads:
    def __init__(self, meta, members, shape, first=1, cost=1):
        self.meta, self.members, self.shape = meta, members, shape
        self.size = lax.axis_size("dp")
        bits = bits_of(self.size)
        widths = [left[0].shape[1] // self.size for left, *_ in members]
        self.plain = any(w % LANES for w in widths) or self.size < 8
        self.first, self.cost = first, cost
        self.order = [first] + [b for b in bits if b != first]
        self.pending = list(self.order)

    def run(self, side, got):
        half, first = self.size // 2, self.first
        before = None
        for left, right, split, at in self.members:
            part = left[0].shape[1] // self.size
            inner = right[0].shape[1]
            block = (1, 2 * part, inner // 2) if split else (1, part, inner)
            place = lambda i, m, at=at: (i,) + at
            pair_place = lambda i, m, at=at: (i // 2,) + at
            column = lambda i, m: (
                0,
                m[GROUP] ^ ((i // first) * 2 * first + side * first + i % first),
            )
            ins = [(a, (a.shape[0], part), column) for a in left] + [(a,) for a in right]
            if got is not None:
                ins.append((got, block, place))
                outs = [((half // 2,) + self.shape, BF, block, pair_place)] * 2
            else:
                outs = [((half,) + self.shape, BF, block, place)]
            aliases = {}
            if before is not None:
                aliases = {len(ins) + 1 + n: n for n in range(len(outs))}
                ins += [(a, None) for a in before]
            before = call(
                functools.partial(
                    weight_body,
                    lefts=len(left),
                    rights=len(right),
                    before=before is not None,
                    has_got=got is not None,
                    split=split,
                ),
                self.meta,
                (half,),
                ins,
                outs,
                aliases=aliases,
                cost=self.cost,
            )
        return before

    def start(self):
        if not self.plain:
            self.got = swap(self.run(1, None)[0], "dp", self.pending.pop(0))

    def step(self):
        if self.plain:
            return
        if len(self.pending) == len(self.order) - 1:
            self.keep, send = self.run(0, self.got)
        else:
            self.keep, send = split_sum(self.meta, self.keep, self.got)
        self.got = swap(send, "dp", self.pending.pop(0))

    def finish(self):
        if not self.plain:
            while self.pending:
                self.step()
            self.total = plus(self.meta, self.keep[0], self.got[0], F32)

    def end(self):
        me = lax.axis_index("dp")
        results = []
        if self.plain:
            for left, right, split, at in self.members:
                whole = dot(jnp.concatenate(left), jnp.concatenate(right), OVER_ROWS).astype(BF)
                whole = whole.reshape(self.size, -1, whole.shape[1])
                whole = pick(whole, [me ^ k for k in range(self.size)])
                results.append(scatter_dp(whole, bits_of(self.size), F32))
            return results
        for left, right, split, at in self.members:
            part = left[0].shape[1] // self.size
            inner = right[0].shape[1]
            high, wide = (2 * part, inner // 2) if split else (part, inner)
            cut = (slice(at[0] * high, (at[0] + 1) * high), slice(at[1] * wide, (at[1] + 1) * wide))
            value = self.total[cut]
            if split:
                value = jnp.concatenate([value[:part], value[part:]], axis=1)
            results.append(value)
        return results


def shards(
    text_embed,
    clip_feats,
    type_table,
    gain_attn_in,
    qkv_weight,
    gain_attn_out,
    out_weight,
    gain_ffn_in,
    up_weight,
    gain_ffn_out,
    down_weight,
    res_query,
    res_key,
    res_value,
    res_out,
    cotangent,
    owner_count,
    image_seq,
    slot_block,
    seq_kind,
):
    mp = lax.axis_size("mp")
    dp = lax.axis_size("dp")
    rows, width = text_embed.shape
    length = rows * mp
    latent = res_query.shape[0]
    slots = slot_block.shape[1]
    images, patches, clip_width = clip_feats.shape
    wide = qkv_weight.shape[2]
    heads = wide // HEAD
    ff = up_weight.shape[1]
    ff_all = ff * mp
    here = rows // latent
    part = latent // mp
    tile = 512

    Order.mark, Order.channel = None, 0
    meta = make_meta(owner_count, image_seq, slot_block, seq_kind, images)
    table = type_table.astype(F32)
    gain_in, gain_out = gain_attn_in[None], gain_attn_out[None]
    gain_ffn, gain_ff = gain_ffn_in[None], gain_ffn_out[None]
    row_block = lambda i, m: (i, 0)
    few = (latent, width)
    weight = jnp.moveaxis(qkv_weight, 1, 0)
    turn = turn_tables(length)

    clip = clip_feats.reshape(images * patches, clip_width)
    key_proj, value_proj, pool_out = call(
        functools.partial(pool_body, images=images),
        image_seq,
        (1,),
        [(clip,), (res_key,), (res_value,), (res_query,)],
        [
            ((images * patches, wide), BF, None, None),
            ((images * patches, wide), BF, None, None),
            ((images * latent, wide), BF, None, None),
        ],
        room=4 * VMEM_BYTES,
    )
    gathering = GatherDp(meta, pool_out)

    text_in = call(
        text_body,
        meta,
        (4,),
        [(text_embed, (rows // 4, width), row_block), (table,), (gain_in,)],
        [((rows, width), BF, (rows // 4, width), row_block)],
    )[0]
    text_pieces = gather_start(text_in)
    gathering.step()
    state = project(meta, text_pieces[:2], weight, turn, None, 0)
    gathering.step()
    gather_end(meta, text_pieces)
    state = project(meta, text_pieces[2:], weight, turn, state, 2)

    def d_up_half(which):
        return call(
            functools.partial(times_rows_body, count=2),
            meta,
            (ff // tile,),
            [(cot_pieces[which + n],) for n in range(2)]
            + [(down_weight, (tile, width), row_block)],
            [((rows, ff), BF, (rows, tile), lambda i, m: (0, i))] * 2,
        )

    pool_rows = gathering.end().reshape(dp * images * latent, wide)
    slot_terms = call(
        functools.partial(pooled_body, slots=slots, mp=mp),
        meta,
        (1,),
        [
            (pool_rows, (latent, wide), lambda i, m, s=s: (m[SOURCE + s], 0))
            for s in range(slots)
        ]
        + [(res_out,)],
        [((mp // 2, slots, part, width), BF, None, None)] * 2,
        scratch=[pltpu.VMEM((slots * latent, width), F32)],
    )
    slot_own, slot_far = scatter_now(meta, *slot_terms)
    slot_pieces = gather_now(meta, add_low(slot_own, slot_far))

    cot = call(
        copy_body,
        meta,
        (2,),
        [(cotangent, (rows // 2, width), row_block)],
        [((rows, width), BF, (rows // 2, width), row_block)],
    )[0]
    cot_pieces = gather_start(cot)

    at_slot = lambda i, m: (m[POS + jnp.maximum(i - 3, 0)], 0)
    state = call(
        functools.partial(slot_body, mp=mp, slots=slots, latent=latent),
        meta,
        (3 + slots,),
        [(p,) for p in slot_pieces]
        + [(table,), (gain_in,)]
        + [(weight, (1, width, wide), lambda i, m: (jnp.minimum(i, 2), 0, 0))]
        + [(turn, (3, 2, latent, LANES), lambda i, m: (0, 0) + at_slot(i, m))]
        + [(a, (latent, a.shape[1]), at_slot) for a in state],
        [(a.shape, BF, (latent, a.shape[1]), at_slot) for a in state]
        + [((slots, latent, width), BF, None, None)],
        scratch=[
            pltpu.VMEM((slots, latent, width), F32),
            pltpu.VMEM((3, slots, latent, wide), F32),
            pltpu.VMEM((slots, latent, width), BF),
        ],
        aliases={mp + 5 + n: n for n in range(2)},
    )
    qkv, in_full, slot_rows = state

    att, lse, att_stats = call(
        functools.partial(attend_body, block=rows),
        meta,
        (1,),
        [(qkv,)],
        [
            ((length, wide), BF, None, None),
            ((heads, length), F32, None, None),
            ((8, length), F32, None, None),
        ],
        scratch=[pltpu.VMEM((length, LANES), F32)] * 3,
    )
    att_stats = spread_stats(meta, att_stats)

    mids = call(
        functools.partial(mid_body, mp=mp, width=width),
        meta,
        (mp,),
        [(att, (rows, wide), lambda j, m: (m[PART] ^ j, 0)), (gain_out,)]
        + [(s, (8, rows), lambda j, m: (0, m[PART] ^ j)) for s in att_stats],
        [((length, wide), BF, (rows, wide), lambda j, m: (j, 0))],
    )[0]
    steps = width // tile

    def summed(body, array, weights, which):
        return call(
            body,
            meta,
            (steps,),
            [(array, (2 * rows, array.shape[1]), lambda i, m: (which // 2, 0)), weights],
            [((rows, width), BF, None, None)],
            scratch=pair_scratch(1, steps, rows, tile),
            remote=True,
        )[0]

    out_w = (out_weight, (wide, tile), lambda i, m: (0, i))
    out_far = swap(summed(out_body, mids, out_w, 2), "mp", 2)
    out_terms = [summed(out_body, mids, out_w, 0), out_far]
    d_up_near = d_up_half(0)
    gather_end(meta, cot_pieces)
    d_up = d_up_near + d_up_half(2)
    after_attn, ffn_in = call(
        after_body,
        meta,
        (here,),
        [(t, few, row_block) for t in out_terms]
        + [(text_embed, few, row_block), (slot_rows, (1,) + few, slot_index(here))]
        + [(table,), (gain_ffn,)],
        [((rows, width), F32, few, row_block), ((rows, width), BF, few, row_block)],
    )
    ffn_pieces = gather_start(ffn_in)

    def up_half(which, before):
        lanes_of = lambda i, m: (0, i)
        half = lambda i, m: (which // 2, i)
        ins = [(ffn_pieces[which],), (ffn_pieces[which + 1],)]
        ins += [(up_weight, (width, tile), lanes_of)]
        ins += [(d_up[which + n], (rows, tile), lanes_of) for n in range(2)]
        ins += [(gain_ff, (1, tile), lanes_of)]
        aliases = {}
        if before is not None:
            aliases = {len(ins) + 1 + n: n for n in range(3)}
            ins += [(a, None) for a in before]
        return call(
            up_body,
            meta,
            (ff // tile,),
            ins,
            [
                ((length, ff), BF, (2 * rows, tile), half),
                ((length, ff), BF, (2 * rows, tile), half),
                ((8, length), F32, (8, 2 * rows), lambda i, m: (0, which // 2)),
            ],
            scratch=[pltpu.VMEM((2 * rows, LANES), F32)] * 4,
            aliases=aliases,
        )

    state = up_half(0, None)
    gather_end(meta, ffn_pieces)
    act, slope, ff_stats = up_half(2, state)
    ff_stats = spread_stats(meta, ff_stats)
    cut = rows // 2
    fine = lambda i, m: (i, 0)
    pre, low, gain_ff_local = call(
        functools.partial(spread_body, mp=mp, width=ff_all),
        meta,
        (length // cut,),
        [(act, (cut, ff), fine), (slope, (cut, ff), fine)]
        + [
            (d_up[j], (cut, ff), lambda i, m, j=j: (jnp.clip(i - 2 * j, 0, 1), 0))
            for j in range(mp)
        ]
        + [(gain_ff,)]
        + [
            (s, (8, cut), lambda i, m, b=b: (0, (((i // 2) ^ b) * 2) + i % 2))
            for b, s in enumerate(ff_stats)
        ],
        [((length, ff), BF, (cut, ff), fine)] * 2 + [((1, ff), F32, None, None)],
    )

    up_w = (up_weight, (tile, ff), row_block)
    down_grad = WeightGrads(meta, [(cot_pieces, [low], False, (0, 0))], (width // dp, ff))
    up_grad = WeightGrads(meta, [(ffn_pieces, [pre], False, (0, 0))], (width // dp, ff), 2)
    down_grad.start()
    up_grad.start()
    back_far = swap(summed(back_body, pre, up_w, 2), "mp", 2)
    ffn_terms = [summed(back_body, pre, up_w, 0), back_far]
    d_after, d_after_low, gain_ffn_local = call(
        ffn_back_body,
        meta,
        (here,),
        [(t, few, row_block) for t in ffn_terms]
        + [(after_attn, few, row_block), (cotangent, few, row_block), (gain_ffn,)],
        [
            ((rows, width), F32, few, row_block),
            ((rows, width), BF, few, row_block),
            ((1, width), F32, None, None),
        ],
    )
    after_pieces = gather_start(d_after_low)

    def d_mid_half(which, before):
        block = lambda i, m: (m[PART] ^ (which + i), 0)
        lane_block = lambda i, m: (0, m[PART] ^ (which + i))
        aliases = {}
        ins = [(after_pieces[which],), (after_pieces[which + 1],), (out_weight,), (gain_out,)]
        ins += [(att, (rows, wide), block)] + [(s, (8, rows), lane_block) for s in att_stats]
        if before is not None:
            aliases = {len(ins) + 1 + n: n for n in range(2)}
            ins += [(a, None) for a in before]
        return call(
            functools.partial(d_mid_body, mp=mp, width=width),
            meta,
            (2,),
            ins,
            [
                ((length, wide), BF, (rows, wide), block),
                ((8, length), F32, (8, rows), lane_block),
                ((1, wide), F32, None, None),
            ],
            aliases=aliases,
        )

    d_mid, mid_stats, gain_mid_near = d_mid_half(0, None)
    down_near, down_far = call(
        down_body,
        meta,
        (steps,),
        [(low,), (down_weight, (ff, tile), lambda i, m: (0, i))],
        [((rows, width), BF, None, None)] * 2,
        scratch=pair_scratch(2, steps, rows, tile),
        remote=True,
    )
    gather_end(meta, after_pieces)
    d_mid, mid_stats, gain_mid_far = d_mid_half(2, (d_mid, mid_stats))
    mid_stats = spread_stats(meta, mid_stats)
    down_far = swap(
        call(
            copy_body,
            meta,
            (2,),
            [(down_far, (rows // 2, width), row_block)],
            [((rows, width), BF, (rows // 2, width), row_block)],
        )[0],
        "mp",
        2,
    )
    out_grad = WeightGrads(meta, [(after_pieces, [mids], False, (0, 0))], (width // dp, wide))
    out_grad.start()
    down_grad.step()
    d_qkv = call(
        functools.partial(attend_back_body, mp=mp, width=width, block=rows),
        meta,
        (1,),
        [(a,) for a in (qkv, att, d_mid, lse, gain_out, turn)]
        + [(s,) for s in att_stats]
        + [(s,) for s in mid_stats],
        [((length, 3 * wide), BF, None, None)],
        scratch=[pltpu.VMEM((length, wide), BF)] + [pltpu.VMEM((length, LANES), F32)] * 3,
    )[0]

    slot_terms = call(
        functools.partial(slot_back_body, slots=slots, mp=mp),
        meta,
        (1,),
        [
            (d_qkv, (latent, 3 * wide), lambda i, m, s=s: (m[POS + s], 0))
            for s in range(slots)
        ]
        + [(weight,)],
        [((mp // 2, slots, part, width), BF, None, None)] * 2,
        scratch=[pltpu.VMEM((slots * latent, width), F32)],
    )
    slot_terms = scatter_now(meta, *slot_terms)
    image_keep, image_send, _ = call(
        functools.partial(
            slot_grad_body, mp=mp, slots=slots, latent=latent, images=images, groups=dp
        ),
        meta,
        (1,),
        [(t,) for t in slot_terms]
        + [(slot_rows,), (table,), (gain_in,)]
        + [(a,) for a in after_pieces],
        [((dp // 2, images * part, width), BF, None, None)] * 2
        + [((slots, part, width), BF, None, None)],
    )
    image_got = exchange(meta, (image_send, "dp", 1))[0]
    in_grad = WeightGrads(meta, [([in_full], [d_qkv], False, (0, 0))], (width // dp, 3 * wide))
    def row_terms(which):
        return call(
            functools.partial(row_back_body, which=which),
            meta,
            (steps,),
            [(d_qkv,), (weight, (3, tile, wide), lambda i, m: (0, i, 0))],
            [((rows, width), BF, None, None)],
            scratch=pair_scratch(1, steps, rows, tile),
            remote=True,
        )[0]

    for bit in bits_of(dp)[1:]:
        image_keep, image_send = split_sum(meta, image_keep, image_got)
        image_got = exchange(meta, (image_send, "dp", bit))[0]
        if bit == 2:
            layer_out = call(
                sum_body,
                meta,
                (here,),
                [(after_attn, few, row_block), (down_near, few, row_block), (down_far, few, row_block)],
                [((rows, width), F32, few, row_block)],
            )[0]
            out_grad.step()
            up_grad.step()
            in_grad.start()
            in_far = swap(row_terms(2), "mp", 2)
    down_grad.step()
    out_grad.step()
    owned = plus(meta, image_keep, image_got, BF).reshape(images, part, width)
    owned_pieces = gather_now(meta, owned)
    d_kv, query_local, clip_even, clip_odd, pool_grad = call(
        functools.partial(pool_back_body, images=images, mp=mp),
        meta,
        (1,),
        [(a,) for a in owned_pieces]
        + [(a,) for a in (res_out, key_proj, value_proj, res_query, res_key, res_value)],
        [
            ((images * patches, 2 * wide), BF, None, None),
            ((latent, wide), F32, None, None),
            ((mp // 2, images, patches // mp, clip_width), BF, None, None),
            ((mp // 2, images, patches // mp, clip_width), BF, None, None),
            ((images * latent, width), BF, None, None),
        ],
        scratch=[pltpu.VMEM((images * patches, clip_width), F32)],
    )
    pool_grads = WeightGrads(
        meta,
        [
            ([pool_grad], [pool_out], False, (0, 0)),
            ([clip], [d_kv], True, (1, 0)),
        ],
        (width // dp + 2 * (clip_width // dp), wide),
    )
    down_grad.finish()
    in_grad.step()
    pool_grads.start()
    in_terms = [row_terms(0), in_far]
    text_grad, gain_in_local, type_local = call(
        in_back_body,
        meta,
        (here,),
        [(t, few, row_block) for t in in_terms]
        + [(d_after, few, row_block), (text_embed, few, row_block)]
        + [(slot_rows, (1,) + few, slot_index(here)), (table,), (gain_in,)],
        [
            ((rows, width), F32, few, row_block),
            ((1, width), F32, None, None),
            ((1, width), F32, None, None),
        ],
    )
    down_grad.finish()
    hops = bits_of(dp)[1:] + [1]
    small = (type_local, gain_in_local, gain_ffn_local, gain_mid_near, gain_mid_far, gain_ff_local)
    sizes = 5 * width + wide + ff
    lines = -(-sizes // (16 * LANES)) * 16 + latent * wide // LANES
    flat = call(
        flat_body,
        meta,
        (1,),
        [(x,) for x in small] + [(query_local,)],
        [((lines, LANES), BF, None, None)],
        scratch=[pltpu.VMEM((lines, LANES), F32)],
    )[0]
    for n, bit in enumerate(hops):
        got = swap(flat, "dp", bit)
        if n == 0:
            up_grad.step()
            clip_even = add_low(clip_even, exchange(meta, (clip_odd, "mp", 1))[0])
            clip_far = exchange(meta, (clip_even[1], "mp", 2))[0]
        elif n == len(hops) - 2:
            pool_grads.step()
            in_grad.step()
        elif n == len(hops) - 1:
            up_grad.finish()
            pool_grads.step()
        flat = plus(meta, flat, got, BF)
    flat_far, flat_near = exchange(meta, (flat, "mp", 2), (flat, "mp", 1))
    flat_last = exchange(meta, (flat_far, "mp", 1))[0]
    out_grad.finish()
    pool_grads.finish()
    in_grad.finish()
    clip_grad = clip_even[0].astype(F32) + clip_far.astype(F32)
    flat = by_mp(jnp.stack([flat, flat_near, flat_far, flat_last])).astype(F32)
    edge = flat.shape[1] - latent * wide // LANES
    parts = flat[:, :edge].reshape(mp, -1)
    sums = jnp.sum(parts[:, : 5 * width].reshape(mp, 5, width), axis=0)
    parts = parts[:, 5 * width :]
    query_grad = flat[:, edge:].reshape(mp, wide // LANES, latent, LANES).swapaxes(1, 2)
    query_grad = jnp.swapaxes(query_grad.reshape(mp, latent, wide), 0, 1)
    res_out_grad, kv_grad = pool_grads.end()
    qkv_grad, out_grad = in_grad.end()[0], out_grad.end()[0]
    return (
        layer_out,
        text_grad,
        clip_grad,
        sums[:3],
        sums[3],
        qkv_grad.reshape(-1, 3, wide),
        parts[:, :wide].reshape(-1),
        out_grad.T,
        sums[4],
        up_grad.end()[0],
        parts[:, wide : wide + ff].reshape(-1),
        down_grad.end()[0].T,
        query_grad.reshape(latent, width),
        kv_grad[:, :wide],
        kv_grad[:, wide:],
        res_out_grad.T,
    )


def solution(mesh):
    return jax.shard_map(
        shards,
        mesh=mesh,
        in_specs=(
            P(("dp", "mp"), None),
            P("dp", None, None),
            P(),
            P(),
            P(None, None, "mp"),
            P("mp"),
            P("mp", None),
            P(),
            P(None, "mp"),
            P("mp"),
            P("mp", None),
            P(None, "mp"),
            P(None, "mp"),
            P(None, "mp"),
            P("mp", None),
            P(("dp", "mp"), None),
            P(),
            P(),
            P(),
            P(),
        ),
        out_specs=(
            P(("dp", "mp"), None),
            P(("dp", "mp"), None),
            P("dp", "mp", None),
            P(),
            P(),
            P("dp", None, "mp"),
            P(),
            P("mp", "dp"),
            P(),
            P("dp", "mp"),
            P(),
            P("mp", "dp"),
            P(),
            P("dp", "mp"),
            P("dp", "mp"),
            P("mp", "dp"),
        ),
        check_vma=False,
    )
```
